512 devices in a mesh: pipe: 32 (over z_lo, x), tensor: 16 (over z_hi, y, core).
Axes of the slice: x: 4, y: 4, z: 16 (z_hi: 2, z_lo: 8; z = z_hi * 8 + z_lo), core: 2. Of those that a mesh axis runs over, the one named last changes fastest.
Arguments:
- hidden: bfloat16 [32, 448, 8192], P('pipe', None, 'tensor'), may hold values from -9 to 9
- heads: bfloat16 [3, 8192, 20480], P(None, 'tensor', 'pipe')
- valid: int32 [448], P('tensor'), may hold values from 0 to 1, as said below
- exit_section: int32 [2], replicated, may hold values from 0 to 30, as said below
Outputs:
- d_heads: bfloat16 [2, 8192, 20480], P(None, 'tensor', 'pipe')
- d_hidden: bfloat16 [32, 448, 8192], P('pipe', None, 'tensor')
The draws below stay inside these ranges and needn't reach their ends.
Inputs may be any that keep to these rules, and one draw needn't show every extreme that they name: `exit_section`: the 2 exit sections are distinct and lie below the last section; the last exit lies on section 30. At least one position is valid.
All inputs are finite; a program needn't handle non-finite values.
Results may differ from the reference program's by a relative error of at most 0.0052.
Values may be sent and summed in bfloat16 or wider, within the bound.
No kernel may reach another device: no remote copies, remote signals or barrier semaphores. Data moves between devices by JAX's collectives and lax.ppermute only.
A program may use at most 64 MiB of HBM per device.

```python
import jax
import jax.numpy as jnp
from jax import lax

D = 8192
VOCAB = 20480
EXITS = 2
TOKENS = 448
SECTIONS = 32
HEADS = 3


def shared_signs(key):
    return jnp.where(jax.random.bernoulli(key, 0.5, (D,)), 1.0, -1.0).astype(jnp.float32)


def row_strength():
    place = jnp.arange(TOKENS)
    return jnp.where(place % 16 == 3, 1.0 + 0.5 * (place % 5).astype(jnp.float32), 0.0)


def draw_hidden(key, part):
    signs = shared_signs(key)
    key = jax.random.fold_in(key, 11)
    first = jax.random.fold_in(key, 0)
    strength = row_strength()
    base = jax.random.truncated_normal(first, -6.0, 6.0, (SECTIONS, TOKENS, D), jnp.float32)
    return (base + strength[None, :, None] * signs[None, None, :]).astype(jnp.bfloat16)


def draw_heads(key, part):
    signs = shared_signs(key)
    key = jax.random.fold_in(key, 23)
    scale = 3.0 / jnp.sqrt(jnp.float32(D))
    column = jnp.arange(VOCAB) % 640
    beta = jnp.where(column == 7, 1.0, jnp.where(column == 8, 1.01, 0.0))
    extra = 100.0 * beta[None, None, :] * signs[None, :, None] / jnp.float32(D)
    base = jax.random.truncated_normal(key, -6.0, 6.0, (HEADS, D, VOCAB), jnp.float32) * scale
    return (base + extra).astype(jnp.bfloat16)


def draw_valid(key, part):
    key = jax.random.fold_in(key, 37)
    place = jnp.arange(TOKENS)
    draws = jax.random.randint(key, (TOKENS,), 0, 5 * TOKENS)
    flags = (draws < TOKENS + 3 * place).astype(jnp.int32)
    return jnp.where(place == TOKENS - 1, 1, flags).astype(jnp.int32)


def draw_exit_section(key, part):
    key = jax.random.fold_in(key, 53)
    others = jax.random.permutation(key, SECTIONS - 2)[:EXITS - 1].astype(jnp.int32)
    return jnp.concatenate([others, jnp.array([SECTIONS - 2], jnp.int32)]).astype(jnp.int32)


def setup_inputs(seed: int = 0) -> dict:
    key_of = jax.random.split(jax.random.key(seed), 5)
    hidden = draw_hidden(jax.random.fold_in(key_of[4], 71), 0)
    heads = draw_heads(jax.random.fold_in(key_of[4], 71), 0)
    valid = draw_valid(jax.random.fold_in(key_of[4], 71), 0)
    exit_section = draw_exit_section(jax.random.fold_in(key_of[4], 71), 0)
    return {"hidden": hidden, "heads": heads, "valid": valid, "exit_section": exit_section}


loss_scale = 16384.0


def reference(hidden, heads, valid, exit_section):
    sources = jnp.concatenate([exit_section.astype(jnp.int32), jnp.array([SECTIONS - 1], jnp.int32)])
    flags = valid.astype(jnp.float32)
    count = jnp.sum(flags)
    probs = []
    tiles = []
    for j in range(EXITS + 1):
        tile = lax.dynamic_index_in_dim(hidden, sources[j], 0, keepdims=False)
        logits = jnp.dot(tile, heads[j], preferred_element_type=jnp.float32)
        probs.append(jax.nn.softmax(logits, axis=-1))
        tiles.append(tile)
    grads_heads = []
    d_hidden = jnp.zeros((SECTIONS, TOKENS, D), jnp.float32)
    for k in range(EXITS):
        delta = (loss_scale * flags[:, None] / count * (probs[k] - probs[EXITS])).astype(jnp.bfloat16)
        grads_heads.append(jnp.dot(tiles[k].T, delta, preferred_element_type=jnp.float32).astype(jnp.bfloat16))
        grad = jnp.dot(delta, heads[k].T, preferred_element_type=jnp.float32)
        d_hidden = d_hidden.at[exit_section[k]].add(grad)
    return jnp.stack(grads_heads), d_hidden.astype(jnp.bfloat16)
```

```python
import functools

import jax
import jax.numpy as jnp
from jax import lax
from jax.experimental import pallas as pl
from jax.experimental.pallas import tpu as pltpu
from jax.sharding import Mesh, PartitionSpec as P

loss_scale = 16384.0
ZL, X, ZH, Y, C = 8, 4, 2, 4, 2
PIPE = ("zl", "x")
TENSOR = ("zh", "y", "c")
SLOT = 32
ROWS = ZH * Y * C * SLOT
HALF = ROWS // 2
PART = ROWS // X
BIT = PART // ZL
f32, bf16 = jnp.float32, jnp.bfloat16


def swap(block, axis):
    return lax.ppermute(block, axis, [(0, 1), (1, 0)])


def exchange(block, axis):
    return lax.all_to_all(block, axis, 0, 0, tiled=True)


def spread(block, axis):
    copies = jnp.broadcast_to(block[None], (lax.axis_size(axis),) + block.shape)
    return exchange(copies, axis)


def pick(blocks, place):
    return lax.dynamic_index_in_dim(blocks, place, 0, keepdims=False)


def logits_kernel(half_ref, tally_ref, tiles_ref, heads_ref, out_ref):
    groups = HALF // BIT
    rows = tiles_ref[pl.ds(half_ref[0] * groups, groups), 0].reshape(HALF, -1)
    product = jnp.dot(rows, heads_ref[0], preferred_element_type=f32)
    row = lax.broadcasted_iota(jnp.int32, product.shape, 0) % SLOT
    out_ref[...] = jnp.where(row == SLOT - 4, tally_ref[0], product)


def half_logits(tiles, heads, half, tally):
    total, depth, width = heads.shape
    return pl.pallas_call(
        logits_kernel,
        grid_spec=pltpu.PrefetchScalarGridSpec(
            num_scalar_prefetch=1,
            grid=(total,),
            in_specs=[
                pl.BlockSpec(memory_space=pltpu.SMEM),
                pl.BlockSpec((ROWS // BIT, 1, BIT, depth), lambda j, _: (0, j, 0, 0)),
                pl.BlockSpec((1, depth, width), lambda j, _: (j, 0, 0)),
            ],
            out_specs=pl.BlockSpec((HALF, width), lambda j, _: (0, j)),
        ),
        out_shape=jax.ShapeDtypeStruct((HALF, total * width), f32),
        compiler_params=pltpu.CompilerParams(vmem_limit_bytes=32 << 20),
        cost_estimate=pl.CostEstimate(
            flops=2 * HALF * depth * width * total,
            bytes_accessed=2 * heads.size + 4 * HALF * total * width,
            transcendentals=0,
        ),
    )(half.reshape(1), tally.reshape(1), tiles, heads)


def grads_kernel(half_ref, tiles_ref, heads_ref, mine_ref, other_ref, dheads_ref, dhid_ref):
    groups = HALF // BIT
    half = half_ref[0]
    parts = HALF // PART
    total = None
    for place, delta_ref in ((half, mine_ref), (1 - half, other_ref)):
        rows = tiles_ref[pl.ds(place * groups, groups), 0].reshape(HALF, -1)
        delta = delta_ref[...]
        term = lax.dot_general(rows, delta, (((0,), (0,)), ((), ())), preferred_element_type=f32)
        total = term if total is None else total + term
        grad = lax.dot_general(
            delta, heads_ref[0], (((1,), (1,)), ((), ())), preferred_element_type=f32
        )
        dhid_ref[pl.ds(place * parts, parts), 0] = grad.reshape(parts, PART, -1).astype(bf16)
    dheads_ref[0] = total.astype(bf16)


def grads(tiles, heads, half, mine, other):
    total, depth, width = heads.shape
    exits = total - 1
    return pl.pallas_call(
        grads_kernel,
        grid_spec=pltpu.PrefetchScalarGridSpec(
            num_scalar_prefetch=1,
            grid=(exits,),
            in_specs=[
                pl.BlockSpec((ROWS // BIT, 1, BIT, depth), lambda k, _: (0, k, 0, 0)),
                pl.BlockSpec((1, depth, width), lambda k, _: (k, 0, 0)),
                pl.BlockSpec((HALF, width), lambda k, _: (0, k)),
                pl.BlockSpec((HALF, width), lambda k, _: (0, k)),
            ],
            out_specs=[
                pl.BlockSpec((1, depth, width), lambda k, _: (k, 0, 0)),
                pl.BlockSpec((X, 1, PART, depth), lambda k, _: (0, k, 0, 0)),
            ],
        ),
        out_shape=[
            jax.ShapeDtypeStruct((exits, depth, width), bf16),
            jax.ShapeDtypeStruct((X, exits, PART, depth), bf16),
        ],
        compiler_params=pltpu.CompilerParams(vmem_limit_bytes=40 << 20),
        cost_estimate=pl.CostEstimate(
            flops=4 * ROWS * depth * width * exits,
            bytes_accessed=6 * heads.size,
            transcendentals=0,
        ),
    )(half.reshape(1), tiles, heads, mine, other)


def local(hidden, heads, valid, exit_section):
    total, depth, width = heads.shape
    exits = total - 1
    tokens = valid.shape[0]
    zl, x, c = lax.axis_index("zl"), lax.axis_index("x"), lax.axis_index("c")
    zh = lax.axis_index("zh")
    last = ZL * X - 1
    sources = [exit_section[k] for k in range(exits)] + [jnp.int32(last)]

    own = hidden[0].reshape(ZH, Y, C, tokens, depth).transpose(2, 1, 0, 3, 4)
    own = jnp.pad(own, ((0, 0),) * 3 + ((0, SLOT - tokens), (0, 0))).reshape(ROWS, depth)
    row_parts = exchange(own, "x").reshape(X, PART, depth)
    chosen = jnp.stack([pick(row_parts, s % X).reshape(ZL, BIT, depth) for s in sources], 1)
    bits = exchange(chosen, "zl")
    mine = jnp.stack([pick(bits[:, j], s // X) for j, s in enumerate(sources)])
    column = spread(mine, "zl")
    tiles = spread(column, "x").reshape(ROWS // BIT, total, BIT, depth)

    tally = jnp.sum(valid.astype(f32))
    send = half_logits(tiles, heads, 1 - c, tally)
    keep = half_logits(tiles, heads, c, tally)
    both = keep + swap(send, "c")
    both = jnp.sum(exchange(both, "y").reshape(Y, ZH, SLOT, total * width), 0)
    logits = pick(both, zh) + swap(pick(both, 1 - zh), "zh")
    count = logits[SLOT - 4, 0]
    logits = logits.reshape(SLOT, total, width)

    local_top = jnp.max(logits, axis=2)
    powers = jnp.exp(logits - local_top[:, :, None])
    local_sum = jnp.sum(powers, axis=2)
    stats = exchange(
        jnp.broadcast_to(
            jnp.concatenate([local_top.T, local_sum.T])[None], (ZL * X, 2 * total, SLOT)
        ),
        PIPE,
    )
    tops, sums = stats[:, :total], stats[:, total:]
    top = jnp.max(tops, axis=0)
    denominator = jnp.sum(sums * jnp.exp(tops - top[None]), axis=0)
    probs = jnp.exp(logits - top.T[:, :, None]) / denominator.T[:, :, None]
    weights = loss_scale * jnp.pad(valid.astype(f32), (0, SLOT - tokens)) / count
    delta = weights[:, None, None] * (probs[:, :exits] - probs[:, exits:])
    delta = delta.reshape(SLOT, exits * width).astype(bf16)

    across = swap(delta, "zh")
    pair = jnp.where(zh == 0, jnp.stack([delta, across]), jnp.stack([across, delta]))
    near = spread(pair, "y").reshape(HALF, exits * width)
    far = swap(near, "c")
    d_heads, partial = grads(tiles, heads, c, near, far)

    summed = jnp.sum(exchange(partial, "x").astype(f32), axis=0).astype(bf16)
    summed = exchange(summed.reshape(exits, ZL, BIT, depth).transpose(1, 0, 2, 3), "zl")
    summed = jnp.sum(summed.astype(f32), axis=0).astype(bf16)
    summed = spread(summed, "zl").transpose(1, 0, 2, 3).reshape(exits, PART, depth)
    outgoing = summed[0][None]
    places = zl * X + jnp.arange(X, dtype=jnp.int32)
    for k in range(1, exits):
        outgoing = jnp.where((places == exit_section[k])[:, None, None], summed[k][None], outgoing)
    grad = exchange(outgoing, "x").reshape(ROWS, depth)
    grad = grad.reshape(C, Y, ZH, SLOT, depth)[:, :, :, :tokens].transpose(2, 1, 0, 3, 4)
    is_exit = jnp.any(exit_section == zl * X + x)
    grad = jnp.where(is_exit, grad.reshape(hidden.shape), jnp.zeros(hidden.shape, bf16))
    return d_heads, grad


def solution(mesh):
    fine = Mesh(mesh.devices.reshape(ZL, X, ZH, Y, C), ("zl", "x", "zh", "y", "c"))
    placed = (P(PIPE, None, TENSOR), P(None, TENSOR, PIPE), P(TENSOR), P())
    return jax.shard_map(
        local,
        mesh=fine,
        in_specs=placed,
        out_specs=(P(None, TENSOR, PIPE), P(PIPE, None, TENSOR)),
        check_vma=False,
    )
```

```python
import functools

import jax
import jax.numpy as jnp
from jax import lax
from jax.experimental import pallas as pl
from jax.experimental.pallas import tpu as pltpu
from jax.sharding import Mesh, PartitionSpec as P

loss_scale = 16384.0
ZL, X, ZH, Y, C = 8, 4, 2, 4, 2
PIPE = ("zl", "x")
TENSOR = ("zh", "y", "c")
SLOT = 32
ROWS = ZH * Y * C * SLOT
HALF = ROWS // 2
PART = ROWS // X
BIT = PART // ZL
LANES = 128
GROUP = 8
f32, bf16 = jnp.float32, jnp.bfloat16
SMALL = pl.BlockSpec(memory_space=pltpu.SMEM)
WHOLE = pl.BlockSpec(memory_space=pltpu.VMEM)
LIMIT = pltpu.CompilerParams(vmem_limit_bytes=40 << 20)


def swap(block, axis):
    return lax.ppermute(block, axis, [(0, 1), (1, 0)])


def exchange(block, axis):
    return lax.all_to_all(block, axis, 0, 0, tiled=True)


def spread(block, axis):
    copies = jnp.broadcast_to(block[None], (lax.axis_size(axis),) + block.shape)
    return exchange(copies, axis)


def pick(blocks, place):
    return lax.dynamic_index_in_dim(blocks, place, 0, keepdims=False)


def packed_width(count, width):
    return 3 * count * width + (width if count == 2 else 3 * LANES)


def pack(product, place, count, tally, out_ref):
    slots, width = HALF // SLOT, product.shape[1]
    groups = product.reshape(slots, 4, GROUP, width)
    for g in range(3):
        start = (g * count + place) * width
        out_ref[:, :, start : start + width] = groups[:, g]
    rest = groups[:, 3]
    base = 3 * count * width
    if count == 2:
        lower = slice(4 * place, 4 * place + 4)
        out_ref[:, lower, base : base + width] = rest[:, lower]
    else:
        cut = 3 * LANES
        out_ref[:, 0:4, base : base + cut] = rest[:, 0:4, :cut]
        out_ref[:, 4:8, base : base + width - cut] = rest[:, 4:8, cut:]
        spare = base + width - cut
        out_ref[:, 4:8, spare:] = jnp.full((slots, 4, base + cut - spare), tally, f32)


def unpack(block, place, count, width):
    rows = [
        block[:, (g * count + place) * width : (g * count + place + 1) * width] for g in range(3)
    ]
    base = 3 * count * width
    rest = block[:, base:]
    turned = pltpu.roll(rest, 4, 0)
    if count == 2:
        rows.append(turned if place else rest)
    else:
        cut = 3 * LANES
        rows.append(jnp.concatenate([rest, turned[:, : width - cut]], axis=1))
    return jnp.concatenate(rows, axis=0)


def logits_kernel(places, half_ref, tally_ref, tiles_ref, heads_ref, out_ref):
    parts = HALF // PART
    for j, place in enumerate(places):
        rows = tiles_ref[pl.ds(half_ref[0] * parts, parts), j].reshape(HALF, -1)
        product = jnp.dot(rows, heads_ref[place], preferred_element_type=f32)
        pack(product, j, len(places), tally_ref[0], out_ref)


def half_logits(tiles, heads, places, half, tally):
    count, (_, depth, width) = len(places), heads.shape
    shape = (HALF // SLOT, GROUP, packed_width(count, width))
    return pl.pallas_call(
        functools.partial(logits_kernel, places),
        in_specs=[SMALL, SMALL, WHOLE, WHOLE],
        out_specs=WHOLE,
        out_shape=jax.ShapeDtypeStruct(shape, f32),
        compiler_params=LIMIT,
        cost_estimate=pl.CostEstimate(
            flops=2 * HALF * depth * width * count,
            bytes_accessed=2 * count * depth * width + 2 * tiles.size,
            transcendentals=0,
        ),
    )(half.reshape(1), tally.reshape(1), tiles, heads)


def fold_kernel(place_ref, parts_ref, keep_ref, send_ref):
    place = place_ref[0]
    for side, out_ref in ((place, keep_ref), (1 - place, send_ref)):
        total = parts_ref[0, side]
        for i in range(1, parts_ref.shape[0]):
            total = total + parts_ref[i, side]
        out_ref[...] = total


def fold(parts, place):
    shape = jax.ShapeDtypeStruct(parts.shape[2:], f32)
    return pl.pallas_call(
        fold_kernel,
        in_specs=[SMALL, WHOLE],
        out_specs=[WHOLE, WHOLE],
        out_shape=[shape, shape],
        compiler_params=LIMIT,
    )(place.reshape(1), parts)


def stats_kernel(width, flags_ref, a_keep, a_come, b_keep, b_come, logits_ref, weights_ref, out_ref):
    first = a_keep[...] + a_come[...]
    pair = b_keep[...] + b_come[...]
    heads = [unpack(first, 0, 1, width)] + [unpack(pair, j, 2, width) for j in range(2)]
    lane = lax.broadcasted_iota(jnp.int32, (SLOT, LANES), 1)
    table = jnp.zeros((SLOT, LANES), f32)
    for j, logits in enumerate(heads):
        logits_ref[j] = logits
        top = jnp.max(logits, axis=1, keepdims=True)
        total = jnp.sum(jnp.exp(logits - top), axis=1, keepdims=True)
        table = jnp.where(lane == j, top, table)
        table = jnp.where(lane == 4 + j, total, table)
    table = jnp.concatenate([table, jnp.zeros((LANES - SLOT, LANES), f32)], axis=0).T[:GROUP]
    out_ref[...] = jnp.broadcast_to(table[None], out_ref.shape)
    count = first[GROUP - 1 :, first.shape[1] - 1 :]
    weights_ref[...] = jnp.broadcast_to(loss_scale * flags_ref[...] / count, (SLOT, LANES))


def delta_kernel(stats_ref, logits_ref, weights_ref, out_ref):
    tops = jnp.max(stats_ref[...], axis=0)
    total = jnp.zeros_like(tops)
    for i in range(stats_ref.shape[0]):
        tile = stats_ref[i]
        total += pltpu.roll(tile, 4, 0) * jnp.exp(tile - tops)
    row = lax.broadcasted_iota(jnp.int32, tops.shape, 0)
    table = jnp.where(row < 4, tops, pltpu.roll(total, 4, 0))
    table = jnp.concatenate([table, jnp.zeros((LANES - GROUP, LANES), f32)], axis=0).T[:SLOT]
    probs = [
        jnp.exp(logits_ref[j] - table[:, j : j + 1]) / table[:, 4 + j : 5 + j] for j in range(3)
    ]
    width = logits_ref.shape[2]
    for k in range(2):
        delta = weights_ref[:, :1] * (probs[k] - probs[2])
        out_ref[:, k * width : (k + 1) * width] = delta.astype(bf16)


def hidden_grads_kernel(half_ref, heads_ref, near_ref, far_ref, out_ref):
    exits, width = out_ref.shape[1], heads_ref.shape[2]
    parts = HALF // PART
    for place, delta_ref in ((half_ref[0], near_ref), (1 - half_ref[0], far_ref)):
        for k in range(exits):
            grad = lax.dot_general(
                delta_ref[:, k * width : (k + 1) * width],
                heads_ref[k],
                (((1,), (1,)), ((), ())),
                preferred_element_type=f32,
            )
            out_ref[pl.ds(place * parts, parts), k] = grad.reshape(parts, PART, -1).astype(bf16)


def head_grads_kernel(half_ref, first_ref, pair_ref, near_ref, far_ref, out_ref):
    exits, _, width = out_ref.shape
    parts = HALF // PART
    for k, tiles_ref in enumerate((first_ref, pair_ref)):
        total = None
        for place, delta_ref in ((half_ref[0], near_ref), (1 - half_ref[0], far_ref)):
            rows = tiles_ref[pl.ds(place * parts, parts), 0].reshape(HALF, -1)
            term = lax.dot_general(
                rows,
                delta_ref[:, k * width : (k + 1) * width],
                (((0,), (0,)), ((), ())),
                preferred_element_type=f32,
            )
            total = term if total is None else total + term
        out_ref[k] = total.astype(bf16)


def local(hidden, heads, valid, exit_section):
    total, depth, width = heads.shape
    exits = total - 1
    tokens = valid.shape[0]
    zl, x, c = lax.axis_index("zl"), lax.axis_index("x"), lax.axis_index("c")
    zh = lax.axis_index("zh")
    last = ZL * X - 1
    dynamic = exit_section[0]

    own = hidden[0].reshape(ZH, Y, C, tokens, depth).transpose(2, 1, 0, 3, 4)
    own = jnp.concatenate([own, own[:, :, :, 2 * tokens - SLOT :]], axis=3).reshape(ROWS, depth)
    row_parts = exchange(own, "x").reshape(X, PART, depth)

    def down(tree, step):
        pairs = [(z, z - step) for z in range(ZL - 1, -1, -2 * step)]
        return lax.ppermute(tree, "zl", pairs)

    def grown(tree, come, step):
        return jnp.where((zl % (2 * step)) == step - 1, come, tree)

    tree = jnp.stack([pick(row_parts, exit_section[1] % X), row_parts[last % X]])
    come = down(tree, 4)
    bits = exchange(pick(row_parts, dynamic % X).reshape(ZL, BIT, depth), "zl")
    come, bits = lax.optimization_barrier((come, bits))
    tree = grown(tree, come, 4)
    come = down(tree, 2)
    column = spread(pick(bits, dynamic // X), "zl")
    come, column = lax.optimization_barrier((come, column))
    tree = grown(tree, come, 2)
    tree = grown(tree, down(tree, 1), 1)

    pair_tiles = spread(tree, "x")
    first_tiles = spread(column, "x").reshape(X, 1, PART, depth)

    tally = jnp.sum(valid.astype(f32))
    pieces = []
    for tiles, places in ((pair_tiles, (1, 2)), (first_tiles, (0,))):
        send = half_logits(tiles, heads, places, 1 - c, tally)
        keep = half_logits(tiles, heads, places, c, tally)
        both = keep + swap(send, "c")
        parts = exchange(both, "y").reshape(Y, ZH, GROUP, both.shape[-1])
        keep, send = fold(parts, zh)
        pieces.append((keep, swap(send, "zh")))

    flags = jnp.pad(valid.astype(f32), (0, SLOT - tokens))[:, None]
    logits, weights, stats = pl.pallas_call(
        functools.partial(stats_kernel, width),
        in_specs=[WHOLE] * 5,
        out_specs=[WHOLE] * 3,
        out_shape=[
            jax.ShapeDtypeStruct((total, SLOT, width), f32),
            jax.ShapeDtypeStruct((SLOT, LANES), f32),
            jax.ShapeDtypeStruct((ZL * X, GROUP, LANES), f32),
        ],
        compiler_params=LIMIT,
    )(flags, *pieces[1], *pieces[0])
    delta = pl.pallas_call(
        delta_kernel,
        in_specs=[WHOLE] * 3,
        out_specs=WHOLE,
        out_shape=jax.ShapeDtypeStruct((SLOT, exits * width), bf16),
        compiler_params=LIMIT,
    )(exchange(stats, PIPE), logits, weights)

    across = swap(delta, "zh")
    pair = jnp.where(zh == 0, jnp.stack([delta, across]), jnp.stack([across, delta]))
    near = spread(pair, "y").reshape(HALF, exits * width)
    far = swap(near, "c")
    half = c.reshape(1)
    partial = pl.pallas_call(
        hidden_grads_kernel,
        in_specs=[SMALL, WHOLE, WHOLE, WHOLE],
        out_specs=WHOLE,
        out_shape=jax.ShapeDtypeStruct((X, exits, PART, depth), bf16),
        compiler_params=LIMIT,
    )(half, heads, near, far)
    d_heads = pl.pallas_call(
        head_grads_kernel,
        in_specs=[SMALL, WHOLE, WHOLE, WHOLE, WHOLE],
        out_specs=WHOLE,
        out_shape=jax.ShapeDtypeStruct((exits, depth, width), bf16),
        compiler_params=LIMIT,
    )(half, first_tiles, pair_tiles, near, far)

    summed = jnp.sum(exchange(partial, "x").astype(f32), axis=0).astype(bf16)
    summed = exchange(summed.reshape(exits, ZL, BIT, depth).transpose(1, 0, 2, 3), "zl")
    summed = jnp.sum(summed.astype(f32), axis=0).astype(bf16)
    summed = spread(summed, "zl").transpose(1, 0, 2, 3).reshape(exits, PART, depth)
    outgoing = summed[0][None]
    places = zl * X + jnp.arange(X, dtype=jnp.int32)
    for k in range(1, exits):
        outgoing = jnp.where((places == exit_section[k])[:, None, None], summed[k][None], outgoing)
    grad = exchange(outgoing, "x").reshape(ROWS, depth)
    grad = grad.reshape(C, Y, ZH, SLOT, depth)[:, :, :, :tokens].transpose(2, 1, 0, 3, 4)
    is_exit = jnp.any(exit_section == zl * X + x)
    grad = jnp.where(is_exit, grad.reshape(hidden.shape), jnp.zeros(hidden.shape, bf16))
    return d_heads, grad


def solution(mesh):
    fine = Mesh(mesh.devices.reshape(ZL, X, ZH, Y, C), ("zl", "x", "zh", "y", "c"))
    placed = (P(PIPE, None, TENSOR), P(None, TENSOR, PIPE), P(TENSOR), P())
    return jax.shard_map(
        local,
        mesh=fine,
        in_specs=placed,
        out_specs=(P(None, TENSOR, PIPE), P(PIPE, None, TENSOR)),
        check_vma=False,
    )
```

```python
import functools

import jax
import jax.numpy as jnp
from jax import lax
from jax.experimental import pallas as pl
from jax.experimental.pallas import tpu as pltpu
from jax.sharding import Mesh, PartitionSpec as P

loss_scale = 16384.0
ZL, X, ZH, Y, C = 8, 4, 2, 4, 2
PIPE = ("zl", "x")
TENSOR = ("zh", "y", "c")
SLOT = 32
ROWS = ZH * Y * C * SLOT
HALF = ROWS // 2
PART = ROWS // X
BIT = PART // ZL
LANES = 128
GROUP = 8
f32, bf16 = jnp.float32, jnp.bfloat16
SMALL = pl.BlockSpec(memory_space=pltpu.SMEM)
WHOLE = pl.BlockSpec(memory_space=pltpu.VMEM)
LIMIT = pltpu.CompilerParams(vmem_limit_bytes=40 << 20)


def swap(block, axis):
    return lax.ppermute(block, axis, [(0, 1), (1, 0)])


def exchange(block, axis):
    return lax.all_to_all(block, axis, 0, 0, tiled=True)


def spread(block, axis):
    copies = jnp.broadcast_to(block[None], (lax.axis_size(axis),) + block.shape)
    return exchange(copies, axis)


def pick(blocks, place):
    return lax.dynamic_index_in_dim(blocks, place, 0, keepdims=False)


def packed_width(count, width):
    return 3 * count * width + (width if count == 2 else 3 * LANES)


def pack(product, place, count, tally, out_ref):
    slots, width = HALF // SLOT, product.shape[1]
    groups = product.reshape(slots, 4, GROUP, width)
    for g in range(3):
        start = (g * count + place) * width
        out_ref[:, :, start : start + width] = groups[:, g]
    rest = groups[:, 3]
    base = 3 * count * width
    if count == 2:
        lower = slice(4 * place, 4 * place + 4)
        out_ref[:, lower, base : base + width] = rest[:, lower]
    else:
        cut = 3 * LANES
        out_ref[:, 0:4, base : base + cut] = rest[:, 0:4, :cut]
        out_ref[:, 4:8, base : base + width - cut] = rest[:, 4:8, cut:]
        spare = base + width - cut
        out_ref[:, 4:8, spare:] = jnp.full((slots, 4, base + cut - spare), tally, f32)


def unpack(block, place, count, width):
    rows = [
        block[:, (g * count + place) * width : (g * count + place + 1) * width] for g in range(3)
    ]
    base = 3 * count * width
    rest = block[:, base:]
    turned = pltpu.roll(rest, 4, 0)
    if count == 2:
        rows.append(turned if place else rest)
    else:
        cut = 3 * LANES
        rows.append(jnp.concatenate([rest, turned[:, : width - cut]], axis=1))
    return jnp.concatenate(rows, axis=0)


def logits_kernel(places, half_ref, tally_ref, tiles_ref, heads_ref, out_ref):
    parts = HALF // PART
    for j, place in enumerate(places):
        rows = tiles_ref[pl.ds(half_ref[0] * parts, parts), j].reshape(HALF, -1)
        product = jnp.dot(rows, heads_ref[place], preferred_element_type=f32)
        pack(product, j, len(places), tally_ref[0], out_ref)


def half_logits(tiles, heads, places, half, tally):
    count, (_, depth, width) = len(places), heads.shape
    shape = (HALF // SLOT, GROUP, packed_width(count, width))
    return pl.pallas_call(
        functools.partial(logits_kernel, places),
        in_specs=[SMALL, SMALL, WHOLE, WHOLE],
        out_specs=WHOLE,
        out_shape=jax.ShapeDtypeStruct(shape, f32),
        compiler_params=LIMIT,
        cost_estimate=pl.CostEstimate(
            flops=2 * HALF * depth * width * count,
            bytes_accessed=2 * count * depth * width + 2 * tiles.size,
            transcendentals=0,
        ),
    )(half.reshape(1), tally.reshape(1), tiles, heads)


def fold_kernel(place_ref, parts_ref, keep_ref, send_ref):
    place = place_ref[0]
    for side, out_ref in ((place, keep_ref), (1 - place, send_ref)):
        total = parts_ref[0, side]
        for i in range(1, parts_ref.shape[0]):
            total = total + parts_ref[i, side]
        out_ref[...] = total


def fold(parts, place):
    shape = jax.ShapeDtypeStruct(parts.shape[2:], f32)
    return pl.pallas_call(
        fold_kernel,
        in_specs=[SMALL, WHOLE],
        out_specs=[WHOLE, WHOLE],
        out_shape=[shape, shape],
        compiler_params=LIMIT,
    )(place.reshape(1), parts)


def stats_kernel(width, flags_ref, a_keep, a_come, b_keep, b_come, logits_ref, weights_ref, out_ref):
    first = a_keep[...] + a_come[...]
    pair = b_keep[...] + b_come[...]
    heads = [unpack(first, 0, 1, width)] + [unpack(pair, j, 2, width) for j in range(2)]
    tops, sums = [], []
    for j, logits in enumerate(heads):
        logits_ref[j] = logits
        tops.append(jnp.max(logits, axis=1, keepdims=True))
        sums.append(jnp.sum(jnp.exp(logits - tops[-1]), axis=1, keepdims=True))
    blank = jnp.zeros((LANES - len(heads) * SLOT, 1), f32)
    lane = lax.broadcasted_iota(jnp.int32, (LANES, LANES), 1)
    table = jnp.where(
        lane == 0,
        jnp.concatenate(tops + [blank], axis=0),
        jnp.where(lane == 1, jnp.concatenate(sums + [blank], axis=0), 0.0),
    ).T
    line = jnp.concatenate([table[0:1], table[1:2]], axis=1)
    out_ref[...] = jnp.broadcast_to(line[None], out_ref.shape)
    count = first[GROUP - 1 :, first.shape[1] - 1 :]
    weights_ref[...] = jnp.broadcast_to(loss_scale * flags_ref[...] / count, (SLOT, LANES))


def delta_kernel(stats_ref, logits_ref, weights_ref, out_ref):
    lines = stats_ref[...].reshape(stats_ref.shape[0], 2 * LANES)
    tops, sums = lines[:, :LANES], lines[:, LANES:]
    top = jnp.max(tops, axis=0, keepdims=True)
    total = jnp.sum(sums * jnp.exp(tops - top), axis=0, keepdims=True)
    row = lax.broadcasted_iota(jnp.int32, (LANES, LANES), 0)
    table = jnp.where(row == 0, top, jnp.where(row == 1, total, 0.0)).T
    probs = []
    for j in range(logits_ref.shape[0]):
        rows = table[j * SLOT : (j + 1) * SLOT]
        probs.append(jnp.exp(logits_ref[j] - rows[:, 0:1]) / rows[:, 1:2])
    width = logits_ref.shape[2]
    for k in range(2):
        delta = weights_ref[:, :1] * (probs[k] - probs[2])
        out_ref[:, k * width : (k + 1) * width] = delta.astype(bf16)


def halves(place_ref, deltas, k, width):
    c, zh = place_ref[0], place_ref[1]
    cols = slice(k * width, (k + 1) * width)
    for place, (own_ref, across_ref) in ((c, deltas[0::2]), (1 - c, deltas[1::2])):
        own, across = own_ref[:, :, cols], across_ref[:, :, cols]
        low, high = jnp.where(zh == 0, own, across), jnp.where(zh == 0, across, own)
        yield place, jnp.stack([low, high], axis=1).reshape(HALF, width)


def hidden_grads_kernel(place_ref, heads_ref, *refs):
    out_ref = refs[-1]
    exits, width = out_ref.shape[1], heads_ref.shape[2]
    parts = HALF // PART
    for k in range(exits):
        for place, delta in halves(place_ref, refs[:-1], k, width):
            grad = lax.dot_general(
                delta, heads_ref[k], (((1,), (1,)), ((), ())), preferred_element_type=f32
            )
            out_ref[pl.ds(place * parts, parts), k] = grad.reshape(parts, PART, -1).astype(bf16)


def head_grads_kernel(place_ref, first_ref, pair_ref, *refs):
    out_ref = refs[-1]
    exits, _, width = out_ref.shape
    parts = HALF // PART
    for k, tiles_ref in enumerate((first_ref, pair_ref)):
        total = None
        for place, delta in halves(place_ref, refs[:-1], k, width):
            rows = tiles_ref[pl.ds(place * parts, parts), 0].reshape(HALF, -1)
            term = lax.dot_general(
                rows, delta, (((0,), (0,)), ((), ())), preferred_element_type=f32
            )
            total = term if total is None else total + term
        out_ref[k] = total.astype(bf16)


def local(hidden, heads, valid, exit_section):
    total, depth, width = heads.shape
    exits = total - 1
    tokens = valid.shape[0]
    zl, x, c = lax.axis_index("zl"), lax.axis_index("x"), lax.axis_index("c")
    zh = lax.axis_index("zh")
    last = ZL * X - 1
    dynamic = exit_section[0]

    own = hidden[0].reshape(ZH, Y, C, tokens, depth).transpose(2, 1, 0, 3, 4)
    own = jnp.concatenate([own, own[:, :, :, 2 * tokens - SLOT :]], axis=3).reshape(ROWS, depth)
    row_parts = exchange(own, "x").reshape(X, PART, depth)

    def down(tree, step):
        pairs = [(z, z - step) for z in range(ZL - 1, -1, -2 * step)]
        return lax.ppermute(tree, "zl", pairs)

    def grown(tree, come, step):
        return jnp.where((zl % (2 * step)) == step - 1, come, tree)

    tree = jnp.stack([pick(row_parts, exit_section[1] % X), row_parts[last % X]])
    come = down(tree, 4)
    bits = exchange(pick(row_parts, dynamic % X).reshape(ZL, BIT, depth), "zl")
    come, bits = lax.optimization_barrier((come, bits))
    tree = grown(tree, come, 4)
    come = down(tree, 2)
    column = spread(pick(bits, dynamic // X), "zl")
    come, column = lax.optimization_barrier((come, column))
    tree = grown(tree, come, 2)
    come = down(tree, 1)
    first_tiles = spread(column, "x").reshape(X, 1, PART, depth)
    come, first_tiles = lax.optimization_barrier((come, first_tiles))
    tree = grown(tree, come, 1)
    pair_tiles = spread(tree, "x")

    tally = jnp.sum(valid.astype(f32))
    pieces, earlier = [], None
    for tiles, places in ((first_tiles, (0,)), (pair_tiles, (1, 2))):
        send = half_logits(tiles, heads, places, 1 - c, tally)
        keep = half_logits(tiles, heads, places, c, tally)
        both = keep + swap(send, "c")
        if earlier is not None:
            both = lax.optimization_barrier((both, earlier))[0]
        parts = exchange(both, "y").reshape(Y, ZH, GROUP, both.shape[-1])
        earlier = parts
        keep, send = fold(parts, zh)
        pieces.append((keep, swap(send, "zh")))

    flags = jnp.pad(valid.astype(f32), (0, SLOT - tokens))[:, None]
    logits, weights, stats = pl.pallas_call(
        functools.partial(stats_kernel, width),
        in_specs=[WHOLE] * 5,
        out_specs=[WHOLE] * 3,
        out_shape=[
            jax.ShapeDtypeStruct((total, SLOT, width), f32),
            jax.ShapeDtypeStruct((SLOT, LANES), f32),
            jax.ShapeDtypeStruct((ZL * X, 1, 2 * LANES), f32),
        ],
        compiler_params=LIMIT,
    )(flags, *pieces[0], *pieces[1])
    delta = pl.pallas_call(
        delta_kernel,
        in_specs=[WHOLE] * 3,
        out_specs=WHOLE,
        out_shape=jax.ShapeDtypeStruct((SLOT, exits * width), bf16),
        compiler_params=LIMIT,
    )(exchange(stats, PIPE), logits, weights)

    across = swap(delta, "zh")
    deltas = []
    for block in (delta, across):
        near = spread(block, "y")
        deltas += [near, swap(near, "c")]
    place = jnp.stack([c, zh])
    partial = pl.pallas_call(
        hidden_grads_kernel,
        in_specs=[SMALL] + [WHOLE] * 5,
        out_specs=WHOLE,
        out_shape=jax.ShapeDtypeStruct((X, exits, PART, depth), bf16),
        compiler_params=LIMIT,
    )(place, heads, *deltas)
    d_heads = pl.pallas_call(
        head_grads_kernel,
        in_specs=[SMALL] + [WHOLE] * 6,
        out_specs=WHOLE,
        out_shape=jax.ShapeDtypeStruct((exits, depth, width), bf16),
        compiler_params=LIMIT,
    )(place, first_tiles, pair_tiles, *deltas)

    summed = jnp.sum(exchange(partial, "x").astype(f32), axis=0).astype(bf16)
    summed = exchange(summed.reshape(exits, ZL, BIT, depth).transpose(1, 0, 2, 3), "zl")
    summed = jnp.sum(summed.astype(f32), axis=0).astype(bf16)
    summed = spread(summed, "zl").transpose(1, 0, 2, 3).reshape(exits, PART, depth)
    outgoing = summed[0][None]
    places = zl * X + jnp.arange(X, dtype=jnp.int32)
    for k in range(1, exits):
        outgoing = jnp.where((places == exit_section[k])[:, None, None], summed[k][None], outgoing)
    grad = exchange(outgoing, "x").reshape(ROWS, depth)
    grad = grad.reshape(C, Y, ZH, SLOT, depth)[:, :, :, :tokens].transpose(2, 1, 0, 3, 4)
    is_exit = jnp.any(exit_section == zl * X + x)
    grad = jnp.where(is_exit, grad.reshape(hidden.shape), jnp.zeros(hidden.shape, bf16))
    return d_heads, grad


def solution(mesh):
    fine = Mesh(mesh.devices.reshape(ZL, X, ZH, Y, C), ("zl", "x", "zh", "y", "c"))
    placed = (P(PIPE, None, TENSOR), P(None, TENSOR, PIPE), P(TENSOR), P())
    return jax.shard_map(
        local,
        mesh=fine,
        in_specs=placed,
        out_specs=(P(None, TENSOR, PIPE), P(PIPE, None, TENSOR)),
        check_vma=False,
    )
```

```python
import functools

import jax
import jax.numpy as jnp
from jax import lax
from jax.experimental import pallas as pl
from jax.experimental.pallas import tpu as pltpu
from jax.sharding import Mesh, PartitionSpec as P

loss_scale = 16384.0
ZL, X, ZH, Y, C = 8, 4, 2, 4, 2
PIPE = ("zl", "x")
TENSOR = ("zh", "y", "c")
SLOT = 32
ROWS = ZH * Y * C * SLOT
HALF = ROWS // 2
PART = ROWS // X
BIT = PART // ZL
LANES = 128
GROUP = 8
f32, bf16 = jnp.float32, jnp.bfloat16
SMALL = pl.BlockSpec(memory_space=pltpu.SMEM)
WHOLE = pl.BlockSpec(memory_space=pltpu.VMEM)
LIMIT = pltpu.CompilerParams(vmem_limit_bytes=40 << 20)


def swap(block, axis):
    return lax.ppermute(block, axis, [(0, 1), (1, 0)])


def exchange(block, axis):
    return lax.all_to_all(block, axis, 0, 0, tiled=True)


def spread(block, axis):
    copies = jnp.broadcast_to(block[None], (lax.axis_size(axis),) + block.shape)
    return exchange(copies, axis)


def pick(blocks, place):
    return lax.dynamic_index_in_dim(blocks, place, 0, keepdims=False)


def packed_width(count, width):
    return 3 * count * width + (width if count == 2 else 3 * LANES)


def pack(product, place, count, tally, out_ref):
    slots, width = HALF // SLOT, product.shape[1]
    groups = product.reshape(slots, 4, GROUP, width)
    for g in range(3):
        start = (g * count + place) * width
        out_ref[:, :, start : start + width] = groups[:, g]
    rest = groups[:, 3]
    base = 3 * count * width
    if count == 2:
        lower = slice(4 * place, 4 * place + 4)
        out_ref[:, lower, base : base + width] = rest[:, lower]
    else:
        cut = 3 * LANES
        out_ref[:, 0:4, base : base + cut] = rest[:, 0:4, :cut]
        out_ref[:, 4:8, base : base + width - cut] = rest[:, 4:8, cut:]
        spare = base + width - cut
        out_ref[:, 4:8, spare:] = jnp.full((slots, 4, base + cut - spare), tally, f32)


def unpack(block, place, count, width):
    rows = [
        block[:, (g * count + place) * width : (g * count + place + 1) * width] for g in range(3)
    ]
    base = 3 * count * width
    rest = block[:, base:]
    turned = pltpu.roll(rest, 4, 0)
    if count == 2:
        rows.append(turned if place else rest)
    else:
        cut = 3 * LANES
        rows.append(jnp.concatenate([rest, turned[:, : width - cut]], axis=1))
    return jnp.concatenate(rows, axis=0)


def logits_kernel(places, half_ref, tally_ref, tiles_ref, heads_ref, out_ref):
    parts = HALF // PART
    for j, place in enumerate(places):
        rows = tiles_ref[pl.ds(half_ref[0] * parts, parts), j].reshape(HALF, -1)
        product = jnp.dot(rows, heads_ref[place], preferred_element_type=f32)
        pack(product, j, len(places), tally_ref[0], out_ref)


def half_logits(tiles, heads, places, half, tally):
    count, (_, depth, width) = len(places), heads.shape
    shape = (HALF // SLOT, GROUP, packed_width(count, width))
    return pl.pallas_call(
        functools.partial(logits_kernel, places),
        in_specs=[SMALL, SMALL, WHOLE, WHOLE],
        out_specs=WHOLE,
        out_shape=jax.ShapeDtypeStruct(shape, f32),
        compiler_params=LIMIT,
        cost_estimate=pl.CostEstimate(
            flops=2 * HALF * depth * width * count,
            bytes_accessed=2 * count * depth * width + 2 * tiles.size,
            transcendentals=0,
        ),
    )(half.reshape(1), tally.reshape(1), tiles, heads)


def fold_kernel(place_ref, parts_ref, keep_ref, send_ref):
    place = place_ref[0]
    for side, out_ref in ((place, keep_ref), (1 - place, send_ref)):
        total = parts_ref[0, side]
        for i in range(1, parts_ref.shape[0]):
            total = total + parts_ref[i, side]
        out_ref[...] = total


def fold(parts, place):
    shape = jax.ShapeDtypeStruct(parts.shape[2:], f32)
    return pl.pallas_call(
        fold_kernel,
        in_specs=[SMALL, WHOLE],
        out_specs=[WHOLE, WHOLE],
        out_shape=[shape, shape],
        compiler_params=LIMIT,
    )(place.reshape(1), parts)


def stats_kernel(width, flags_ref, a_keep, a_come, b_keep, b_come, logits_ref, weights_ref, out_ref):
    first = a_keep[...] + a_come[...]
    pair = b_keep[...] + b_come[...]
    heads = [unpack(first, 0, 1, width)] + [unpack(pair, j, 2, width) for j in range(2)]
    tops, sums = [], []
    for j, logits in enumerate(heads):
        logits_ref[j] = logits
        tops.append(jnp.max(logits, axis=1, keepdims=True))
        sums.append(jnp.sum(jnp.exp(logits - tops[-1]), axis=1, keepdims=True))
    blank = jnp.zeros((LANES - len(heads) * SLOT, 1), f32)
    lane = lax.broadcasted_iota(jnp.int32, (LANES, LANES), 1)
    table = jnp.where(
        lane == 0,
        jnp.concatenate(tops + [blank], axis=0),
        jnp.where(lane == 1, jnp.concatenate(sums + [blank], axis=0), 0.0),
    ).T
    line = jnp.concatenate([table[0:1], table[1:2]], axis=1)
    out_ref[...] = jnp.broadcast_to(line[None], out_ref.shape)
    count = first[GROUP - 1 :, first.shape[1] - 1 :]
    weights_ref[...] = jnp.broadcast_to(loss_scale * flags_ref[...] / count, (SLOT, LANES))


def delta_kernel(stats_ref, logits_ref, weights_ref, out_ref):
    lines = stats_ref[...].reshape(stats_ref.shape[0], 2 * LANES)
    tops, sums = lines[:, :LANES], lines[:, LANES:]
    top = jnp.max(tops, axis=0, keepdims=True)
    total = jnp.sum(sums * jnp.exp(tops - top), axis=0, keepdims=True)
    row = lax.broadcasted_iota(jnp.int32, (LANES, LANES), 0)
    table = jnp.where(row == 0, top, jnp.where(row == 1, total, 0.0)).T
    probs = []
    for j in range(logits_ref.shape[0]):
        rows = table[j * SLOT : (j + 1) * SLOT]
        probs.append(jnp.exp(logits_ref[j] - rows[:, 0:1]) / rows[:, 1:2])
    width = logits_ref.shape[2]
    for k in range(2):
        delta = weights_ref[:, :1] * (probs[k] - probs[2])
        out_ref[:, k * width : (k + 1) * width] = delta.astype(bf16)


def hidden_grads_kernel(half_ref, heads_ref, near_ref, far_ref, out_ref):
    exits, width = out_ref.shape[1], heads_ref.shape[2]
    parts = HALF // PART
    for place, delta_ref in ((half_ref[0], near_ref), (1 - half_ref[0], far_ref)):
        for k in range(exits):
            grad = lax.dot_general(
                delta_ref[:, k * width : (k + 1) * width],
                heads_ref[k],
                (((1,), (1,)), ((), ())),
                preferred_element_type=f32,
            )
            out_ref[pl.ds(place * parts, parts), k] = grad.reshape(parts, PART, -1).astype(bf16)


def head_grads_kernel(half_ref, first_ref, pair_ref, near_ref, far_ref, out_ref):
    exits, _, width = out_ref.shape
    parts = HALF // PART
    for k, tiles_ref in enumerate((first_ref, pair_ref)):
        total = None
        for place, delta_ref in ((half_ref[0], near_ref), (1 - half_ref[0], far_ref)):
            rows = tiles_ref[pl.ds(place * parts, parts), 0].reshape(HALF, -1)
            term = lax.dot_general(
                rows,
                delta_ref[:, k * width : (k + 1) * width],
                (((0,), (0,)), ((), ())),
                preferred_element_type=f32,
            )
            total = term if total is None else total + term
        out_ref[k] = total.astype(bf16)


def local(hidden, heads, valid, exit_section):
    total, depth, width = heads.shape
    exits = total - 1
    tokens = valid.shape[0]
    zl, x, c = lax.axis_index("zl"), lax.axis_index("x"), lax.axis_index("c")
    zh = lax.axis_index("zh")
    last = ZL * X - 1
    dynamic = exit_section[0]

    own = hidden[0].reshape(ZH, Y, C, tokens, depth).transpose(2, 1, 0, 3, 4)
    own = jnp.concatenate([own, own[:, :, :, 2 * tokens - SLOT :]], axis=3).reshape(ROWS, depth)
    row_parts = exchange(own, "x").reshape(X, PART, depth)

    def down(step):
        pairs = [(z, z - step) for z in range(ZL - 1, -1, -2 * step)]
        return lax.ppermute(tree, "zl", pairs)

    def across_zl(step):
        return lax.ppermute(first, "zl", [(z, z ^ step) for z in range(ZL)])

    def grown(come, step):
        return jnp.where((zl % (2 * step)) == step - 1, come, tree)

    def taken(come, step):
        return jnp.where((zl ^ (dynamic // X)) & step != 0, come, first)

    tree = jnp.stack([pick(row_parts, exit_section[1] % X), row_parts[last % X]])
    first = pick(row_parts, dynamic % X)
    first_come = across_zl(4)
    tree = grown(down(4), 4)
    tree_come, first_come = lax.optimization_barrier((down(2), first_come))
    tree, first = grown(tree_come, 2), taken(first_come, 4)
    tree_come, first_come = lax.optimization_barrier((down(1), across_zl(2)))
    tree, first = grown(tree_come, 1), taken(first_come, 2)
    pair_tiles = spread(tree, "x")
    first = taken(across_zl(1), 1)
    first_tiles = spread(first[None], "x").reshape(X, 1, PART, depth)

    tally = jnp.sum(valid.astype(f32))
    def halved(tiles, places):
        send = half_logits(tiles, heads, places, 1 - c, tally)
        return half_logits(tiles, heads, places, c, tally) + swap(send, "c")

    def over_y(both):
        return exchange(both, "y").reshape(Y, ZH, GROUP, both.shape[-1])

    pair, first_tiles = lax.optimization_barrier((halved(pair_tiles, (1, 2)), first_tiles))
    pair, first = lax.optimization_barrier((over_y(pair), halved(first_tiles, (0,))))
    pieces = []
    for parts in (over_y(first), pair):
        keep, send = fold(parts, zh)
        pieces += [keep, swap(send, "zh")]

    flags = jnp.pad(valid.astype(f32), (0, SLOT - tokens))[:, None]
    logits, weights, stats = pl.pallas_call(
        functools.partial(stats_kernel, width),
        in_specs=[WHOLE] * 5,
        out_specs=[WHOLE] * 3,
        out_shape=[
            jax.ShapeDtypeStruct((total, SLOT, width), f32),
            jax.ShapeDtypeStruct((SLOT, LANES), f32),
            jax.ShapeDtypeStruct((ZL * X, 1, 2 * LANES), f32),
        ],
        compiler_params=LIMIT,
    )(flags, *pieces)
    delta = pl.pallas_call(
        delta_kernel,
        in_specs=[WHOLE] * 3,
        out_specs=WHOLE,
        out_shape=jax.ShapeDtypeStruct((SLOT, exits * width), bf16),
        compiler_params=LIMIT,
    )(exchange(stats, PIPE), logits, weights)

    across = swap(delta, "zh")
    pair = jnp.where(zh == 0, jnp.stack([delta, across]), jnp.stack([across, delta]))
    near = spread(pair, "y").reshape(HALF, exits * width)
    far = swap(near, "c")
    half = c.reshape(1)
    partial = pl.pallas_call(
        hidden_grads_kernel,
        in_specs=[SMALL, WHOLE, WHOLE, WHOLE],
        out_specs=WHOLE,
        out_shape=jax.ShapeDtypeStruct((X, exits, PART, depth), bf16),
        compiler_params=LIMIT,
    )(half, heads, near, far)
    d_heads = pl.pallas_call(
        head_grads_kernel,
        in_specs=[SMALL, WHOLE, WHOLE, WHOLE, WHOLE],
        out_specs=WHOLE,
        out_shape=jax.ShapeDtypeStruct((exits, depth, width), bf16),
        compiler_params=LIMIT,
    )(half, first_tiles, pair_tiles, near, far)

    summed = jnp.sum(exchange(partial, "x").astype(f32), axis=0).astype(bf16)
    summed = exchange(summed.reshape(exits, ZL, BIT, depth).transpose(1, 0, 2, 3), "zl")
    summed = jnp.sum(summed.astype(f32), axis=0).astype(bf16)
    summed = spread(summed, "zl").transpose(1, 0, 2, 3).reshape(exits, PART, depth)
    outgoing = summed[0][None]
    places = zl * X + jnp.arange(X, dtype=jnp.int32)
    for k in range(1, exits):
        outgoing = jnp.where((places == exit_section[k])[:, None, None], summed[k][None], outgoing)
    grad = exchange(outgoing, "x").reshape(ROWS, depth)
    grad = grad.reshape(C, Y, ZH, SLOT, depth)[:, :, :, :tokens].transpose(2, 1, 0, 3, 4)
    is_exit = jnp.any(exit_section == zl * X + x)
    grad = jnp.where(is_exit, grad.reshape(hidden.shape), jnp.zeros(hidden.shape, bf16))
    return d_heads, grad


def solution(mesh):
    fine = Mesh(mesh.devices.reshape(ZL, X, ZH, Y, C), ("zl", "x", "zh", "y", "c"))
    placed = (P(PIPE, None, TENSOR), P(None, TENSOR, PIPE), P(TENSOR), P())
    return jax.shard_map(
        local,
        mesh=fine,
        in_specs=placed,
        out_specs=(P(None, TENSOR, PIPE), P(PIPE, None, TENSOR)),
        check_vma=False,
    )
```

```python
import functools

import jax
import jax.numpy as jnp
from jax import lax
from jax.experimental import pallas as pl
from jax.experimental.pallas import tpu as pltpu
from jax.sharding import Mesh, PartitionSpec as P

loss_scale = 16384.0
ZL, X, ZH, Y, C = 8, 4, 2, 4, 2
PIPE = ("zl", "x")
TENSOR = ("zh", "y", "c")
SLOT = 32
ROWS = ZH * Y * C * SLOT
HALF = ROWS // 2
PART = ROWS // X
BIT = PART // ZL
LANES = 128
GROUP = 8
f32, bf16 = jnp.float32, jnp.bfloat16
SMALL = pl.BlockSpec(memory_space=pltpu.SMEM)
WHOLE = pl.BlockSpec(memory_space=pltpu.VMEM)
LIMIT = pltpu.CompilerParams(vmem_limit_bytes=40 << 20)


def swap(block, axis):
    return lax.ppermute(block, axis, [(0, 1), (1, 0)])


def exchange(block, axis):
    return lax.all_to_all(block, axis, 0, 0, tiled=True)


def spread(block, axis):
    copies = jnp.broadcast_to(block[None], (lax.axis_size(axis),) + block.shape)
    return exchange(copies, axis)


def pick(blocks, place):
    return lax.dynamic_index_in_dim(blocks, place, 0, keepdims=False)


def packed_width(count, width):
    return 3 * count * width + (width if count == 2 else 3 * LANES)


def pack(product, place, count, tally, out_ref):
    slots, width = HALF // SLOT, product.shape[1]
    groups = product.reshape(slots, 4, GROUP, width)
    for g in range(3):
        start = (g * count + place) * width
        out_ref[:, :, start : start + width] = groups[:, g]
    rest = groups[:, 3]
    base = 3 * count * width
    if count == 2:
        lower = slice(4 * place, 4 * place + 4)
        out_ref[:, lower, base : base + width] = rest[:, lower]
    else:
        cut = 3 * LANES
        out_ref[:, 0:4, base : base + cut] = rest[:, 0:4, :cut]
        out_ref[:, 4:8, base : base + width - cut] = rest[:, 4:8, cut:]
        spare = base + width - cut
        out_ref[:, 4:8, spare:] = jnp.full((slots, 4, base + cut - spare), tally, f32)


def unpack(block, place, count, width):
    rows = [
        block[:, (g * count + place) * width : (g * count + place + 1) * width] for g in range(3)
    ]
    base = 3 * count * width
    rest = block[:, base:]
    turned = pltpu.roll(rest, 4, 0)
    if count == 2:
        rows.append(turned if place else rest)
    else:
        cut = 3 * LANES
        rows.append(jnp.concatenate([rest, turned[:, : width - cut]], axis=1))
    return jnp.concatenate(rows, axis=0)


def logits_kernel(places, half_ref, tally_ref, tiles_ref, heads_ref, out_ref):
    parts = HALF // PART
    for j, place in enumerate(places):
        rows = tiles_ref[pl.ds(half_ref[0] * parts, parts), j].reshape(HALF, -1)
        product = jnp.dot(rows, heads_ref[place], preferred_element_type=f32)
        pack(product, j, len(places), tally_ref[0], out_ref)


def half_logits(tiles, heads, places, half, tally):
    count, (_, depth, width) = len(places), heads.shape
    shape = (HALF // SLOT, GROUP, packed_width(count, width))
    return pl.pallas_call(
        functools.partial(logits_kernel, places),
        in_specs=[SMALL, SMALL, WHOLE, WHOLE],
        out_specs=WHOLE,
        out_shape=jax.ShapeDtypeStruct(shape, f32),
        compiler_params=LIMIT,
        cost_estimate=pl.CostEstimate(
            flops=2 * HALF * depth * width * count,
            bytes_accessed=2 * count * depth * width + 2 * tiles.size,
            transcendentals=0,
        ),
    )(half.reshape(1), tally.reshape(1), tiles, heads)


def fold_kernel(place_ref, parts_ref, keep_ref, send_ref):
    place = place_ref[0]
    for side, out_ref in ((place, keep_ref), (1 - place, send_ref)):
        total = parts_ref[0, side]
        for i in range(1, parts_ref.shape[0]):
            total = total + parts_ref[i, side]
        out_ref[...] = total


def fold(parts, place):
    shape = jax.ShapeDtypeStruct(parts.shape[2:], f32)
    return pl.pallas_call(
        fold_kernel,
        in_specs=[SMALL, WHOLE],
        out_specs=[WHOLE, WHOLE],
        out_shape=[shape, shape],
        compiler_params=LIMIT,
    )(place.reshape(1), parts)


def stats_kernel(width, flags_ref, a_keep, a_come, b_keep, b_come, logits_ref, weights_ref, out_ref):
    first = a_keep[...] + a_come[...]
    pair = b_keep[...] + b_come[...]
    heads = [unpack(first, 0, 1, width)] + [unpack(pair, j, 2, width) for j in range(2)]
    tops, sums = [], []
    for j, logits in enumerate(heads):
        logits_ref[j] = logits
        tops.append(jnp.max(logits, axis=1, keepdims=True))
        sums.append(jnp.sum(jnp.exp(logits - tops[-1]), axis=1, keepdims=True))
    blank = jnp.zeros((LANES - len(heads) * SLOT, 1), f32)
    lane = lax.broadcasted_iota(jnp.int32, (LANES, LANES), 1)
    table = jnp.where(
        lane == 0,
        jnp.concatenate(tops + [blank], axis=0),
        jnp.where(lane == 1, jnp.concatenate(sums + [blank], axis=0), 0.0),
    ).T
    line = jnp.concatenate([table[0:1], table[1:2]], axis=1)
    out_ref[...] = jnp.broadcast_to(line[None], out_ref.shape)
    count = first[GROUP - 1 :, first.shape[1] - 1 :]
    weights_ref[...] = jnp.broadcast_to(loss_scale * flags_ref[...] / count, (SLOT, LANES))


def delta_kernel(stats_ref, logits_ref, weights_ref, out_ref):
    lines = stats_ref[...].reshape(stats_ref.shape[0], 2 * LANES)
    tops, sums = lines[:, :LANES], lines[:, LANES:]
    top = jnp.max(tops, axis=0, keepdims=True)
    total = jnp.sum(sums * jnp.exp(tops - top), axis=0, keepdims=True)
    row = lax.broadcasted_iota(jnp.int32, (LANES, LANES), 0)
    table = jnp.where(row == 0, top, jnp.where(row == 1, total, 0.0)).T
    probs = []
    for j in range(logits_ref.shape[0]):
        rows = table[j * SLOT : (j + 1) * SLOT]
        probs.append(jnp.exp(logits_ref[j] - rows[:, 0:1]) / rows[:, 1:2])
    width = logits_ref.shape[2]
    for k in range(2):
        delta = weights_ref[:, :1] * (probs[k] - probs[2])
        out_ref[:, k * width : (k + 1) * width] = delta.astype(bf16)


def hidden_grads_kernel(half_ref, heads_ref, near_ref, far_ref, out_ref):
    exits, width = out_ref.shape[1], heads_ref.shape[2]
    parts = HALF // PART
    for place, delta_ref in ((half_ref[0], near_ref), (1 - half_ref[0], far_ref)):
        for k in range(exits):
            grad = lax.dot_general(
                delta_ref[:, k * width : (k + 1) * width],
                heads_ref[k],
                (((1,), (1,)), ((), ())),
                preferred_element_type=f32,
            )
            out_ref[pl.ds(place * parts, parts), k] = grad.reshape(parts, PART, -1).astype(bf16)


def head_grads_kernel(half_ref, first_ref, pair_ref, near_ref, far_ref, out_ref):
    exits, _, width = out_ref.shape
    parts = HALF // PART
    for k, tiles_ref in enumerate((first_ref, pair_ref)):
        total = None
        for place, delta_ref in ((half_ref[0], near_ref), (1 - half_ref[0], far_ref)):
            rows = tiles_ref[pl.ds(place * parts, parts), 0].reshape(HALF, -1)
            term = lax.dot_general(
                rows,
                delta_ref[:, k * width : (k + 1) * width],
                (((0,), (0,)), ((), ())),
                preferred_element_type=f32,
            )
            total = term if total is None else total + term
        out_ref[k] = total.astype(bf16)


def local(hidden, heads, valid, exit_section):
    total, depth, width = heads.shape
    exits = total - 1
    tokens = valid.shape[0]
    zl, x, c = lax.axis_index("zl"), lax.axis_index("x"), lax.axis_index("c")
    zh = lax.axis_index("zh")
    last = ZL * X - 1
    dynamic = exit_section[0]

    own = hidden[0].reshape(ZH, Y, C, tokens, depth).transpose(2, 1, 0, 3, 4)
    own = jnp.concatenate([own, own[:, :, :, 2 * tokens - SLOT :]], axis=3).reshape(ROWS, depth)
    row_parts = exchange(own, "x").reshape(X, PART, depth)

    def down(step):
        pairs = [(z, z - step) for z in range(ZL - 1, -1, -2 * step)]
        return lax.ppermute(tree, "zl", pairs)

    def across_zl(step):
        return lax.ppermute(first, "zl", [(z, z ^ step) for z in range(ZL)])

    def grown(come, step):
        return jnp.where((zl % (2 * step)) == step - 1, come, tree)

    def taken(come, step):
        return jnp.where((zl ^ (dynamic // X)) & step != 0, come, first)

    tree = jnp.stack([pick(row_parts, exit_section[1] % X), row_parts[last % X]])
    first = pick(row_parts, dynamic % X)
    first_come = across_zl(4)
    tree = grown(down(4), 4)
    tree_come, first_come = lax.optimization_barrier((down(2), first_come))
    tree, first = grown(tree_come, 2), taken(first_come, 4)
    tree = grown(down(1), 1)
    first = taken(across_zl(2), 2)
    pair_tiles, first_come = lax.optimization_barrier((spread(tree, "x"), across_zl(1)))
    first = taken(first_come, 1)
    first_tiles = spread(first[None], "x").reshape(X, 1, PART, depth)

    tally = jnp.sum(valid.astype(f32))
    def halved(tiles, places):
        send = half_logits(tiles, heads, places, 1 - c, tally)
        return half_logits(tiles, heads, places, c, tally) + swap(send, "c")

    def over_y(both):
        return exchange(both, "y").reshape(Y, ZH, GROUP, both.shape[-1])

    pair, first_tiles = lax.optimization_barrier((halved(pair_tiles, (1, 2)), first_tiles))
    pair, first = lax.optimization_barrier((over_y(pair), halved(first_tiles, (0,))))
    pieces = []
    for parts in (over_y(first), pair):
        keep, send = fold(parts, zh)
        pieces += [keep, swap(send, "zh")]

    flags = jnp.pad(valid.astype(f32), (0, SLOT - tokens))[:, None]
    logits, weights, stats = pl.pallas_call(
        functools.partial(stats_kernel, width),
        in_specs=[WHOLE] * 5,
        out_specs=[WHOLE] * 3,
        out_shape=[
            jax.ShapeDtypeStruct((total, SLOT, width), f32),
            jax.ShapeDtypeStruct((SLOT, LANES), f32),
            jax.ShapeDtypeStruct((ZL * X, 1, 2 * LANES), f32),
        ],
        compiler_params=LIMIT,
    )(flags, *pieces)
    delta = pl.pallas_call(
        delta_kernel,
        in_specs=[WHOLE] * 3,
        out_specs=WHOLE,
        out_shape=jax.ShapeDtypeStruct((SLOT, exits * width), bf16),
        compiler_params=LIMIT,
    )(exchange(stats, PIPE), logits, weights)

    across = swap(delta, "zh")
    pair = jnp.where(zh == 0, jnp.stack([delta, across]), jnp.stack([across, delta]))
    near = spread(pair, "y").reshape(HALF, exits * width)
    far = swap(near, "c")
    half = c.reshape(1)
    partial = pl.pallas_call(
        hidden_grads_kernel,
        in_specs=[SMALL, WHOLE, WHOLE, WHOLE],
        out_specs=WHOLE,
        out_shape=jax.ShapeDtypeStruct((X, exits, PART, depth), bf16),
        compiler_params=LIMIT,
    )(half, heads, near, far)
    d_heads = pl.pallas_call(
        head_grads_kernel,
        in_specs=[SMALL, WHOLE, WHOLE, WHOLE, WHOLE],
        out_specs=WHOLE,
        out_shape=jax.ShapeDtypeStruct((exits, depth, width), bf16),
        compiler_params=LIMIT,
    )(half, first_tiles, pair_tiles, near, far)

    def up(block, step):
        pairs = [(z, z + step) for z in range(step - 1, ZL, 2 * step)]
        return lax.ppermute(block.astype(bf16), "zl", pairs)

    summed = jnp.sum(exchange(partial, "x").astype(f32), axis=0)
    tree = summed[1]
    tree = tree + up(tree, 1).astype(f32)
    come, bits = lax.optimization_barrier(
        (up(tree, 2), exchange(summed[0].astype(bf16).reshape(ZL, BIT, depth), "zl"))
    )
    tree = tree + come.astype(f32)
    bit = jnp.sum(bits.astype(f32), axis=0).astype(bf16)
    come, first = lax.optimization_barrier((up(tree, 4), spread(bit, "zl")))
    tree = (tree + come.astype(f32)).astype(bf16)
    places = zl * X + jnp.arange(X, dtype=jnp.int32)
    outgoing = jnp.where(
        (places == exit_section[1])[:, None, None], tree[None], first.reshape(1, PART, depth)
    )
    grad = exchange(outgoing, "x").reshape(ROWS, depth)
    grad = grad.reshape(C, Y, ZH, SLOT, depth)[:, :, :, :tokens].transpose(2, 1, 0, 3, 4)
    is_exit = jnp.any(exit_section == zl * X + x)
    grad = jnp.where(is_exit, grad.reshape(hidden.shape), jnp.zeros(hidden.shape, bf16))
    return d_heads, grad


def solution(mesh):
    fine = Mesh(mesh.devices.reshape(ZL, X, ZH, Y, C), ("zl", "x", "zh", "y", "c"))
    placed = (P(PIPE, None, TENSOR), P(None, TENSOR, PIPE), P(TENSOR), P())
    return jax.shard_map(
        local,
        mesh=fine,
        in_specs=placed,
        out_specs=(P(None, TENSOR, PIPE), P(PIPE, None, TENSOR)),
        check_vma=False,
    )
```

```python
import functools

import jax
import jax.numpy as jnp
from jax import lax
from jax.experimental import pallas as pl
from jax.experimental.pallas import tpu as pltpu
from jax.sharding import Mesh, PartitionSpec as P

loss_scale = 16384.0
ZL, X, ZH, Y, C = 8, 4, 2, 4, 2
PIPE = ("zl", "x")
TENSOR = ("zh", "y", "c")
SLOT = 32
ROWS = ZH * Y * C * SLOT
HALF = ROWS // 2
PART = ROWS // X
BIT = PART // ZL
LANES = 128
GROUP = 8
f32, bf16 = jnp.float32, jnp.bfloat16
SMALL = pl.BlockSpec(memory_space=pltpu.SMEM)
WHOLE = pl.BlockSpec(memory_space=pltpu.VMEM)
LIMIT = pltpu.CompilerParams(vmem_limit_bytes=40 << 20)


def swap(block, axis):
    return lax.ppermute(block, axis, [(0, 1), (1, 0)])


def exchange(block, axis):
    return lax.all_to_all(block, axis, 0, 0, tiled=True)


def spread(block, axis):
    copies = jnp.broadcast_to(block[None], (lax.axis_size(axis),) + block.shape)
    return exchange(copies, axis)


def pick(blocks, place):
    return lax.dynamic_index_in_dim(blocks, place, 0, keepdims=False)


def packed_width(count, width):
    return 3 * count * width + (width if count == 2 else 3 * LANES)


def pack(product, place, count, tally, out_ref):
    slots, width = HALF // SLOT, product.shape[1]
    groups = product.reshape(slots, 4, GROUP, width)
    for g in range(3):
        start = (g * count + place) * width
        out_ref[:, :, start : start + width] = groups[:, g]
    rest = groups[:, 3]
    base = 3 * count * width
    if count == 2:
        lower = slice(4 * place, 4 * place + 4)
        out_ref[:, lower, base : base + width] = rest[:, lower]
    else:
        cut = 3 * LANES
        out_ref[:, 0:4, base : base + cut] = rest[:, 0:4, :cut]
        out_ref[:, 4:8, base : base + width - cut] = rest[:, 4:8, cut:]
        spare = base + width - cut
        out_ref[:, 4:8, spare:] = jnp.full((slots, 4, base + cut - spare), tally, f32)


def unpack(block, place, count, width):
    rows = [
        block[:, (g * count + place) * width : (g * count + place + 1) * width] for g in range(3)
    ]
    base = 3 * count * width
    rest = block[:, base:]
    turned = pltpu.roll(rest, 4, 0)
    if count == 2:
        rows.append(turned if place else rest)
    else:
        cut = 3 * LANES
        rows.append(jnp.concatenate([rest, turned[:, : width - cut]], axis=1))
    return jnp.concatenate(rows, axis=0)


def logits_kernel(places, half_ref, tally_ref, tiles_ref, heads_ref, out_ref):
    parts = HALF // PART
    for j, place in enumerate(places):
        rows = tiles_ref[pl.ds(half_ref[0] * parts, parts), j].reshape(HALF, -1)
        product = jnp.dot(rows, heads_ref[place], preferred_element_type=f32)
        pack(product, j, len(places), tally_ref[0], out_ref)


def half_logits(tiles, heads, places, half, tally):
    count, (_, depth, width) = len(places), heads.shape
    shape = (HALF // SLOT, GROUP, packed_width(count, width))
    return pl.pallas_call(
        functools.partial(logits_kernel, places),
        in_specs=[SMALL, SMALL, WHOLE, WHOLE],
        out_specs=WHOLE,
        out_shape=jax.ShapeDtypeStruct(shape, f32),
        compiler_params=LIMIT,
        cost_estimate=pl.CostEstimate(
            flops=2 * HALF * depth * width * count,
            bytes_accessed=2 * count * depth * width + 2 * tiles.size,
            transcendentals=0,
        ),
    )(half.reshape(1), tally.reshape(1), tiles, heads)


def fold_kernel(place_ref, parts_ref, keep_ref, send_ref):
    place = place_ref[0]
    for side, out_ref in ((place, keep_ref), (1 - place, send_ref)):
        total = parts_ref[0, side]
        for i in range(1, parts_ref.shape[0]):
            total = total + parts_ref[i, side]
        out_ref[...] = total


def fold(parts, place):
    shape = jax.ShapeDtypeStruct(parts.shape[2:], f32)
    return pl.pallas_call(
        fold_kernel,
        in_specs=[SMALL, WHOLE],
        out_specs=[WHOLE, WHOLE],
        out_shape=[shape, shape],
        compiler_params=LIMIT,
    )(place.reshape(1), parts)


def stats_kernel(width, flags_ref, a_keep, a_come, b_keep, b_come, logits_ref, weights_ref, out_ref):
    first = a_keep[...] + a_come[...]
    pair = b_keep[...] + b_come[...]
    heads = [unpack(first, 0, 1, width)] + [unpack(pair, j, 2, width) for j in range(2)]
    tops, sums = [], []
    for j, logits in enumerate(heads):
        logits_ref[j] = logits
        tops.append(jnp.max(logits, axis=1, keepdims=True))
        sums.append(jnp.sum(jnp.exp(logits - tops[-1]), axis=1, keepdims=True))
    blank = jnp.zeros((LANES - len(heads) * SLOT, 1), f32)
    lane = lax.broadcasted_iota(jnp.int32, (LANES, LANES), 1)
    table = jnp.where(
        lane == 0,
        jnp.concatenate(tops + [blank], axis=0),
        jnp.where(lane == 1, jnp.concatenate(sums + [blank], axis=0), 0.0),
    ).T
    line = jnp.concatenate([table[0:1], table[1:2]], axis=1)
    out_ref[...] = jnp.broadcast_to(line[None], out_ref.shape)
    count = first[GROUP - 1 :, first.shape[1] - 1 :]
    weights_ref[...] = jnp.broadcast_to(loss_scale * flags_ref[...] / count, (SLOT, LANES))


def delta_kernel(stats_ref, logits_ref, weights_ref, out_ref):
    lines = stats_ref[...].reshape(stats_ref.shape[0], 2 * LANES)
    tops, sums = lines[:, :LANES], lines[:, LANES:]
    top = jnp.max(tops, axis=0, keepdims=True)
    total = jnp.sum(sums * jnp.exp(tops - top), axis=0, keepdims=True)
    row = lax.broadcasted_iota(jnp.int32, (LANES, LANES), 0)
    table = jnp.where(row == 0, top, jnp.where(row == 1, total, 0.0)).T
    probs = []
    for j in range(logits_ref.shape[0]):
        rows = table[j * SLOT : (j + 1) * SLOT]
        probs.append(jnp.exp(logits_ref[j] - rows[:, 0:1]) / rows[:, 1:2])
    width = logits_ref.shape[2]
    for k in range(2):
        delta = weights_ref[:, :1] * (probs[k] - probs[2])
        out_ref[:, k * width : (k + 1) * width] = delta.astype(bf16)


def hidden_grads_kernel(half_ref, heads_ref, near_ref, far_ref, out_ref):
    exits, width = out_ref.shape[1], heads_ref.shape[2]
    parts = HALF // PART
    for place, delta_ref in ((half_ref[0], near_ref), (1 - half_ref[0], far_ref)):
        for k in range(exits):
            grad = lax.dot_general(
                delta_ref[:, k * width : (k + 1) * width],
                heads_ref[k],
                (((1,), (1,)), ((), ())),
                preferred_element_type=f32,
            )
            out_ref[pl.ds(place * parts, parts), k] = grad.reshape(parts, PART, -1).astype(bf16)


def head_grads_kernel(half_ref, first_ref, pair_ref, near_ref, far_ref, out_ref):
    exits, _, width = out_ref.shape
    parts = HALF // PART
    for k, tiles_ref in enumerate((first_ref, pair_ref)):
        total = None
        for place, delta_ref in ((half_ref[0], near_ref), (1 - half_ref[0], far_ref)):
            rows = tiles_ref[pl.ds(place * parts, parts), 0].reshape(HALF, -1)
            term = lax.dot_general(
                rows,
                delta_ref[:, k * width : (k + 1) * width],
                (((0,), (0,)), ((), ())),
                preferred_element_type=f32,
            )
            total = term if total is None else total + term
        out_ref[k] = total.astype(bf16)


def local(hidden, heads, valid, exit_section):
    total, depth, width = heads.shape
    exits = total - 1
    tokens = valid.shape[0]
    zl, x, c = lax.axis_index("zl"), lax.axis_index("x"), lax.axis_index("c")
    zh = lax.axis_index("zh")
    last = ZL * X - 1
    dynamic = exit_section[0]

    own = hidden[0].reshape(ZH, Y, C, tokens, depth).transpose(2, 1, 0, 3, 4)
    own = jnp.concatenate([own, own[:, :, :, 2 * tokens - SLOT :]], axis=3).reshape(ROWS, depth)
    row_parts = exchange(own, "x").reshape(X, PART, depth)

    def down(step):
        pairs = [(z, z - step) for z in range(ZL - 1, -1, -2 * step)]
        return lax.ppermute(tree, "zl", pairs)

    def across_zl(step):
        return lax.ppermute(first, "zl", [(z, z ^ step) for z in range(ZL)])

    def grown(come, step):
        return jnp.where((zl % (2 * step)) == step - 1, come, tree)

    def taken(come, step):
        return jnp.where((zl ^ (dynamic // X)) & step != 0, come, first)

    tree = jnp.stack([pick(row_parts, exit_section[1] % X), row_parts[last % X]])
    first = pick(row_parts, dynamic % X)
    first_come = across_zl(4)
    tree = grown(down(4), 4)
    tree_come, first_come = lax.optimization_barrier((down(2), first_come))
    tree, first = grown(tree_come, 2), taken(first_come, 4)
    tree = grown(down(1), 1)
    pair_tiles, first_come = lax.optimization_barrier((spread(tree, "x"), across_zl(2)))
    first = taken(first_come, 2)

    tally = jnp.sum(valid.astype(f32))
    def halved(tiles, places):
        send = half_logits(tiles, heads, places, 1 - c, tally)
        return half_logits(tiles, heads, places, c, tally) + swap(send, "c")

    def over_y(both):
        return exchange(both, "y").reshape(Y, ZH, GROUP, both.shape[-1])

    parts, first_come = lax.optimization_barrier(
        (over_y(halved(pair_tiles, (1, 2))), across_zl(1))
    )
    first = taken(first_come, 1)
    pair_keep, send = fold(parts, zh)
    first_tiles = spread(first[None], "x").reshape(X, 1, PART, depth)
    both, pair_come = lax.optimization_barrier((halved(first_tiles, (0,)), swap(send, "zh")))
    first_keep, send = fold(over_y(both), zh)
    pieces = (first_keep, swap(send, "zh"), pair_keep, pair_come)

    flags = jnp.pad(valid.astype(f32), (0, SLOT - tokens))[:, None]
    logits, weights, stats = pl.pallas_call(
        functools.partial(stats_kernel, width),
        in_specs=[WHOLE] * 5,
        out_specs=[WHOLE] * 3,
        out_shape=[
            jax.ShapeDtypeStruct((total, SLOT, width), f32),
            jax.ShapeDtypeStruct((SLOT, LANES), f32),
            jax.ShapeDtypeStruct((ZL * X, 1, 2 * LANES), f32),
        ],
        compiler_params=LIMIT,
    )(flags, *pieces)
    delta = pl.pallas_call(
        delta_kernel,
        in_specs=[WHOLE] * 3,
        out_specs=WHOLE,
        out_shape=jax.ShapeDtypeStruct((SLOT, exits * width), bf16),
        compiler_params=LIMIT,
    )(exchange(stats, PIPE), logits, weights)

    across = swap(delta, "zh")
    pair = jnp.where(zh == 0, jnp.stack([delta, across]), jnp.stack([across, delta]))
    near = spread(pair, "y").reshape(HALF, exits * width)
    far = swap(near, "c")
    half = c.reshape(1)
    partial = pl.pallas_call(
        hidden_grads_kernel,
        in_specs=[SMALL, WHOLE, WHOLE, WHOLE],
        out_specs=WHOLE,
        out_shape=jax.ShapeDtypeStruct((X, exits, PART, depth), bf16),
        compiler_params=LIMIT,
    )(half, heads, near, far)
    d_heads = pl.pallas_call(
        head_grads_kernel,
        in_specs=[SMALL, WHOLE, WHOLE, WHOLE, WHOLE],
        out_specs=WHOLE,
        out_shape=jax.ShapeDtypeStruct((exits, depth, width), bf16),
        compiler_params=LIMIT,
    )(half, first_tiles, pair_tiles, near, far)

    def up(block, step):
        pairs = [(z, z + step) for z in range(step - 1, ZL, 2 * step)]
        return lax.ppermute(block.astype(bf16), "zl", pairs)

    summed = jnp.sum(exchange(partial, "x").astype(f32), axis=0)
    tree = summed[1]
    tree = tree + up(tree, 1).astype(f32)
    come, bits = lax.optimization_barrier(
        (up(tree, 2), exchange(summed[0].astype(bf16).reshape(ZL, BIT, depth), "zl"))
    )
    tree = tree + come.astype(f32)
    bit = jnp.sum(bits.astype(f32), axis=0).astype(bf16)
    come, first = lax.optimization_barrier((up(tree, 4), spread(bit, "zl")))
    tree = (tree + come.astype(f32)).astype(bf16)
    places = zl * X + jnp.arange(X, dtype=jnp.int32)
    outgoing = jnp.where(
        (places == exit_section[1])[:, None, None], tree[None], first.reshape(1, PART, depth)
    )
    grad = exchange(outgoing, "x").reshape(ROWS, depth)
    grad = grad.reshape(C, Y, ZH, SLOT, depth)[:, :, :, :tokens].transpose(2, 1, 0, 3, 4)
    is_exit = jnp.any(exit_section == zl * X + x)
    grad = jnp.where(is_exit, grad.reshape(hidden.shape), jnp.zeros(hidden.shape, bf16))
    return d_heads, grad


def solution(mesh):
    fine = Mesh(mesh.devices.reshape(ZL, X, ZH, Y, C), ("zl", "x", "zh", "y", "c"))
    placed = (P(PIPE, None, TENSOR), P(None, TENSOR, PIPE), P(TENSOR), P())
    return jax.shard_map(
        local,
        mesh=fine,
        in_specs=placed,
        out_specs=(P(None, TENSOR, PIPE), P(PIPE, None, TENSOR)),
        check_vma=False,
    )
```

```python
import functools

import jax
import jax.numpy as jnp
from jax import lax
from jax.experimental import pallas as pl
from jax.experimental.pallas import tpu as pltpu
from jax.sharding import Mesh, PartitionSpec as P

loss_scale = 16384.0
ZL, X, ZH, Y, C = 8, 4, 2, 4, 2
PIPE = ("zl", "x")
TENSOR = ("zh", "y", "c")
SLOT = 32
ROWS = ZH * Y * C * SLOT
HALF = ROWS // 2
PART = ROWS // X
BIT = PART // ZL
LANES = 128
GROUP = 8
f32, bf16 = jnp.float32, jnp.bfloat16
SMALL = pl.BlockSpec(memory_space=pltpu.SMEM)
WHOLE = pl.BlockSpec(memory_space=pltpu.VMEM)
LIMIT = pltpu.CompilerParams(vmem_limit_bytes=40 << 20)


def swap(block, axis):
    return lax.ppermute(block, axis, [(0, 1), (1, 0)])


def exchange(block, axis):
    return lax.all_to_all(block, axis, 0, 0, tiled=True)


def spread(block, axis):
    copies = jnp.broadcast_to(block[None], (lax.axis_size(axis),) + block.shape)
    return exchange(copies, axis)


def pick(blocks, place):
    return lax.dynamic_index_in_dim(blocks, place, 0, keepdims=False)


def packed_width(count, width):
    return 3 * count * width + (width if count == 2 else 3 * LANES)


def pack(product, place, count, tally, out_ref):
    slots, width = HALF // SLOT, product.shape[1]
    groups = product.reshape(slots, 4, GROUP, width)
    for g in range(3):
        start = (g * count + place) * width
        out_ref[:, :, start : start + width] = groups[:, g]
    rest = groups[:, 3]
    base = 3 * count * width
    if count == 2:
        lower = slice(4 * place, 4 * place + 4)
        out_ref[:, lower, base : base + width] = rest[:, lower]
    else:
        cut = 3 * LANES
        out_ref[:, 0:4, base : base + cut] = rest[:, 0:4, :cut]
        out_ref[:, 4:8, base : base + width - cut] = rest[:, 4:8, cut:]
        spare = base + width - cut
        out_ref[:, 4:8, spare:] = jnp.full((slots, 4, base + cut - spare), tally, f32)


def unpack(block, place, count, width):
    rows = [
        block[:, (g * count + place) * width : (g * count + place + 1) * width] for g in range(3)
    ]
    base = 3 * count * width
    rest = block[:, base:]
    turned = pltpu.roll(rest, 4, 0)
    if count == 2:
        rows.append(turned if place else rest)
    else:
        cut = 3 * LANES
        rows.append(jnp.concatenate([rest, turned[:, : width - cut]], axis=1))
    return jnp.concatenate(rows, axis=0)


def logits_kernel(places, half_ref, tally_ref, tiles_ref, heads_ref, out_ref):
    parts = HALF // PART
    for j, place in enumerate(places):
        rows = tiles_ref[pl.ds(half_ref[0] * parts, parts), j].reshape(HALF, -1)
        product = jnp.dot(rows, heads_ref[place], preferred_element_type=f32)
        pack(product, j, len(places), tally_ref[0], out_ref)


def half_logits(tiles, heads, places, half, tally):
    count, (_, depth, width) = len(places), heads.shape
    shape = (HALF // SLOT, GROUP, packed_width(count, width))
    return pl.pallas_call(
        functools.partial(logits_kernel, places),
        in_specs=[SMALL, SMALL, WHOLE, WHOLE],
        out_specs=WHOLE,
        out_shape=jax.ShapeDtypeStruct(shape, f32),
        compiler_params=LIMIT,
        cost_estimate=pl.CostEstimate(
            flops=2 * HALF * depth * width * count,
            bytes_accessed=2 * count * depth * width + 2 * tiles.size,
            transcendentals=0,
        ),
    )(half.reshape(1), tally.reshape(1), tiles, heads)


def fold_kernel(place_ref, parts_ref, keep_ref, send_ref):
    place = place_ref[0]
    for side, out_ref in ((place, keep_ref), (1 - place, send_ref)):
        total = parts_ref[0, side]
        for i in range(1, parts_ref.shape[0]):
            total = total + parts_ref[i, side]
        out_ref[...] = total


def fold(parts, place):
    shape = jax.ShapeDtypeStruct(parts.shape[2:], f32)
    return pl.pallas_call(
        fold_kernel,
        in_specs=[SMALL, WHOLE],
        out_specs=[WHOLE, WHOLE],
        out_shape=[shape, shape],
        compiler_params=LIMIT,
    )(place.reshape(1), parts)


def stats_kernel(width, flags_ref, a_keep, a_come, b_keep, b_come, logits_ref, weights_ref, out_ref):
    first = a_keep[...] + a_come[...]
    pair = b_keep[...] + b_come[...]
    heads = [unpack(first, 0, 1, width)] + [unpack(pair, j, 2, width) for j in range(2)]
    tops, sums = [], []
    for j, logits in enumerate(heads):
        logits_ref[j] = logits
        tops.append(jnp.max(logits, axis=1, keepdims=True))
        sums.append(jnp.sum(jnp.exp(logits - tops[-1]), axis=1, keepdims=True))
    blank = jnp.zeros((LANES - len(heads) * SLOT, 1), f32)
    lane = lax.broadcasted_iota(jnp.int32, (LANES, LANES), 1)
    table = jnp.where(
        lane == 0,
        jnp.concatenate(tops + [blank], axis=0),
        jnp.where(lane == 1, jnp.concatenate(sums + [blank], axis=0), 0.0),
    ).T
    line = jnp.concatenate([table[0:1], table[1:2]], axis=1)
    out_ref[...] = jnp.broadcast_to(line[None], out_ref.shape)
    count = first[GROUP - 1 :, first.shape[1] - 1 :]
    weights_ref[...] = jnp.broadcast_to(loss_scale * flags_ref[...] / count, (SLOT, LANES))


def delta_kernel(stats_ref, logits_ref, weights_ref, out_ref):
    lines = stats_ref[...].reshape(stats_ref.shape[0], 2 * LANES)
    tops, sums = lines[:, :LANES], lines[:, LANES:]
    top = jnp.max(tops, axis=0, keepdims=True)
    total = jnp.sum(sums * jnp.exp(tops - top), axis=0, keepdims=True)
    row = lax.broadcasted_iota(jnp.int32, (LANES, LANES), 0)
    table = jnp.where(row == 0, top, jnp.where(row == 1, total, 0.0)).T
    probs = []
    for j in range(logits_ref.shape[0]):
        rows = table[j * SLOT : (j + 1) * SLOT]
        probs.append(jnp.exp(logits_ref[j] - rows[:, 0:1]) / rows[:, 1:2])
    width = logits_ref.shape[2]
    for k in range(2):
        delta = weights_ref[:, :1] * (probs[k] - probs[2])
        out_ref[:, k * width : (k + 1) * width] = delta.astype(bf16)


def hidden_grads_kernel(half_ref, heads_ref, near_ref, far_ref, out_ref):
    exits, width = out_ref.shape[1], heads_ref.shape[2]
    parts = HALF // PART
    for place, delta_ref in ((half_ref[0], near_ref), (1 - half_ref[0], far_ref)):
        for k in range(exits):
            grad = lax.dot_general(
                delta_ref[:, k * width : (k + 1) * width],
                heads_ref[k],
                (((1,), (1,)), ((), ())),
                preferred_element_type=f32,
            )
            out_ref[pl.ds(place * parts, parts), k] = grad.reshape(parts, PART, -1).astype(bf16)


def head_grads_kernel(half_ref, first_ref, pair_ref, near_ref, far_ref, out_ref):
    exits, _, width = out_ref.shape
    parts = HALF // PART
    for k, tiles_ref in enumerate((first_ref, pair_ref)):
        total = None
        for place, delta_ref in ((half_ref[0], near_ref), (1 - half_ref[0], far_ref)):
            rows = tiles_ref[pl.ds(place * parts, parts), 0].reshape(HALF, -1)
            term = lax.dot_general(
                rows,
                delta_ref[:, k * width : (k + 1) * width],
                (((0,), (0,)), ((), ())),
                preferred_element_type=f32,
            )
            total = term if total is None else total + term
        out_ref[k] = total.astype(bf16)


def local(hidden, heads, valid, exit_section):
    total, depth, width = heads.shape
    exits = total - 1
    tokens = valid.shape[0]
    zl, x, c = lax.axis_index("zl"), lax.axis_index("x"), lax.axis_index("c")
    zh = lax.axis_index("zh")
    last = ZL * X - 1
    dynamic = exit_section[0]

    own = hidden[0].reshape(ZH, Y, C, tokens, depth).transpose(2, 1, 0, 3, 4)
    own = jnp.concatenate([own, own[:, :, :, 2 * tokens - SLOT :]], axis=3).reshape(ROWS, depth)
    row_parts = exchange(own, "x").reshape(X, PART, depth)

    def down(step):
        pairs = [(z, z - step) for z in range(ZL - 1, -1, -2 * step)]
        return lax.ppermute(tree, "zl", pairs)

    def across_zl(step):
        return lax.ppermute(first, "zl", [(z, z ^ step) for z in range(ZL)])

    def grown(come, step):
        return jnp.where((zl % (2 * step)) == step - 1, come, tree)

    def taken(come, step):
        return jnp.where((zl ^ (dynamic // X)) & step != 0, come, first)

    tree = jnp.stack([pick(row_parts, exit_section[1] % X), row_parts[last % X]])
    first = pick(row_parts, dynamic % X)
    first_come = across_zl(4)
    tree = grown(down(4), 4)
    tree_come, first_come = lax.optimization_barrier((down(2), first_come))
    tree, first = grown(tree_come, 2), taken(first_come, 4)
    tree = grown(down(1), 1)
    first = taken(across_zl(2), 2)
    pair_tiles, first_come = lax.optimization_barrier((spread(tree, "x"), across_zl(1)))
    first = taken(first_come, 1)

    def over_x(i):
        return lax.ppermute(first, "x", [(n, n ^ i) for n in range(X)])

    def swapped(low, high, bit):
        flip = x & bit != 0
        return [jnp.where(flip, b, a) for a, b in ((low, high), (high, low))]

    a, b = swapped(first, over_x(1), 1)
    d, e = swapped(over_x(2), over_x(3), 1)
    low, high = swapped(jnp.stack([a, b]), jnp.stack([d, e]), 2)
    first_tiles = jnp.concatenate([low, high])[:, None]

    tally = jnp.sum(valid.astype(f32))
    def halved(tiles, places):
        send = half_logits(tiles, heads, places, 1 - c, tally)
        return half_logits(tiles, heads, places, c, tally) + swap(send, "c")

    def over_y(both):
        return exchange(both, "y").reshape(Y, ZH, GROUP, both.shape[-1])

    pair, first = lax.optimization_barrier(
        (over_y(halved(pair_tiles, (1, 2))), halved(first_tiles, (0,)))
    )
    pieces = []
    for parts in (over_y(first), pair):
        keep, send = fold(parts, zh)
        pieces += [keep, swap(send, "zh")]

    flags = jnp.pad(valid.astype(f32), (0, SLOT - tokens))[:, None]
    logits, weights, stats = pl.pallas_call(
        functools.partial(stats_kernel, width),
        in_specs=[WHOLE] * 5,
        out_specs=[WHOLE] * 3,
        out_shape=[
            jax.ShapeDtypeStruct((total, SLOT, width), f32),
            jax.ShapeDtypeStruct((SLOT, LANES), f32),
            jax.ShapeDtypeStruct((ZL * X, 1, 2 * LANES), f32),
        ],
        compiler_params=LIMIT,
    )(flags, *pieces)
    delta = pl.pallas_call(
        delta_kernel,
        in_specs=[WHOLE] * 3,
        out_specs=WHOLE,
        out_shape=jax.ShapeDtypeStruct((SLOT, exits * width), bf16),
        compiler_params=LIMIT,
    )(exchange(stats, PIPE), logits, weights)

    across = swap(delta, "zh")
    pair = jnp.where(zh == 0, jnp.stack([delta, across]), jnp.stack([across, delta]))
    near = spread(pair, "y").reshape(HALF, exits * width)
    far = swap(near, "c")
    half = c.reshape(1)
    partial = pl.pallas_call(
        hidden_grads_kernel,
        in_specs=[SMALL, WHOLE, WHOLE, WHOLE],
        out_specs=WHOLE,
        out_shape=jax.ShapeDtypeStruct((X, exits, PART, depth), bf16),
        compiler_params=LIMIT,
    )(half, heads, near, far)
    d_heads = pl.pallas_call(
        head_grads_kernel,
        in_specs=[SMALL, WHOLE, WHOLE, WHOLE, WHOLE],
        out_specs=WHOLE,
        out_shape=jax.ShapeDtypeStruct((exits, depth, width), bf16),
        compiler_params=LIMIT,
    )(half, first_tiles, pair_tiles, near, far)

    def up(block, step):
        pairs = [(z, z + step) for z in range(step - 1, ZL, 2 * step)]
        return lax.ppermute(block.astype(bf16), "zl", pairs)

    summed = jnp.sum(exchange(partial, "x").astype(f32), axis=0)
    tree = summed[1]
    tree = tree + up(tree, 1).astype(f32)
    come, bits = lax.optimization_barrier(
        (up(tree, 2), exchange(summed[0].astype(bf16).reshape(ZL, BIT, depth), "zl"))
    )
    tree = tree + come.astype(f32)
    bit = jnp.sum(bits.astype(f32), axis=0).astype(bf16)
    come, first = lax.optimization_barrier((up(tree, 4), spread(bit, "zl")))
    tree = (tree + come.astype(f32)).astype(bf16)
    places = zl * X + jnp.arange(X, dtype=jnp.int32)
    outgoing = jnp.where(
        (places == exit_section[1])[:, None, None], tree[None], first.reshape(1, PART, depth)
    )
    grad = exchange(outgoing, "x").reshape(ROWS, depth)
    grad = grad.reshape(C, Y, ZH, SLOT, depth)[:, :, :, :tokens].transpose(2, 1, 0, 3, 4)
    is_exit = jnp.any(exit_section == zl * X + x)
    grad = jnp.where(is_exit, grad.reshape(hidden.shape), jnp.zeros(hidden.shape, bf16))
    return d_heads, grad


def solution(mesh):
    fine = Mesh(mesh.devices.reshape(ZL, X, ZH, Y, C), ("zl", "x", "zh", "y", "c"))
    placed = (P(PIPE, None, TENSOR), P(None, TENSOR, PIPE), P(TENSOR), P())
    return jax.shard_map(
        local,
        mesh=fine,
        in_specs=placed,
        out_specs=(P(None, TENSOR, PIPE), P(PIPE, None, TENSOR)),
        check_vma=False,
    )
```

```python
import functools

import jax
import jax.numpy as jnp
from jax import lax
from jax.experimental import pallas as pl
from jax.experimental.pallas import tpu as pltpu
from jax.sharding import Mesh, PartitionSpec as P

loss_scale = 16384.0
ZL, X, ZH, Y, C = 8, 4, 2, 4, 2
PIPE = ("zl", "x")
TENSOR = ("zh", "y", "c")
SLOT = 32
ROWS = ZH * Y * C * SLOT
HALF = ROWS // 2
PART = ROWS // X
BIT = PART // ZL
LANES = 128
GROUP = 8
f32, bf16 = jnp.float32, jnp.bfloat16
SMALL = pl.BlockSpec(memory_space=pltpu.SMEM)
WHOLE = pl.BlockSpec(memory_space=pltpu.VMEM)
LIMIT = pltpu.CompilerParams(vmem_limit_bytes=40 << 20)


def swap(block, axis):
    return lax.ppermute(block, axis, [(0, 1), (1, 0)])


def exchange(block, axis):
    return lax.all_to_all(block, axis, 0, 0, tiled=True)


def spread(block, axis):
    copies = jnp.broadcast_to(block[None], (lax.axis_size(axis),) + block.shape)
    return exchange(copies, axis)


def pick(blocks, place):
    return lax.dynamic_index_in_dim(blocks, place, 0, keepdims=False)


def slot_orders():
    for c in range(C):
        for y in range(Y):
            for zh in range(ZH):
                yield (c * Y + y) * ZH + zh, (zh * Y + y) * C + c


def to_slots_kernel(tokens, rows_ref, out_ref):
    rows = rows_ref[...].astype(f32)
    for slot, place in slot_orders():
        block = rows[place * tokens : (place + 1) * tokens]
        block = jnp.concatenate([block, block[2 * tokens - SLOT :]], axis=0)
        out_ref[slot * SLOT : (slot + 1) * SLOT] = block.astype(bf16)


def from_slots_kernel(tokens, mask_ref, slots_ref, out_ref):
    blocks = [None] * (ZH * Y * C)
    for slot, place in slot_orders():
        rows = slots_ref[slot * SLOT : (slot + 1) * SLOT].astype(f32)
        blocks[place] = rows[:tokens]
    rows = jnp.concatenate(blocks, axis=0)
    out_ref[...] = jnp.where(mask_ref[0] != 0, rows, 0.0).astype(bf16)


def packed_width(count, width):
    return 3 * count * width + (width if count == 2 else 3 * LANES)


def pack(product, place, count, tally, out_ref):
    slots, width = HALF // SLOT, product.shape[1]
    groups = product.reshape(slots, 4, GROUP, width)
    for g in range(3):
        start = (g * count + place) * width
        out_ref[:, :, start : start + width] = groups[:, g]
    rest = groups[:, 3]
    base = 3 * count * width
    if count == 2:
        lower = slice(4 * place, 4 * place + 4)
        out_ref[:, lower, base : base + width] = rest[:, lower]
    else:
        cut = 3 * LANES
        out_ref[:, 0:4, base : base + cut] = rest[:, 0:4, :cut]
        out_ref[:, 4:8, base : base + width - cut] = rest[:, 4:8, cut:]
        spare = base + width - cut
        out_ref[:, 4:8, spare:] = jnp.full((slots, 4, base + cut - spare), tally, f32)


def unpack(block, place, count, width):
    rows = [
        block[:, (g * count + place) * width : (g * count + place + 1) * width] for g in range(3)
    ]
    base = 3 * count * width
    rest = block[:, base:]
    turned = pltpu.roll(rest, 4, 0)
    if count == 2:
        rows.append(turned if place else rest)
    else:
        cut = 3 * LANES
        rows.append(jnp.concatenate([rest, turned[:, : width - cut]], axis=1))
    return jnp.concatenate(rows, axis=0)


def logits_kernel(places, half_ref, tally_ref, tiles_ref, heads_ref, out_ref):
    parts = HALF // PART
    for j, place in enumerate(places):
        rows = tiles_ref[pl.ds(half_ref[0] * parts, parts), j].reshape(HALF, -1)
        product = jnp.dot(rows, heads_ref[place], preferred_element_type=f32)
        pack(product, j, len(places), tally_ref[0], out_ref)


def half_logits(tiles, heads, places, half, tally):
    count, (_, depth, width) = len(places), heads.shape
    shape = (HALF // SLOT, GROUP, packed_width(count, width))
    return pl.pallas_call(
        functools.partial(logits_kernel, places),
        in_specs=[SMALL, SMALL, WHOLE, WHOLE],
        out_specs=WHOLE,
        out_shape=jax.ShapeDtypeStruct(shape, f32),
        compiler_params=LIMIT,
        cost_estimate=pl.CostEstimate(
            flops=2 * HALF * depth * width * count,
            bytes_accessed=2 * count * depth * width + 2 * tiles.size,
            transcendentals=0,
        ),
    )(half.reshape(1), tally.reshape(1), tiles, heads)


def fold_kernel(place_ref, parts_ref, keep_ref, send_ref):
    place = place_ref[0]
    for side, out_ref in ((place, keep_ref), (1 - place, send_ref)):
        total = parts_ref[0, side]
        for i in range(1, parts_ref.shape[0]):
            total = total + parts_ref[i, side]
        out_ref[...] = total


def fold(parts, place):
    shape = jax.ShapeDtypeStruct(parts.shape[2:], f32)
    return pl.pallas_call(
        fold_kernel,
        in_specs=[SMALL, WHOLE],
        out_specs=[WHOLE, WHOLE],
        out_shape=[shape, shape],
        compiler_params=LIMIT,
    )(place.reshape(1), parts)


def stats_kernel(width, flags_ref, a_keep, a_come, b_keep, b_come, logits_ref, weights_ref, out_ref):
    first = a_keep[...] + a_come[...]
    pair = b_keep[...] + b_come[...]
    heads = [unpack(first, 0, 1, width)] + [unpack(pair, j, 2, width) for j in range(2)]
    tops, sums = [], []
    for j, logits in enumerate(heads):
        logits_ref[j] = logits
        tops.append(jnp.max(logits, axis=1, keepdims=True))
        sums.append(jnp.sum(jnp.exp(logits - tops[-1]), axis=1, keepdims=True))
    blank = jnp.zeros((LANES - len(heads) * SLOT, 1), f32)
    lane = lax.broadcasted_iota(jnp.int32, (LANES, LANES), 1)
    table = jnp.where(
        lane == 0,
        jnp.concatenate(tops + [blank], axis=0),
        jnp.where(lane == 1, jnp.concatenate(sums + [blank], axis=0), 0.0),
    ).T
    line = jnp.concatenate([table[0:1], table[1:2]], axis=1)
    out_ref[...] = jnp.broadcast_to(line[None], out_ref.shape)
    count = first[GROUP - 1 :, first.shape[1] - 1 :]
    weights_ref[...] = jnp.broadcast_to(loss_scale * flags_ref[...] / count, (SLOT, LANES))


def delta_kernel(stats_ref, logits_ref, weights_ref, out_ref):
    lines = stats_ref[...].reshape(stats_ref.shape[0], 2 * LANES)
    tops, sums = lines[:, :LANES], lines[:, LANES:]
    top = jnp.max(tops, axis=0, keepdims=True)
    total = jnp.sum(sums * jnp.exp(tops - top), axis=0, keepdims=True)
    row = lax.broadcasted_iota(jnp.int32, (LANES, LANES), 0)
    table = jnp.where(row == 0, top, jnp.where(row == 1, total, 0.0)).T
    probs = []
    for j in range(logits_ref.shape[0]):
        rows = table[j * SLOT : (j + 1) * SLOT]
        probs.append(jnp.exp(logits_ref[j] - rows[:, 0:1]) / rows[:, 1:2])
    width = logits_ref.shape[2]
    for k in range(2):
        delta = weights_ref[:, :1] * (probs[k] - probs[2])
        out_ref[:, k * width : (k + 1) * width] = delta.astype(bf16)


def hidden_grads_kernel(half_ref, heads_ref, near_ref, far_ref, out_ref):
    exits, width = out_ref.shape[1], heads_ref.shape[2]
    parts = HALF // PART
    for place, delta_ref in ((half_ref[0], near_ref), (1 - half_ref[0], far_ref)):
        for k in range(exits):
            grad = lax.dot_general(
                delta_ref[:, k * width : (k + 1) * width],
                heads_ref[k],
                (((1,), (1,)), ((), ())),
                preferred_element_type=f32,
            )
            out_ref[pl.ds(place * parts, parts), k] = grad.reshape(parts, PART, -1).astype(bf16)


def head_grads_kernel(half_ref, first_ref, pair_ref, near_ref, far_ref, out_ref):
    exits, _, width = out_ref.shape
    parts = HALF // PART
    for k, tiles_ref in enumerate((first_ref, pair_ref)):
        total = None
        for place, delta_ref in ((half_ref[0], near_ref), (1 - half_ref[0], far_ref)):
            rows = tiles_ref[pl.ds(place * parts, parts), 0].reshape(HALF, -1)
            term = lax.dot_general(
                rows,
                delta_ref[:, k * width : (k + 1) * width],
                (((0,), (0,)), ((), ())),
                preferred_element_type=f32,
            )
            total = term if total is None else total + term
        out_ref[k] = total.astype(bf16)


def local(hidden, heads, valid, exit_section):
    total, depth, width = heads.shape
    exits = total - 1
    tokens = valid.shape[0]
    zl, x, c = lax.axis_index("zl"), lax.axis_index("x"), lax.axis_index("c")
    zh = lax.axis_index("zh")
    last = ZL * X - 1
    dynamic = exit_section[0]

    own = pl.pallas_call(
        functools.partial(to_slots_kernel, tokens),
        in_specs=[WHOLE],
        out_specs=WHOLE,
        out_shape=jax.ShapeDtypeStruct((ROWS, depth), bf16),
        compiler_params=LIMIT,
    )(hidden[0])
    row_parts = exchange(own, "x").reshape(X, PART, depth)

    def down(step):
        pairs = [(z, z - step) for z in range(ZL - 1, -1, -2 * step)]
        return lax.ppermute(tree, "zl", pairs)

    def across_zl(step):
        return lax.ppermute(first, "zl", [(z, z ^ step) for z in range(ZL)])

    def grown(come, step):
        return jnp.where((zl % (2 * step)) == step - 1, come, tree)

    def taken(come, step):
        return jnp.where((zl ^ (dynamic // X)) & step != 0, come, first)

    tree = jnp.stack([pick(row_parts, exit_section[1] % X), row_parts[last % X]])
    first = pick(row_parts, dynamic % X)
    for step in (4, 2):
        tree_come, first_come = lax.optimization_barrier((down(step), across_zl(4 // step)))
        tree, first = grown(tree_come, step), taken(first_come, 4 // step)
    tree = grown(down(1), 1)
    pair_tiles, first_come = lax.optimization_barrier((spread(tree, "x"), across_zl(4)))
    first = taken(first_come, 4)
    first_tiles = spread(first[None], "x").reshape(X, 1, PART, depth)

    tally = jnp.sum(valid.astype(f32))
    def halved(tiles, places):
        send = half_logits(tiles, heads, places, 1 - c, tally)
        return half_logits(tiles, heads, places, c, tally) + swap(send, "c")

    def over_y(both):
        return exchange(both, "y").reshape(Y, ZH, GROUP, both.shape[-1])

    pair, first_tiles = lax.optimization_barrier((halved(pair_tiles, (1, 2)), first_tiles))
    pair, first = lax.optimization_barrier((over_y(pair), halved(first_tiles, (0,))))
    pieces = []
    for parts in (over_y(first), pair):
        keep, send = fold(parts, zh)
        pieces += [keep, swap(send, "zh")]

    flags = jnp.pad(valid.astype(f32), (0, SLOT - tokens))[:, None]
    logits, weights, stats = pl.pallas_call(
        functools.partial(stats_kernel, width),
        in_specs=[WHOLE] * 5,
        out_specs=[WHOLE] * 3,
        out_shape=[
            jax.ShapeDtypeStruct((total, SLOT, width), f32),
            jax.ShapeDtypeStruct((SLOT, LANES), f32),
            jax.ShapeDtypeStruct((ZL * X, 1, 2 * LANES), f32),
        ],
        compiler_params=LIMIT,
    )(flags, *pieces)
    delta = pl.pallas_call(
        delta_kernel,
        in_specs=[WHOLE] * 3,
        out_specs=WHOLE,
        out_shape=jax.ShapeDtypeStruct((SLOT, exits * width), bf16),
        compiler_params=LIMIT,
    )(exchange(stats, PIPE), logits, weights)

    across = swap(delta, "zh")
    pair = jnp.where(zh == 0, jnp.stack([delta, across]), jnp.stack([across, delta]))
    near = spread(pair, "y").reshape(HALF, exits * width)
    far = swap(near, "c")
    half = c.reshape(1)
    partial = pl.pallas_call(
        hidden_grads_kernel,
        in_specs=[SMALL, WHOLE, WHOLE, WHOLE],
        out_specs=WHOLE,
        out_shape=jax.ShapeDtypeStruct((X, exits, PART, depth), bf16),
        compiler_params=LIMIT,
    )(half, heads, near, far)
    d_heads = pl.pallas_call(
        head_grads_kernel,
        in_specs=[SMALL, WHOLE, WHOLE, WHOLE, WHOLE],
        out_specs=WHOLE,
        out_shape=jax.ShapeDtypeStruct((exits, depth, width), bf16),
        compiler_params=LIMIT,
    )(half, first_tiles, pair_tiles, near, far)

    def up(block, step):
        pairs = [(z, z + step) for z in range(step - 1, ZL, 2 * step)]
        return lax.ppermute(block.astype(bf16), "zl", pairs)

    summed = jnp.sum(exchange(partial, "x").astype(f32), axis=0)
    tree = summed[1]
    tree = tree + up(tree, 1).astype(f32)
    come, bits = lax.optimization_barrier(
        (up(tree, 2), exchange(summed[0].astype(bf16).reshape(ZL, BIT, depth), "zl"))
    )
    tree = tree + come.astype(f32)
    bit = jnp.sum(bits.astype(f32), axis=0).astype(bf16)
    come, first = lax.optimization_barrier((up(tree, 4), spread(bit, "zl")))
    tree = (tree + come.astype(f32)).astype(bf16)
    places = zl * X + jnp.arange(X, dtype=jnp.int32)
    outgoing = jnp.where(
        (places == exit_section[1])[:, None, None], tree[None], first.reshape(1, PART, depth)
    )
    mask = jnp.any(exit_section == zl * X + x).astype(jnp.int32).reshape(1)
    grad = pl.pallas_call(
        functools.partial(from_slots_kernel, tokens),
        in_specs=[SMALL, WHOLE],
        out_specs=WHOLE,
        out_shape=jax.ShapeDtypeStruct(hidden.shape[1:], bf16),
        compiler_params=LIMIT,
    )(mask, exchange(outgoing, "x").reshape(ROWS, depth))
    grad = grad[None]
    return d_heads, grad


def solution(mesh):
    fine = Mesh(mesh.devices.reshape(ZL, X, ZH, Y, C), ("zl", "x", "zh", "y", "c"))
    placed = (P(PIPE, None, TENSOR), P(None, TENSOR, PIPE), P(TENSOR), P())
    return jax.shard_map(
        local,
        mesh=fine,
        in_specs=placed,
        out_specs=(P(None, TENSOR, PIPE), P(PIPE, None, TENSOR)),
        check_vma=False,
    )
```

```python
import functools

import jax
import jax.numpy as jnp
from jax import lax
from jax.experimental import pallas as pl
from jax.experimental.pallas import tpu as pltpu
from jax.sharding import Mesh, PartitionSpec as P

loss_scale = 16384.0
ZL, X, ZH, Y, C = 8, 4, 2, 4, 2
PIPE = ("zl", "x")
TENSOR = ("zh", "y", "c")
SLOT = 32
ROWS = ZH * Y * C * SLOT
HALF = ROWS // 2
PART = ROWS // X
BIT = PART // ZL
LANES = 128
GROUP = 8
f32, bf16 = jnp.float32, jnp.bfloat16
SMALL = pl.BlockSpec(memory_space=pltpu.SMEM)
WHOLE = pl.BlockSpec(memory_space=pltpu.VMEM)
LIMIT = pltpu.CompilerParams(vmem_limit_bytes=16 << 20)


def swap(block, axis):
    return lax.ppermute(block, axis, [(0, 1), (1, 0)])


def exchange(block, axis):
    return lax.all_to_all(block, axis, 0, 0, tiled=True)


def spread(block, axis):
    copies = jnp.broadcast_to(block[None], (lax.axis_size(axis),) + block.shape)
    return exchange(copies, axis)


def pick(blocks, place):
    return lax.dynamic_index_in_dim(blocks, place, 0, keepdims=False)


def slot_orders():
    for c in range(C):
        for y in range(Y):
            for zh in range(ZH):
                yield (c * Y + y) * ZH + zh, (zh * Y + y) * C + c


def to_slots_kernel(tokens, rows_ref, out_ref):
    rows = rows_ref[...].astype(f32)
    for slot, place in slot_orders():
        block = rows[place * tokens : (place + 1) * tokens]
        block = jnp.concatenate([block, block[2 * tokens - SLOT :]], axis=0)
        out_ref[slot * SLOT : (slot + 1) * SLOT] = block.astype(bf16)


def from_slots_kernel(tokens, mask_ref, slots_ref, out_ref):
    blocks = [None] * (ZH * Y * C)
    for slot, place in slot_orders():
        rows = slots_ref[slot * SLOT : (slot + 1) * SLOT].astype(f32)
        blocks[place] = rows[:tokens]
    rows = jnp.concatenate(blocks, axis=0)
    out_ref[...] = jnp.where(mask_ref[0] != 0, rows, 0.0).astype(bf16)


def packed_width(count, width):
    return 3 * count * width + (width if count == 2 else 3 * LANES)


def pack(product, place, count, tally, out_ref):
    slots, width = HALF // SLOT, product.shape[1]
    groups = product.reshape(slots, 4, GROUP, width)
    for g in range(3):
        start = (g * count + place) * width
        out_ref[:, :, start : start + width] = groups[:, g]
    rest = groups[:, 3]
    base = 3 * count * width
    if count == 2:
        lower = slice(4 * place, 4 * place + 4)
        out_ref[:, lower, base : base + width] = rest[:, lower]
    else:
        cut = 3 * LANES
        out_ref[:, 0:4, base : base + cut] = rest[:, 0:4, :cut]
        out_ref[:, 4:8, base : base + width - cut] = rest[:, 4:8, cut:]
        spare = base + width - cut
        out_ref[:, 4:8, spare:] = jnp.full((slots, 4, base + cut - spare), tally, f32)


def unpack(block, place, count, width):
    rows = [
        block[:, (g * count + place) * width : (g * count + place + 1) * width] for g in range(3)
    ]
    base = 3 * count * width
    rest = block[:, base:]
    turned = pltpu.roll(rest, 4, 0)
    if count == 2:
        rows.append(turned if place else rest)
    else:
        cut = 3 * LANES
        rows.append(jnp.concatenate([rest, turned[:, : width - cut]], axis=1))
    return jnp.concatenate(rows, axis=0)


def logits_kernel(places, half_ref, tally_ref, tiles_ref, heads_ref, out_ref):
    parts = HALF // PART
    for j, place in enumerate(places):
        rows = tiles_ref[pl.ds(half_ref[0] * parts, parts), j].reshape(HALF, -1)
        product = jnp.dot(rows, heads_ref[place], preferred_element_type=f32)
        pack(product, j, len(places), tally_ref[0], out_ref)


def half_logits(tiles, heads, places, half, tally):
    count, (_, depth, width) = len(places), heads.shape
    shape = (HALF // SLOT, GROUP, packed_width(count, width))
    return pl.pallas_call(
        functools.partial(logits_kernel, places),
        in_specs=[SMALL, SMALL, WHOLE, WHOLE],
        out_specs=WHOLE,
        out_shape=jax.ShapeDtypeStruct(shape, f32),
        compiler_params=LIMIT,
        cost_estimate=pl.CostEstimate(
            flops=2 * HALF * depth * width * count,
            bytes_accessed=2 * count * depth * width + 2 * tiles.size,
            transcendentals=0,
        ),
    )(half.reshape(1), tally.reshape(1), tiles, heads)


def fold_kernel(place_ref, parts_ref, keep_ref, send_ref):
    place = place_ref[0]
    for side, out_ref in ((place, keep_ref), (1 - place, send_ref)):
        total = parts_ref[0, side]
        for i in range(1, parts_ref.shape[0]):
            total = total + parts_ref[i, side]
        out_ref[...] = total


def fold(parts, place):
    shape = jax.ShapeDtypeStruct(parts.shape[2:], f32)
    return pl.pallas_call(
        fold_kernel,
        in_specs=[SMALL, WHOLE],
        out_specs=[WHOLE, WHOLE],
        out_shape=[shape, shape],
        compiler_params=LIMIT,
    )(place.reshape(1), parts)


def stats_kernel(width, flags_ref, a_keep, a_come, b_keep, b_come, logits_ref, weights_ref, out_ref):
    first = a_keep[...] + a_come[...]
    pair = b_keep[...] + b_come[...]
    heads = [unpack(first, 0, 1, width)] + [unpack(pair, j, 2, width) for j in range(2)]
    tops, sums = [], []
    for j, logits in enumerate(heads):
        logits_ref[j] = logits
        tops.append(jnp.max(logits, axis=1, keepdims=True))
        sums.append(jnp.sum(jnp.exp(logits - tops[-1]), axis=1, keepdims=True))
    blank = jnp.zeros((LANES - len(heads) * SLOT, 1), f32)
    lane = lax.broadcasted_iota(jnp.int32, (LANES, LANES), 1)
    table = jnp.where(
        lane == 0,
        jnp.concatenate(tops + [blank], axis=0),
        jnp.where(lane == 1, jnp.concatenate(sums + [blank], axis=0), 0.0),
    ).T
    line = jnp.concatenate([table[0:1], table[1:2]], axis=1)
    out_ref[...] = jnp.broadcast_to(line[None], out_ref.shape)
    count = first[GROUP - 1 :, first.shape[1] - 1 :]
    weights_ref[...] = jnp.broadcast_to(loss_scale * flags_ref[...] / count, (SLOT, LANES))


def delta_kernel(stats_ref, logits_ref, weights_ref, out_ref):
    lines = stats_ref[...].reshape(stats_ref.shape[0], 2 * LANES)
    tops, sums = lines[:, :LANES], lines[:, LANES:]
    top = jnp.max(tops, axis=0, keepdims=True)
    total = jnp.sum(sums * jnp.exp(tops - top), axis=0, keepdims=True)
    row = lax.broadcasted_iota(jnp.int32, (LANES, LANES), 0)
    table = jnp.where(row == 0, top, jnp.where(row == 1, total, 0.0)).T
    probs = []
    for j in range(logits_ref.shape[0]):
        rows = table[j * SLOT : (j + 1) * SLOT]
        probs.append(jnp.exp(logits_ref[j] - rows[:, 0:1]) / rows[:, 1:2])
    width = logits_ref.shape[2]
    for k in range(2):
        delta = weights_ref[:, :1] * (probs[k] - probs[2])
        out_ref[:, k * width : (k + 1) * width] = delta.astype(bf16)


def hidden_grads_kernel(half_ref, heads_ref, near_ref, far_ref, out_ref):
    exits, width = out_ref.shape[1], heads_ref.shape[2]
    parts = HALF // PART
    for place, delta_ref in ((half_ref[0], near_ref), (1 - half_ref[0], far_ref)):
        for k in range(exits):
            grad = lax.dot_general(
                delta_ref[:, k * width : (k + 1) * width],
                heads_ref[k],
                (((1,), (1,)), ((), ())),
                preferred_element_type=f32,
            )
            out_ref[pl.ds(place * parts, parts), k] = grad.reshape(parts, PART, -1).astype(bf16)


def head_grads_kernel(half_ref, first_ref, pair_ref, near_ref, far_ref, out_ref):
    exits, _, width = out_ref.shape
    parts = HALF // PART
    for k, tiles_ref in enumerate((first_ref, pair_ref)):
        total = None
        for place, delta_ref in ((half_ref[0], near_ref), (1 - half_ref[0], far_ref)):
            rows = tiles_ref[pl.ds(place * parts, parts), 0].reshape(HALF, -1)
            term = lax.dot_general(
                rows,
                delta_ref[:, k * width : (k + 1) * width],
                (((0,), (0,)), ((), ())),
                preferred_element_type=f32,
            )
            total = term if total is None else total + term
        out_ref[k] = total.astype(bf16)


def copies_kernel(place_ref, own_ref, across_ref, out_ref):
    place = place_ref[0]
    for i in range(out_ref.shape[0]):
        out_ref[i, place] = own_ref[...]
        out_ref[i, 1 - place] = across_ref[...]


def outgoing_kernel(place_ref, tree_ref, come_ref, first_ref, out_ref):
    total = tree_ref[...] + come_ref[...].astype(f32)
    first = first_ref[...].astype(f32)
    for i in range(out_ref.shape[0]):
        out_ref[i] = jnp.where(place_ref[0] == i, total, first).astype(bf16)


def local(hidden, heads, valid, exit_section):
    total, depth, width = heads.shape
    exits = total - 1
    tokens = valid.shape[0]
    zl, x, c = lax.axis_index("zl"), lax.axis_index("x"), lax.axis_index("c")
    zh = lax.axis_index("zh")
    last = ZL * X - 1
    dynamic = exit_section[0]

    own = pl.pallas_call(
        functools.partial(to_slots_kernel, tokens),
        in_specs=[WHOLE],
        out_specs=WHOLE,
        out_shape=jax.ShapeDtypeStruct((ROWS, depth), bf16),
        compiler_params=LIMIT,
    )(hidden[0])
    row_parts = exchange(own, "x").reshape(X, PART, depth)

    def down(step):
        pairs = [(z, z - step) for z in range(ZL - 1, -1, -2 * step)]
        return lax.ppermute(tree, "zl", pairs)

    def across_zl(step):
        return lax.ppermute(first, "zl", [(z, z ^ step) for z in range(ZL)])

    def grown(come, step):
        return jnp.where((zl % (2 * step)) == step - 1, come, tree)

    def taken(come, step):
        return jnp.where((zl ^ (dynamic // X)) & step != 0, come, first)

    tree = jnp.stack([pick(row_parts, exit_section[1] % X), row_parts[last % X]])
    first = pick(row_parts, dynamic % X)
    for step in (4, 2):
        tree_come, first_come = lax.optimization_barrier((down(step), across_zl(4 // step)))
        tree, first = grown(tree_come, step), taken(first_come, 4 // step)
    tree = grown(down(1), 1)
    pair_tiles, first_come = lax.optimization_barrier((spread(tree, "x"), across_zl(4)))
    first = taken(first_come, 4)
    first_tiles = spread(first[None], "x").reshape(X, 1, PART, depth)

    tally = jnp.sum(valid.astype(f32))
    def halved(tiles, places):
        send = half_logits(tiles, heads, places, 1 - c, tally)
        return half_logits(tiles, heads, places, c, tally) + swap(send, "c")

    def over_y(both):
        return exchange(both, "y").reshape(Y, ZH, GROUP, both.shape[-1])

    pair, first_tiles = lax.optimization_barrier((halved(pair_tiles, (1, 2)), first_tiles))
    pair, first = lax.optimization_barrier((over_y(pair), halved(first_tiles, (0,))))
    pieces = []
    for parts in (over_y(first), pair):
        keep, send = fold(parts, zh)
        pieces += [keep, swap(send, "zh")]

    flags = jnp.pad(valid.astype(f32), (0, SLOT - tokens))[:, None]
    logits, weights, stats = pl.pallas_call(
        functools.partial(stats_kernel, width),
        in_specs=[WHOLE] * 5,
        out_specs=[WHOLE] * 3,
        out_shape=[
            jax.ShapeDtypeStruct((total, SLOT, width), f32),
            jax.ShapeDtypeStruct((SLOT, LANES), f32),
            jax.ShapeDtypeStruct((ZL * X, 1, 2 * LANES), f32),
        ],
        compiler_params=LIMIT,
    )(flags, *pieces)
    delta = pl.pallas_call(
        delta_kernel,
        in_specs=[WHOLE] * 3,
        out_specs=WHOLE,
        out_shape=jax.ShapeDtypeStruct((SLOT, exits * width), bf16),
        compiler_params=LIMIT,
    )(exchange(stats, PIPE), logits, weights)

    across = swap(delta, "zh")
    copies = pl.pallas_call(
        copies_kernel,
        in_specs=[SMALL, WHOLE, WHOLE],
        out_specs=WHOLE,
        out_shape=jax.ShapeDtypeStruct((Y, ZH) + delta.shape, bf16),
        compiler_params=LIMIT,
    )(zh.reshape(1), delta, across)
    near = exchange(copies, "y").reshape(HALF, exits * width)
    far = swap(near, "c")
    half = c.reshape(1)
    partial = pl.pallas_call(
        hidden_grads_kernel,
        in_specs=[SMALL, WHOLE, WHOLE, WHOLE],
        out_specs=WHOLE,
        out_shape=jax.ShapeDtypeStruct((X, exits, PART, depth), bf16),
        compiler_params=LIMIT,
    )(half, heads, near, far)
    d_heads = pl.pallas_call(
        head_grads_kernel,
        in_specs=[SMALL, WHOLE, WHOLE, WHOLE, WHOLE],
        out_specs=WHOLE,
        out_shape=jax.ShapeDtypeStruct((exits, depth, width), bf16),
        compiler_params=LIMIT,
    )(half, first_tiles, pair_tiles, near, far)

    def up(block, step):
        pairs = [(z, z + step) for z in range(step - 1, ZL, 2 * step)]
        return lax.ppermute(block.astype(bf16), "zl", pairs)

    summed = jnp.sum(exchange(partial, "x").astype(f32), axis=0)
    tree = summed[1]
    tree = tree + up(tree, 1).astype(f32)
    come, bits = lax.optimization_barrier(
        (up(tree, 2), exchange(summed[0].astype(bf16).reshape(ZL, BIT, depth), "zl"))
    )
    tree = tree + come.astype(f32)
    bit = jnp.sum(bits.astype(f32), axis=0).astype(bf16)
    come, first = lax.optimization_barrier((up(tree, 4), spread(bit, "zl")))
    outgoing = pl.pallas_call(
        outgoing_kernel,
        in_specs=[SMALL, WHOLE, WHOLE, WHOLE],
        out_specs=WHOLE,
        out_shape=jax.ShapeDtypeStruct((X, PART, depth), bf16),
        compiler_params=LIMIT,
    )((exit_section[1] - zl * X).reshape(1), tree, come, first.reshape(PART, depth))
    mask = jnp.any(exit_section == zl * X + x).astype(jnp.int32).reshape(1)
    grad = pl.pallas_call(
        functools.partial(from_slots_kernel, tokens),
        in_specs=[SMALL, WHOLE],
        out_specs=WHOLE,
        out_shape=jax.ShapeDtypeStruct(hidden.shape[1:], bf16),
        compiler_params=LIMIT,
    )(mask, exchange(outgoing, "x").reshape(ROWS, depth))
    grad = grad[None]
    return d_heads, grad


def solution(mesh):
    fine = Mesh(mesh.devices.reshape(ZL, X, ZH, Y, C), ("zl", "x", "zh", "y", "c"))
    placed = (P(PIPE, None, TENSOR), P(None, TENSOR, PIPE), P(TENSOR), P())
    return jax.shard_map(
        local,
        mesh=fine,
        in_specs=placed,
        out_specs=(P(None, TENSOR, PIPE), P(PIPE, None, TENSOR)),
        check_vma=False,
    )
```

```python
import functools

import jax
import jax.numpy as jnp
from jax import lax
from jax.experimental import pallas as pl
from jax.experimental.pallas import tpu as pltpu
from jax.sharding import Mesh, PartitionSpec as P

loss_scale = 16384.0
ZL, X, ZH, Y, C = 8, 4, 2, 4, 2
PIPE = ("zl", "x")
TENSOR = ("zh", "y", "c")
SLOT = 32
ROWS = ZH * Y * C * SLOT
HALF = ROWS // 2
PART = ROWS // X
BIT = PART // ZL
LANES = 128
GROUP = 8
f32, bf16 = jnp.float32, jnp.bfloat16
SMALL = pl.BlockSpec(memory_space=pltpu.SMEM)
WHOLE = pl.BlockSpec(memory_space=pltpu.VMEM)
LIMIT = pltpu.CompilerParams(vmem_limit_bytes=16 << 20)


def swap(block, axis):
    return lax.ppermute(block, axis, [(0, 1), (1, 0)])


def exchange(block, axis):
    return lax.all_to_all(block, axis, 0, 0, tiled=True)


def spread(block, axis):
    copies = jnp.broadcast_to(block[None], (lax.axis_size(axis),) + block.shape)
    return exchange(copies, axis)


def pick(blocks, place):
    return lax.dynamic_index_in_dim(blocks, place, 0, keepdims=False)


def slot_orders():
    for c in range(C):
        for y in range(Y):
            for zh in range(ZH):
                yield (c * Y + y) * ZH + zh, (zh * Y + y) * C + c


def to_slots_kernel(tokens, rows_ref, out_ref):
    rows = rows_ref[...].astype(f32)
    for slot, place in slot_orders():
        block = rows[place * tokens : (place + 1) * tokens]
        block = jnp.concatenate([block, block[2 * tokens - SLOT :]], axis=0)
        out_ref[slot * SLOT : (slot + 1) * SLOT] = block.astype(bf16)


def from_slots_kernel(tokens, mask_ref, slots_ref, out_ref):
    blocks = [None] * (ZH * Y * C)
    for slot, place in slot_orders():
        rows = slots_ref[slot * SLOT : (slot + 1) * SLOT].astype(f32)
        blocks[place] = rows[:tokens]
    rows = jnp.concatenate(blocks, axis=0)
    out_ref[...] = jnp.where(mask_ref[0] != 0, rows, 0.0).astype(bf16)


def packed_width(count, width):
    return 3 * count * width + (width if count == 2 else 3 * LANES)


def pack(product, place, count, tally, out_ref):
    slots, width = HALF // SLOT, product.shape[1]
    groups = product.reshape(slots, 4, GROUP, width)
    for g in range(3):
        start = (g * count + place) * width
        out_ref[:, :, start : start + width] = groups[:, g]
    rest = groups[:, 3]
    base = 3 * count * width
    if count == 2:
        lower = slice(4 * place, 4 * place + 4)
        out_ref[:, lower, base : base + width] = rest[:, lower]
    else:
        cut = 3 * LANES
        out_ref[:, 0:4, base : base + cut] = rest[:, 0:4, :cut]
        out_ref[:, 4:8, base : base + width - cut] = rest[:, 4:8, cut:]
        spare = base + width - cut
        out_ref[:, 4:8, spare:] = jnp.full((slots, 4, base + cut - spare), tally, f32)


def unpack(block, place, count, width):
    rows = [
        block[:, (g * count + place) * width : (g * count + place + 1) * width] for g in range(3)
    ]
    base = 3 * count * width
    rest = block[:, base:]
    turned = pltpu.roll(rest, 4, 0)
    if count == 2:
        rows.append(turned if place else rest)
    else:
        cut = 3 * LANES
        rows.append(jnp.concatenate([rest, turned[:, : width - cut]], axis=1))
    return jnp.concatenate(rows, axis=0)


def logits_kernel(places, half_ref, tally_ref, tiles_ref, heads_ref, out_ref):
    parts = HALF // PART
    for j, place in enumerate(places):
        rows = tiles_ref[pl.ds(half_ref[0] * parts, parts), j].reshape(HALF, -1)
        product = jnp.dot(rows, heads_ref[place], preferred_element_type=f32)
        pack(product, j, len(places), tally_ref[0], out_ref)


def half_logits(tiles, heads, places, half, tally):
    count, (_, depth, width) = len(places), heads.shape
    shape = (HALF // SLOT, GROUP, packed_width(count, width))
    return pl.pallas_call(
        functools.partial(logits_kernel, places),
        in_specs=[SMALL, SMALL, WHOLE, WHOLE],
        out_specs=WHOLE,
        out_shape=jax.ShapeDtypeStruct(shape, f32),
        compiler_params=LIMIT,
        cost_estimate=pl.CostEstimate(
            flops=2 * HALF * depth * width * count,
            bytes_accessed=2 * count * depth * width + 2 * tiles.size,
            transcendentals=0,
        ),
    )(half.reshape(1), tally.reshape(1), tiles, heads)


def fold_kernel(place_ref, parts_ref, keep_ref, send_ref):
    place = place_ref[0]
    for side, out_ref in ((place, keep_ref), (1 - place, send_ref)):
        total = parts_ref[0, side]
        for i in range(1, parts_ref.shape[0]):
            total = total + parts_ref[i, side]
        out_ref[...] = total


def fold(parts, place):
    shape = jax.ShapeDtypeStruct(parts.shape[2:], f32)
    return pl.pallas_call(
        fold_kernel,
        in_specs=[SMALL, WHOLE],
        out_specs=[WHOLE, WHOLE],
        out_shape=[shape, shape],
        compiler_params=LIMIT,
    )(place.reshape(1), parts)


def stats_kernel(width, flags_ref, a_keep, a_come, b_keep, b_come, logits_ref, weights_ref, out_ref):
    first = a_keep[...] + a_come[...]
    pair = b_keep[...] + b_come[...]
    heads = [unpack(first, 0, 1, width)] + [unpack(pair, j, 2, width) for j in range(2)]
    tops, sums = [], []
    for j, logits in enumerate(heads):
        logits_ref[j] = logits
        tops.append(jnp.max(logits, axis=1, keepdims=True))
        sums.append(jnp.sum(jnp.exp(logits - tops[-1]), axis=1, keepdims=True))
    blank = jnp.zeros((LANES - len(heads) * SLOT, 1), f32)
    lane = lax.broadcasted_iota(jnp.int32, (LANES, LANES), 1)
    table = jnp.where(
        lane == 0,
        jnp.concatenate(tops + [blank], axis=0),
        jnp.where(lane == 1, jnp.concatenate(sums + [blank], axis=0), 0.0),
    ).T
    line = jnp.concatenate([table[0:1], table[1:2]], axis=1)
    out_ref[...] = jnp.broadcast_to(line[None], out_ref.shape)
    count = first[GROUP - 1 :, first.shape[1] - 1 :]
    weights_ref[...] = jnp.broadcast_to(loss_scale * flags_ref[...] / count, (SLOT, LANES))


def delta_kernel(stats_ref, logits_ref, weights_ref, out_ref):
    lines = stats_ref[...].reshape(stats_ref.shape[0], 2 * LANES)
    tops, sums = lines[:, :LANES], lines[:, LANES:]
    top = jnp.max(tops, axis=0, keepdims=True)
    total = jnp.sum(sums * jnp.exp(tops - top), axis=0, keepdims=True)
    row = lax.broadcasted_iota(jnp.int32, (LANES, LANES), 0)
    table = jnp.where(row == 0, top, jnp.where(row == 1, total, 0.0)).T
    probs = []
    for j in range(logits_ref.shape[0]):
        rows = table[j * SLOT : (j + 1) * SLOT]
        probs.append(jnp.exp(logits_ref[j] - rows[:, 0:1]) / rows[:, 1:2])
    width = logits_ref.shape[2]
    for k in range(2):
        delta = weights_ref[:, :1] * (probs[k] - probs[2])
        out_ref[:, k * width : (k + 1) * width] = delta.astype(bf16)


def hidden_grads_kernel(half_ref, heads_ref, near_ref, far_ref, out_ref):
    exits, width = out_ref.shape[1], heads_ref.shape[2]
    parts = HALF // PART
    for place, delta_ref in ((half_ref[0], near_ref), (1 - half_ref[0], far_ref)):
        for k in range(exits):
            grad = lax.dot_general(
                delta_ref[:, k * width : (k + 1) * width],
                heads_ref[k],
                (((1,), (1,)), ((), ())),
                preferred_element_type=f32,
            )
            out_ref[pl.ds(place * parts, parts), k] = grad.reshape(parts, PART, -1).astype(bf16)


def head_grads_kernel(half_ref, first_ref, pair_ref, near_ref, far_ref, out_ref):
    exits, _, width = out_ref.shape
    parts = HALF // PART
    for k, tiles_ref in enumerate((first_ref, pair_ref)):
        total = None
        for place, delta_ref in ((half_ref[0], near_ref), (1 - half_ref[0], far_ref)):
            rows = tiles_ref[pl.ds(place * parts, parts), 0].reshape(HALF, -1)
            term = lax.dot_general(
                rows,
                delta_ref[:, k * width : (k + 1) * width],
                (((0,), (0,)), ((), ())),
                preferred_element_type=f32,
            )
            total = term if total is None else total + term
        out_ref[k] = total.astype(bf16)


def copies_kernel(place_ref, own_ref, across_ref, out_ref):
    place = place_ref[0]
    for i in range(out_ref.shape[0]):
        out_ref[i, place] = own_ref[...]
        out_ref[i, 1 - place] = across_ref[...]


def outgoing_kernel(place_ref, tree_ref, come_ref, first_ref, out_ref):
    total = tree_ref[...] + come_ref[...].astype(f32)
    first = first_ref[...].astype(f32)
    for i in range(out_ref.shape[0]):
        out_ref[i] = jnp.where(place_ref[0] == i, total, first).astype(bf16)


def local(hidden, heads, valid, exit_section):
    total, depth, width = heads.shape
    exits = total - 1
    tokens = valid.shape[0]
    zl, x, c = lax.axis_index("zl"), lax.axis_index("x"), lax.axis_index("c")
    zh = lax.axis_index("zh")
    last = ZL * X - 1
    dynamic = exit_section[0]

    own = pl.pallas_call(
        functools.partial(to_slots_kernel, tokens),
        in_specs=[WHOLE],
        out_specs=WHOLE,
        out_shape=jax.ShapeDtypeStruct((ROWS, depth), bf16),
        compiler_params=LIMIT,
    )(hidden[0])
    row_parts = exchange(own, "x").reshape(X, PART, depth)

    def down(step):
        pairs = [(z, z - step) for z in range(ZL - 1, -1, -2 * step)]
        return lax.ppermute(tree, "zl", pairs)

    def across_zl(step):
        return lax.ppermute(first, "zl", [(z, z ^ step) for z in range(ZL)])

    def grown(come, step):
        return jnp.where((zl % (2 * step)) == step - 1, come, tree)

    def taken(come, step):
        return jnp.where((zl ^ (dynamic // X)) & step != 0, come, first)

    tree = jnp.stack([pick(row_parts, exit_section[1] % X), row_parts[last % X]])
    first = pick(row_parts, dynamic % X)
    for step in (4, 2):
        tree_come, first_come = lax.optimization_barrier((down(step), across_zl(4 // step)))
        tree, first = grown(tree_come, step), taken(first_come, 4 // step)
    tree = grown(down(1), 1)
    pair_tiles, first_come = lax.optimization_barrier((spread(tree, "x"), across_zl(4)))
    first = taken(first_come, 4)
    first_tiles = spread(first[None], "x").reshape(X, 1, PART, depth)

    tally = jnp.sum(valid.astype(f32))
    def halved(tiles, places):
        send = half_logits(tiles, heads, places, 1 - c, tally)
        return half_logits(tiles, heads, places, c, tally), swap(send, "c")

    def over_y(both):
        return exchange(both, "y").reshape(Y, ZH, GROUP, both.shape[-1])

    keep, come = halved(pair_tiles, (1, 2))
    come, first_tiles = lax.optimization_barrier((come, first_tiles))
    pair, first = over_y(keep + come), sum(halved(first_tiles, (0,)))
    pair, first = lax.optimization_barrier((pair, first))
    pieces = []
    for parts in (over_y(first), pair):
        keep, send = fold(parts, zh)
        pieces += [keep, swap(send, "zh")]

    flags = jnp.pad(valid.astype(f32), (0, SLOT - tokens))[:, None]
    logits, weights, stats = pl.pallas_call(
        functools.partial(stats_kernel, width),
        in_specs=[WHOLE] * 5,
        out_specs=[WHOLE] * 3,
        out_shape=[
            jax.ShapeDtypeStruct((total, SLOT, width), f32),
            jax.ShapeDtypeStruct((SLOT, LANES), f32),
            jax.ShapeDtypeStruct((ZL * X, 1, 2 * LANES), f32),
        ],
        compiler_params=LIMIT,
    )(flags, *pieces)
    delta = pl.pallas_call(
        delta_kernel,
        in_specs=[WHOLE] * 3,
        out_specs=WHOLE,
        out_shape=jax.ShapeDtypeStruct((SLOT, exits * width), bf16),
        compiler_params=LIMIT,
    )(exchange(stats, PIPE), logits, weights)

    across = swap(delta, "zh")
    copies = pl.pallas_call(
        copies_kernel,
        in_specs=[SMALL, WHOLE, WHOLE],
        out_specs=WHOLE,
        out_shape=jax.ShapeDtypeStruct((Y, ZH) + delta.shape, bf16),
        compiler_params=LIMIT,
    )(zh.reshape(1), delta, across)
    near = exchange(copies, "y").reshape(HALF, exits * width)
    far = swap(near, "c")
    half = c.reshape(1)
    partial = pl.pallas_call(
        hidden_grads_kernel,
        in_specs=[SMALL, WHOLE, WHOLE, WHOLE],
        out_specs=WHOLE,
        out_shape=jax.ShapeDtypeStruct((X, exits, PART, depth), bf16),
        compiler_params=LIMIT,
    )(half, heads, near, far)
    d_heads = pl.pallas_call(
        head_grads_kernel,
        in_specs=[SMALL, WHOLE, WHOLE, WHOLE, WHOLE],
        out_specs=WHOLE,
        out_shape=jax.ShapeDtypeStruct((exits, depth, width), bf16),
        compiler_params=LIMIT,
    )(half, first_tiles, pair_tiles, near, far)

    def up(block, step):
        pairs = [(z, z + step) for z in range(step - 1, ZL, 2 * step)]
        return lax.ppermute(block.astype(bf16), "zl", pairs)

    summed = jnp.sum(exchange(partial, "x").astype(f32), axis=0)
    tree = summed[1]
    tree = tree + up(tree, 1).astype(f32)
    come, bits = lax.optimization_barrier(
        (up(tree, 2), exchange(summed[0].astype(bf16).reshape(ZL, BIT, depth), "zl"))
    )
    tree = tree + come.astype(f32)
    bit = jnp.sum(bits.astype(f32), axis=0).astype(bf16)
    come, first = lax.optimization_barrier((up(tree, 4), spread(bit, "zl")))
    outgoing = pl.pallas_call(
        outgoing_kernel,
        in_specs=[SMALL, WHOLE, WHOLE, WHOLE],
        out_specs=WHOLE,
        out_shape=jax.ShapeDtypeStruct((X, PART, depth), bf16),
        compiler_params=LIMIT,
    )((exit_section[1] - zl * X).reshape(1), tree, come, first.reshape(PART, depth))
    mask = jnp.any(exit_section == zl * X + x).astype(jnp.int32).reshape(1)
    grad = pl.pallas_call(
        functools.partial(from_slots_kernel, tokens),
        in_specs=[SMALL, WHOLE],
        out_specs=WHOLE,
        out_shape=jax.ShapeDtypeStruct(hidden.shape[1:], bf16),
        compiler_params=LIMIT,
    )(mask, exchange(outgoing, "x").reshape(ROWS, depth))
    grad = grad[None]
    return d_heads, grad


def solution(mesh):
    fine = Mesh(mesh.devices.reshape(ZL, X, ZH, Y, C), ("zl", "x", "zh", "y", "c"))
    placed = (P(PIPE, None, TENSOR), P(None, TENSOR, PIPE), P(TENSOR), P())
    return jax.shard_map(
        local,
        mesh=fine,
        in_specs=placed,
        out_specs=(P(None, TENSOR, PIPE), P(PIPE, None, TENSOR)),
        check_vma=False,
    )
```

```python
import functools

import jax
import jax.numpy as jnp
from jax import lax
from jax.experimental import pallas as pl
from jax.experimental.pallas import tpu as pltpu
from jax.sharding import Mesh, PartitionSpec as P

loss_scale = 16384.0
ZL, X, ZH, Y, C = 8, 4, 2, 4, 2
PIPE = ("zl", "x")
TENSOR = ("zh", "y", "c")
SLOT = 32
ROWS = ZH * Y * C * SLOT
HALF = ROWS // 2
PART = ROWS // X
BIT = PART // ZL
LANES = 128
GROUP = 8
f32, bf16 = jnp.float32, jnp.bfloat16
SMALL = pl.BlockSpec(memory_space=pltpu.SMEM)
WHOLE = pl.BlockSpec(memory_space=pltpu.VMEM)
LIMIT = pltpu.CompilerParams(vmem_limit_bytes=16 << 20)


def swap(block, axis):
    return lax.ppermute(block, axis, [(0, 1), (1, 0)])


def exchange(block, axis):
    return lax.all_to_all(block, axis, 0, 0, tiled=True)


def spread(block, axis):
    copies = jnp.broadcast_to(block[None], (lax.axis_size(axis),) + block.shape)
    return exchange(copies, axis)


def pick(blocks, place):
    return lax.dynamic_index_in_dim(blocks, place, 0, keepdims=False)


def slot_orders():
    for c in range(C):
        for y in range(Y):
            for zh in range(ZH):
                yield (c * Y + y) * ZH + zh, (zh * Y + y) * C + c


def to_slots_kernel(tokens, rows_ref, out_ref):
    rows = rows_ref[...].astype(f32)
    for slot, place in slot_orders():
        block = rows[place * tokens : (place + 1) * tokens]
        block = jnp.concatenate([block, block[2 * tokens - SLOT :]], axis=0)
        out_ref[slot * SLOT : (slot + 1) * SLOT] = block.astype(bf16)


def from_slots_kernel(tokens, mask_ref, slots_ref, out_ref):
    blocks = [None] * (ZH * Y * C)
    for slot, place in slot_orders():
        rows = slots_ref[slot * SLOT : (slot + 1) * SLOT].astype(f32)
        blocks[place] = rows[:tokens]
    rows = jnp.concatenate(blocks, axis=0)
    out_ref[...] = jnp.where(mask_ref[0] != 0, rows, 0.0).astype(bf16)


def packed_width(count, width):
    return 3 * count * width + (width if count == 2 else 3 * LANES)


def pack(product, place, count, tally, out_ref):
    slots, width = HALF // SLOT, product.shape[1]
    groups = product.reshape(slots, 4, GROUP, width)
    for g in range(3):
        start = (g * count + place) * width
        out_ref[:, :, start : start + width] = groups[:, g]
    rest = groups[:, 3]
    base = 3 * count * width
    if count == 2:
        lower = slice(4 * place, 4 * place + 4)
        out_ref[:, lower, base : base + width] = rest[:, lower]
    else:
        cut = 3 * LANES
        out_ref[:, 0:4, base : base + cut] = rest[:, 0:4, :cut]
        out_ref[:, 4:8, base : base + width - cut] = rest[:, 4:8, cut:]
        spare = base + width - cut
        out_ref[:, 4:8, spare:] = jnp.full((slots, 4, base + cut - spare), tally, f32)


def unpack(block, place, count, width):
    rows = [
        block[:, (g * count + place) * width : (g * count + place + 1) * width] for g in range(3)
    ]
    base = 3 * count * width
    rest = block[:, base:]
    turned = pltpu.roll(rest, 4, 0)
    if count == 2:
        rows.append(turned if place else rest)
    else:
        cut = 3 * LANES
        rows.append(jnp.concatenate([rest, turned[:, : width - cut]], axis=1))
    return jnp.concatenate(rows, axis=0)


def logits_kernel(places, half_ref, tally_ref, tiles_ref, heads_ref, out_ref):
    parts = HALF // PART
    for j, place in enumerate(places):
        rows = tiles_ref[pl.ds(half_ref[0] * parts, parts), j].reshape(HALF, -1)
        product = jnp.dot(rows, heads_ref[place], preferred_element_type=f32)
        pack(product, j, len(places), tally_ref[0], out_ref)


def half_logits(tiles, heads, places, half, tally):
    count, (_, depth, width) = len(places), heads.shape
    shape = (HALF // SLOT, GROUP, packed_width(count, width))
    return pl.pallas_call(
        functools.partial(logits_kernel, places),
        in_specs=[SMALL, SMALL, WHOLE, WHOLE],
        out_specs=WHOLE,
        out_shape=jax.ShapeDtypeStruct(shape, f32),
        compiler_params=LIMIT,
        cost_estimate=pl.CostEstimate(
            flops=2 * HALF * depth * width * count,
            bytes_accessed=2 * count * depth * width + 2 * tiles.size,
            transcendentals=0,
        ),
    )(half.reshape(1), tally.reshape(1), tiles, heads)


def fold_kernel(place_ref, first_ref, pair_ref, keep_ref, send_ref):
    place, cut = place_ref[0], first_ref.shape[-1]
    for side, out_ref in ((place, keep_ref), (1 - place, send_ref)):
        for parts_ref, cols in ((first_ref, slice(0, cut)), (pair_ref, slice(cut, None))):
            total = parts_ref[0, side]
            for i in range(1, parts_ref.shape[0]):
                total = total + parts_ref[i, side]
            out_ref[:, cols] = total


def fold(first, pair, place):
    shape = jax.ShapeDtypeStruct((GROUP, first.shape[-1] + pair.shape[-1]), f32)
    return pl.pallas_call(
        fold_kernel,
        in_specs=[SMALL, WHOLE, WHOLE],
        out_specs=[WHOLE, WHOLE],
        out_shape=[shape, shape],
        compiler_params=LIMIT,
    )(place.reshape(1), first, pair)


def stats_kernel(width, flags_ref, keep_ref, come_ref, logits_ref, weights_ref, out_ref):
    both = keep_ref[...] + come_ref[...]
    cut = packed_width(1, width)
    first, pair = both[:, :cut], both[:, cut:]
    heads = [unpack(first, 0, 1, width)] + [unpack(pair, j, 2, width) for j in range(2)]
    tops, sums = [], []
    for j, logits in enumerate(heads):
        logits_ref[j] = logits
        tops.append(jnp.max(logits, axis=1, keepdims=True))
        sums.append(jnp.sum(jnp.exp(logits - tops[-1]), axis=1, keepdims=True))
    blank = jnp.zeros((LANES - len(heads) * SLOT, 1), f32)
    lane = lax.broadcasted_iota(jnp.int32, (LANES, LANES), 1)
    table = jnp.where(
        lane == 0,
        jnp.concatenate(tops + [blank], axis=0),
        jnp.where(lane == 1, jnp.concatenate(sums + [blank], axis=0), 0.0),
    ).T
    line = jnp.concatenate([table[0:1], table[1:2]], axis=1)
    out_ref[...] = jnp.broadcast_to(line[None], out_ref.shape)
    count = first[GROUP - 1 :, first.shape[1] - 1 :]
    weights_ref[...] = jnp.broadcast_to(loss_scale * flags_ref[...] / count, (SLOT, LANES))


def delta_kernel(stats_ref, logits_ref, weights_ref, out_ref):
    lines = stats_ref[...].reshape(stats_ref.shape[0], 2 * LANES)
    tops, sums = lines[:, :LANES], lines[:, LANES:]
    top = jnp.max(tops, axis=0, keepdims=True)
    total = jnp.sum(sums * jnp.exp(tops - top), axis=0, keepdims=True)
    row = lax.broadcasted_iota(jnp.int32, (LANES, LANES), 0)
    table = jnp.where(row == 0, top, jnp.where(row == 1, total, 0.0)).T
    probs = []
    for j in range(logits_ref.shape[0]):
        rows = table[j * SLOT : (j + 1) * SLOT]
        probs.append(jnp.exp(logits_ref[j] - rows[:, 0:1]) / rows[:, 1:2])
    width = logits_ref.shape[2]
    for k in range(2):
        delta = weights_ref[:, :1] * (probs[k] - probs[2])
        out_ref[:, k * width : (k + 1) * width] = delta.astype(bf16)


def hidden_grads_kernel(half_ref, heads_ref, near_ref, far_ref, out_ref):
    exits, width = out_ref.shape[1], heads_ref.shape[2]
    parts = HALF // PART
    for place, delta_ref in ((half_ref[0], near_ref), (1 - half_ref[0], far_ref)):
        for k in range(exits):
            grad = lax.dot_general(
                delta_ref[:, k * width : (k + 1) * width],
                heads_ref[k],
                (((1,), (1,)), ((), ())),
                preferred_element_type=f32,
            )
            out_ref[pl.ds(place * parts, parts), k] = grad.reshape(parts, PART, -1).astype(bf16)


def head_grads_kernel(half_ref, first_ref, pair_ref, near_ref, far_ref, out_ref):
    exits, _, width = out_ref.shape
    parts = HALF // PART
    for k, tiles_ref in enumerate((first_ref, pair_ref)):
        total = None
        for place, delta_ref in ((half_ref[0], near_ref), (1 - half_ref[0], far_ref)):
            rows = tiles_ref[pl.ds(place * parts, parts), 0].reshape(HALF, -1)
            term = lax.dot_general(
                rows,
                delta_ref[:, k * width : (k + 1) * width],
                (((0,), (0,)), ((), ())),
                preferred_element_type=f32,
            )
            total = term if total is None else total + term
        out_ref[k] = total.astype(bf16)


def copies_kernel(place_ref, own_ref, across_ref, out_ref):
    place = place_ref[0]
    for i in range(out_ref.shape[0]):
        out_ref[i, place] = own_ref[...]
        out_ref[i, 1 - place] = across_ref[...]


def outgoing_kernel(place_ref, tree_ref, come_ref, first_ref, out_ref):
    total = tree_ref[...] + come_ref[...].astype(f32)
    first = first_ref[...].astype(f32)
    for i in range(out_ref.shape[0]):
        out_ref[i] = jnp.where(place_ref[0] == i, total, first).astype(bf16)


def local(hidden, heads, valid, exit_section):
    total, depth, width = heads.shape
    exits = total - 1
    tokens = valid.shape[0]
    zl, x, c = lax.axis_index("zl"), lax.axis_index("x"), lax.axis_index("c")
    zh = lax.axis_index("zh")
    last = ZL * X - 1
    dynamic = exit_section[0]

    own = pl.pallas_call(
        functools.partial(to_slots_kernel, tokens),
        in_specs=[WHOLE],
        out_specs=WHOLE,
        out_shape=jax.ShapeDtypeStruct((ROWS, depth), bf16),
        compiler_params=LIMIT,
    )(hidden[0])
    row_parts = exchange(own, "x").reshape(X, PART, depth)

    def down(step):
        pairs = [(z, z - step) for z in range(ZL - 1, -1, -2 * step)]
        return lax.ppermute(tree, "zl", pairs)

    def across_zl(step):
        return lax.ppermute(first, "zl", [(z, z ^ step) for z in range(ZL)])

    def grown(come, step):
        return jnp.where((zl % (2 * step)) == step - 1, come, tree)

    def taken(come, step):
        return jnp.where((zl ^ (dynamic // X)) & step != 0, come, first)

    tree = jnp.stack([pick(row_parts, exit_section[1] % X), row_parts[last % X]])
    first = pick(row_parts, dynamic % X)
    for step in (4, 2):
        tree_come, first_come = lax.optimization_barrier((down(step), across_zl(4 // step)))
        tree, first = grown(tree_come, step), taken(first_come, 4 // step)
    tree = grown(down(1), 1)
    pair_tiles, first_come = lax.optimization_barrier((spread(tree, "x"), across_zl(4)))
    first = taken(first_come, 4)
    first_tiles = spread(first[None], "x").reshape(X, 1, PART, depth)

    tally = jnp.sum(valid.astype(f32))
    def halved(tiles, places):
        send = half_logits(tiles, heads, places, 1 - c, tally)
        return half_logits(tiles, heads, places, c, tally) + swap(send, "c")

    def over_y(both):
        return exchange(both, "y").reshape(Y, ZH, GROUP, both.shape[-1])

    pair, first_tiles = lax.optimization_barrier((halved(pair_tiles, (1, 2)), first_tiles))
    pair, first = lax.optimization_barrier((over_y(pair), halved(first_tiles, (0,))))
    keep, send = fold(over_y(first), pair, zh)

    flags = jnp.pad(valid.astype(f32), (0, SLOT - tokens))[:, None]
    logits, weights, stats = pl.pallas_call(
        functools.partial(stats_kernel, width),
        in_specs=[WHOLE] * 3,
        out_specs=[WHOLE] * 3,
        out_shape=[
            jax.ShapeDtypeStruct((total, SLOT, width), f32),
            jax.ShapeDtypeStruct((SLOT, LANES), f32),
            jax.ShapeDtypeStruct((ZL * X, 1, 2 * LANES), f32),
        ],
        compiler_params=LIMIT,
    )(flags, keep, swap(send, "zh"))
    delta = pl.pallas_call(
        delta_kernel,
        in_specs=[WHOLE] * 3,
        out_specs=WHOLE,
        out_shape=jax.ShapeDtypeStruct((SLOT, exits * width), bf16),
        compiler_params=LIMIT,
    )(exchange(stats, PIPE), logits, weights)

    across = swap(delta, "zh")
    copies = pl.pallas_call(
        copies_kernel,
        in_specs=[SMALL, WHOLE, WHOLE],
        out_specs=WHOLE,
        out_shape=jax.ShapeDtypeStruct((Y, ZH) + delta.shape, bf16),
        compiler_params=LIMIT,
    )(zh.reshape(1), delta, across)
    near = exchange(copies, "y").reshape(HALF, exits * width)
    far = swap(near, "c")
    half = c.reshape(1)
    partial = pl.pallas_call(
        hidden_grads_kernel,
        in_specs=[SMALL, WHOLE, WHOLE, WHOLE],
        out_specs=WHOLE,
        out_shape=jax.ShapeDtypeStruct((X, exits, PART, depth), bf16),
        compiler_params=LIMIT,
    )(half, heads, near, far)
    d_heads = pl.pallas_call(
        head_grads_kernel,
        in_specs=[SMALL, WHOLE, WHOLE, WHOLE, WHOLE],
        out_specs=WHOLE,
        out_shape=jax.ShapeDtypeStruct((exits, depth, width), bf16),
        compiler_params=LIMIT,
    )(half, first_tiles, pair_tiles, near, far)

    def up(block, step):
        pairs = [(z, z + step) for z in range(step - 1, ZL, 2 * step)]
        return lax.ppermute(block.astype(bf16), "zl", pairs)

    summed = jnp.sum(exchange(partial, "x").astype(f32), axis=0)
    tree = summed[1]
    tree = tree + up(tree, 1).astype(f32)
    come, bits = lax.optimization_barrier(
        (up(tree, 2), exchange(summed[0].astype(bf16).reshape(ZL, BIT, depth), "zl"))
    )
    tree = tree + come.astype(f32)
    bit = jnp.sum(bits.astype(f32), axis=0).astype(bf16)
    come, first = lax.optimization_barrier((up(tree, 4), spread(bit, "zl")))
    outgoing = pl.pallas_call(
        outgoing_kernel,
        in_specs=[SMALL, WHOLE, WHOLE, WHOLE],
        out_specs=WHOLE,
        out_shape=jax.ShapeDtypeStruct((X, PART, depth), bf16),
        compiler_params=LIMIT,
    )((exit_section[1] - zl * X).reshape(1), tree, come, first.reshape(PART, depth))
    mask = jnp.any(exit_section == zl * X + x).astype(jnp.int32).reshape(1)
    grad = pl.pallas_call(
        functools.partial(from_slots_kernel, tokens),
        in_specs=[SMALL, WHOLE],
        out_specs=WHOLE,
        out_shape=jax.ShapeDtypeStruct(hidden.shape[1:], bf16),
        compiler_params=LIMIT,
    )(mask, exchange(outgoing, "x").reshape(ROWS, depth))
    grad = grad[None]
    return d_heads, grad


def solution(mesh):
    fine = Mesh(mesh.devices.reshape(ZL, X, ZH, Y, C), ("zl", "x", "zh", "y", "c"))
    placed = (P(PIPE, None, TENSOR), P(None, TENSOR, PIPE), P(TENSOR), P())
    return jax.shard_map(
        local,
        mesh=fine,
        in_specs=placed,
        out_specs=(P(None, TENSOR, PIPE), P(PIPE, None, TENSOR)),
        check_vma=False,
    )
```

```python
import functools

import jax
import jax.numpy as jnp
from jax import lax
from jax.experimental import pallas as pl
from jax.experimental.pallas import tpu as pltpu
from jax.sharding import Mesh, PartitionSpec as P

loss_scale = 16384.0
ZL, X, ZH, Y, C = 8, 4, 2, 4, 2
PIPE = ("zl", "x")
TENSOR = ("zh", "y", "c")
SLOT = 32
ROWS = ZH * Y * C * SLOT
HALF = ROWS // 2
PART = ROWS // X
BIT = PART // ZL
LANES = 128
GROUP = 8
f32, bf16 = jnp.float32, jnp.bfloat16
SMALL = pl.BlockSpec(memory_space=pltpu.SMEM)
WHOLE = pl.BlockSpec(memory_space=pltpu.VMEM)
LIMIT = pltpu.CompilerParams(vmem_limit_bytes=16 << 20)


def swap(block, axis):
    return lax.ppermute(block, axis, [(0, 1), (1, 0)])


def exchange(block, axis):
    return lax.all_to_all(block, axis, 0, 0, tiled=True)


def pick(blocks, place):
    return lax.dynamic_index_in_dim(blocks, place, 0, keepdims=False)


def slot_orders():
    for c in range(C):
        for y in range(Y):
            for zh in range(ZH):
                yield (c * Y + y) * ZH + zh, (zh * Y + y) * C + c


def to_slots_kernel(tokens, rows_ref, out_ref):
    rows = rows_ref[...].astype(f32)
    for slot, place in slot_orders():
        block = rows[place * tokens : (place + 1) * tokens]
        block = jnp.concatenate([block, block[2 * tokens - SLOT :]], axis=0)
        out_ref[slot * SLOT : (slot + 1) * SLOT] = block.astype(bf16)


def from_slots_kernel(tokens, mask_ref, slots_ref, out_ref):
    blocks = [None] * (ZH * Y * C)
    for slot, place in slot_orders():
        rows = slots_ref[slot * SLOT : (slot + 1) * SLOT].astype(f32)
        blocks[place] = rows[:tokens]
    rows = jnp.concatenate(blocks, axis=0)
    out_ref[...] = jnp.where(mask_ref[0] != 0, rows, 0.0).astype(bf16)


def packed_width(count, width):
    return 3 * count * width + (width if count == 2 else 3 * LANES)


def pack(product, place, count, tally, out_ref):
    slots, width = HALF // SLOT, product.shape[1]
    groups = product.reshape(slots, 4, GROUP, width)
    for g in range(3):
        start = (g * count + place) * width
        out_ref[:, :, start : start + width] = groups[:, g]
    rest = groups[:, 3]
    base = 3 * count * width
    if count == 2:
        lower = slice(4 * place, 4 * place + 4)
        out_ref[:, lower, base : base + width] = rest[:, lower]
    else:
        cut = 3 * LANES
        out_ref[:, 0:4, base : base + cut] = rest[:, 0:4, :cut]
        out_ref[:, 4:8, base : base + width - cut] = rest[:, 4:8, cut:]
        spare = base + width - cut
        out_ref[:, 4:8, spare:] = jnp.full((slots, 4, base + cut - spare), tally, f32)


def unpack(block, place, count, width):
    rows = [
        block[:, (g * count + place) * width : (g * count + place + 1) * width] for g in range(3)
    ]
    base = 3 * count * width
    rest = block[:, base:]
    turned = pltpu.roll(rest, 4, 0)
    if count == 2:
        rows.append(turned if place else rest)
    else:
        cut = 3 * LANES
        rows.append(jnp.concatenate([rest, turned[:, : width - cut]], axis=1))
    return jnp.concatenate(rows, axis=0)


def logits_kernel(places, half_ref, tally_ref, tiles_ref, heads_ref, out_ref):
    parts = HALF // PART
    for j, place in enumerate(places):
        rows = tiles_ref[pl.ds(half_ref[0] * parts, parts), j].reshape(HALF, -1)
        product = jnp.dot(rows, heads_ref[place], preferred_element_type=f32)
        pack(product, j, len(places), tally_ref[0], out_ref)


def half_logits(tiles, heads, places, half, tally):
    count, (_, depth, width) = len(places), heads.shape
    shape = (HALF // SLOT, GROUP, packed_width(count, width))
    return pl.pallas_call(
        functools.partial(logits_kernel, places),
        in_specs=[SMALL, SMALL, WHOLE, WHOLE],
        out_specs=WHOLE,
        out_shape=jax.ShapeDtypeStruct(shape, f32),
        compiler_params=LIMIT,
        cost_estimate=pl.CostEstimate(
            flops=2 * HALF * depth * width * count,
            bytes_accessed=2 * count * depth * width + 2 * tiles.size,
            transcendentals=0,
        ),
    )(half.reshape(1), tally.reshape(1), tiles, heads)


def fold_kernel(place_ref, parts_ref, keep_ref, send_ref):
    place = place_ref[0]
    for side, out_ref in ((place, keep_ref), (1 - place, send_ref)):
        total = parts_ref[0, side]
        for i in range(1, parts_ref.shape[0]):
            total = total + parts_ref[i, side]
        out_ref[...] = total


def fold(parts, place):
    shape = jax.ShapeDtypeStruct(parts.shape[2:], f32)
    return pl.pallas_call(
        fold_kernel,
        in_specs=[SMALL, WHOLE],
        out_specs=[WHOLE, WHOLE],
        out_shape=[shape, shape],
        compiler_params=LIMIT,
    )(place.reshape(1), parts)


def stats_kernel(width, flags_ref, a_keep, a_come, b_keep, b_come, logits_ref, weights_ref, out_ref):
    first = a_keep[...] + a_come[...]
    pair = b_keep[...] + b_come[...]
    heads = [unpack(first, 0, 1, width)] + [unpack(pair, j, 2, width) for j in range(2)]
    tops, sums = [], []
    for j, logits in enumerate(heads):
        logits_ref[j] = logits
        tops.append(jnp.max(logits, axis=1, keepdims=True))
        sums.append(jnp.sum(jnp.exp(logits - tops[-1]), axis=1, keepdims=True))
    blank = jnp.zeros((LANES - len(heads) * SLOT, 1), f32)
    lane = lax.broadcasted_iota(jnp.int32, (LANES, LANES), 1)
    table = jnp.where(
        lane == 0,
        jnp.concatenate(tops + [blank], axis=0),
        jnp.where(lane == 1, jnp.concatenate(sums + [blank], axis=0), 0.0),
    ).T
    line = jnp.concatenate([table[0:1], table[1:2]], axis=1)
    out_ref[...] = jnp.broadcast_to(line[None], out_ref.shape)
    count = first[GROUP - 1 :, first.shape[1] - 1 :]
    weights_ref[...] = jnp.broadcast_to(loss_scale * flags_ref[...] / count, (SLOT, LANES))


def delta_kernel(stats_ref, logits_ref, weights_ref, out_ref):
    lines = stats_ref[...].reshape(stats_ref.shape[0], 2 * LANES)
    tops, sums = lines[:, :LANES], lines[:, LANES:]
    top = jnp.max(tops, axis=0, keepdims=True)
    total = jnp.sum(sums * jnp.exp(tops - top), axis=0, keepdims=True)
    row = lax.broadcasted_iota(jnp.int32, (LANES, LANES), 0)
    table = jnp.where(row == 0, top, jnp.where(row == 1, total, 0.0)).T
    probs = []
    for j in range(logits_ref.shape[0]):
        rows = table[j * SLOT : (j + 1) * SLOT]
        probs.append(jnp.exp(logits_ref[j] - rows[:, 0:1]) / rows[:, 1:2])
    width = logits_ref.shape[2]
    for k in range(2):
        delta = weights_ref[:, :1] * (probs[k] - probs[2])
        out_ref[:, k * width : (k + 1) * width] = delta.astype(bf16)


def hidden_grads_kernel(half_ref, heads_ref, near_ref, far_ref, out_ref):
    exits, width = out_ref.shape[1], heads_ref.shape[2]
    parts = HALF // PART
    for place, delta_ref in ((half_ref[0], near_ref), (1 - half_ref[0], far_ref)):
        for k in range(exits):
            grad = lax.dot_general(
                delta_ref[:, k * width : (k + 1) * width],
                heads_ref[k],
                (((1,), (1,)), ((), ())),
                preferred_element_type=f32,
            )
            out_ref[pl.ds(place * parts, parts), k] = grad.reshape(parts, PART, -1).astype(bf16)


def head_grads_kernel(half_ref, first_ref, pair_ref, near_ref, far_ref, out_ref):
    exits, _, width = out_ref.shape
    parts = HALF // PART
    for k, tiles_ref in enumerate((first_ref, pair_ref)):
        total = None
        for place, delta_ref in ((half_ref[0], near_ref), (1 - half_ref[0], far_ref)):
            rows = tiles_ref[pl.ds(place * parts, parts), 0].reshape(HALF, -1)
            term = lax.dot_general(
                rows,
                delta_ref[:, k * width : (k + 1) * width],
                (((0,), (0,)), ((), ())),
                preferred_element_type=f32,
            )
            total = term if total is None else total + term
        out_ref[k] = total.astype(bf16)


def copies_kernel(place_ref, own_ref, across_ref, out_ref):
    place = place_ref[0]
    for i in range(out_ref.shape[0]):
        out_ref[i, place] = own_ref[...]
        out_ref[i, 1 - place] = across_ref[...]


def chosen_kernel(take_ref, come_ref, own_ref, out_ref):
    for take, block_ref in ((1, come_ref), (0, own_ref)):

        @pl.when(take_ref[0] == take)
        def _():
            for i in range(out_ref.shape[0]):
                out_ref[i] = block_ref[...]


def chosen_copies(take, come, own, count):
    return pl.pallas_call(
        chosen_kernel,
        in_specs=[SMALL, WHOLE, WHOLE],
        out_specs=WHOLE,
        out_shape=jax.ShapeDtypeStruct((count,) + own.shape, own.dtype),
        compiler_params=LIMIT,
    )(take.astype(jnp.int32).reshape(1), come, own)


def summed_kernel(bits_ref, out_ref):
    total = bits_ref[0].astype(f32)
    for i in range(1, bits_ref.shape[0]):
        total = total + bits_ref[i].astype(f32)
    for i in range(out_ref.shape[0]):
        out_ref[i] = total.astype(bf16)


def summed_copies(bits):
    return pl.pallas_call(
        summed_kernel,
        in_specs=[WHOLE],
        out_specs=WHOLE,
        out_shape=jax.ShapeDtypeStruct(bits.shape, bits.dtype),
        compiler_params=LIMIT,
    )(bits)


def outgoing_kernel(place_ref, tree_ref, come_ref, first_ref, out_ref):
    total = tree_ref[...] + come_ref[...].astype(f32)
    first = first_ref[...].astype(f32)
    for i in range(out_ref.shape[0]):
        out_ref[i] = jnp.where(place_ref[0] == i, total, first).astype(bf16)


def local(hidden, heads, valid, exit_section):
    total, depth, width = heads.shape
    exits = total - 1
    tokens = valid.shape[0]
    zl, x, c = lax.axis_index("zl"), lax.axis_index("x"), lax.axis_index("c")
    zh = lax.axis_index("zh")
    last = ZL * X - 1
    dynamic = exit_section[0]

    own = pl.pallas_call(
        functools.partial(to_slots_kernel, tokens),
        in_specs=[WHOLE],
        out_specs=WHOLE,
        out_shape=jax.ShapeDtypeStruct((ROWS, depth), bf16),
        compiler_params=LIMIT,
    )(hidden[0])
    row_parts = exchange(own, "x").reshape(X, PART, depth)

    def down(step):
        pairs = [(z, z - step) for z in range(ZL - 1, -1, -2 * step)]
        return lax.ppermute(tree, "zl", pairs)

    def across_zl(step):
        return lax.ppermute(first, "zl", [(z, z ^ step) for z in range(ZL)])

    def grown(come, step):
        return jnp.where((zl % (2 * step)) == step - 1, come, tree)

    def taken(come, step):
        return jnp.where((zl ^ (dynamic // X)) & step != 0, come, first)

    tree = jnp.stack([pick(row_parts, exit_section[1] % X), row_parts[last % X]])
    first = pick(row_parts, dynamic % X)
    for step in (4, 2):
        tree_come, first_come = lax.optimization_barrier((down(step), across_zl(4 // step)))
        tree, first = grown(tree_come, step), taken(first_come, 4 // step)
    copies = chosen_copies(zl % 2 == 0, down(1), tree, X)
    pair_tiles, first_come = lax.optimization_barrier((exchange(copies, "x"), across_zl(4)))
    copies = chosen_copies((zl ^ (dynamic // X)) & 4 != 0, first_come, first, X)
    first_tiles = exchange(copies, "x").reshape(X, 1, PART, depth)

    tally = jnp.sum(valid.astype(f32))
    def halved(tiles, places):
        send = half_logits(tiles, heads, places, 1 - c, tally)
        return half_logits(tiles, heads, places, c, tally) + swap(send, "c")

    def over_y(both):
        return exchange(both, "y").reshape(Y, ZH, GROUP, both.shape[-1])

    pair, first_tiles = lax.optimization_barrier((halved(pair_tiles, (1, 2)), first_tiles))
    pair, first = lax.optimization_barrier((over_y(pair), halved(first_tiles, (0,))))
    pieces = []
    for parts in (over_y(first), pair):
        keep, send = fold(parts, zh)
        pieces += [keep, swap(send, "zh")]

    flags = jnp.pad(valid.astype(f32), (0, SLOT - tokens))[:, None]
    logits, weights, stats = pl.pallas_call(
        functools.partial(stats_kernel, width),
        in_specs=[WHOLE] * 5,
        out_specs=[WHOLE] * 3,
        out_shape=[
            jax.ShapeDtypeStruct((total, SLOT, width), f32),
            jax.ShapeDtypeStruct((SLOT, LANES), f32),
            jax.ShapeDtypeStruct((ZL * X, 1, 2 * LANES), f32),
        ],
        compiler_params=LIMIT,
    )(flags, *pieces)
    delta = pl.pallas_call(
        delta_kernel,
        in_specs=[WHOLE] * 3,
        out_specs=WHOLE,
        out_shape=jax.ShapeDtypeStruct((SLOT, exits * width), bf16),
        compiler_params=LIMIT,
    )(exchange(stats, PIPE), logits, weights)

    across = swap(delta, "zh")
    copies = pl.pallas_call(
        copies_kernel,
        in_specs=[SMALL, WHOLE, WHOLE],
        out_specs=WHOLE,
        out_shape=jax.ShapeDtypeStruct((Y, ZH) + delta.shape, bf16),
        compiler_params=LIMIT,
    )(zh.reshape(1), delta, across)
    near = exchange(copies, "y").reshape(HALF, exits * width)
    far = swap(near, "c")
    half = c.reshape(1)
    partial = pl.pallas_call(
        hidden_grads_kernel,
        in_specs=[SMALL, WHOLE, WHOLE, WHOLE],
        out_specs=WHOLE,
        out_shape=jax.ShapeDtypeStruct((X, exits, PART, depth), bf16),
        compiler_params=LIMIT,
    )(half, heads, near, far)
    d_heads = pl.pallas_call(
        head_grads_kernel,
        in_specs=[SMALL, WHOLE, WHOLE, WHOLE, WHOLE],
        out_specs=WHOLE,
        out_shape=jax.ShapeDtypeStruct((exits, depth, width), bf16),
        compiler_params=LIMIT,
    )(half, first_tiles, pair_tiles, near, far)

    def up(block, step):
        pairs = [(z, z + step) for z in range(step - 1, ZL, 2 * step)]
        return lax.ppermute(block.astype(bf16), "zl", pairs)

    summed = jnp.sum(exchange(partial, "x").astype(f32), axis=0)
    tree = summed[1]
    tree = tree + up(tree, 1).astype(f32)
    come, bits = lax.optimization_barrier(
        (up(tree, 2), exchange(summed[0].astype(bf16).reshape(ZL, BIT, depth), "zl"))
    )
    tree = tree + come.astype(f32)
    come, first = lax.optimization_barrier((up(tree, 4), exchange(summed_copies(bits), "zl")))
    outgoing = pl.pallas_call(
        outgoing_kernel,
        in_specs=[SMALL, WHOLE, WHOLE, WHOLE],
        out_specs=WHOLE,
        out_shape=jax.ShapeDtypeStruct((X, PART, depth), bf16),
        compiler_params=LIMIT,
    )((exit_section[1] - zl * X).reshape(1), tree, come, first.reshape(PART, depth))
    mask = jnp.any(exit_section == zl * X + x).astype(jnp.int32).reshape(1)
    grad = pl.pallas_call(
        functools.partial(from_slots_kernel, tokens),
        in_specs=[SMALL, WHOLE],
        out_specs=WHOLE,
        out_shape=jax.ShapeDtypeStruct(hidden.shape[1:], bf16),
        compiler_params=LIMIT,
    )(mask, exchange(outgoing, "x").reshape(ROWS, depth))
    grad = grad[None]
    return d_heads, grad


def solution(mesh):
    fine = Mesh(mesh.devices.reshape(ZL, X, ZH, Y, C), ("zl", "x", "zh", "y", "c"))
    placed = (P(PIPE, None, TENSOR), P(None, TENSOR, PIPE), P(TENSOR), P())
    return jax.shard_map(
        local,
        mesh=fine,
        in_specs=placed,
        out_specs=(P(None, TENSOR, PIPE), P(PIPE, None, TENSOR)),
        check_vma=False,
    )
```

```python
import functools

import jax
import jax.numpy as jnp
from jax import lax
from jax.experimental import pallas as pl
from jax.experimental.pallas import tpu as pltpu
from jax.sharding import Mesh, PartitionSpec as P

loss_scale = 16384.0
ZL, X, ZH, Y, C = 8, 4, 2, 4, 2
PIPE = ("zl", "x")
TENSOR = ("zh", "y", "c")
SLOT = 32
ROWS = ZH * Y * C * SLOT
HALF = ROWS // 2
PART = ROWS // X
BIT = PART // ZL
LANES = 128
GROUP = 8
f32, bf16 = jnp.float32, jnp.bfloat16
SMALL = pl.BlockSpec(memory_space=pltpu.SMEM)
WHOLE = pl.BlockSpec(memory_space=pltpu.VMEM)
LIMIT = pltpu.CompilerParams(vmem_limit_bytes=16 << 20)


def swap(block, axis):
    return lax.ppermute(block, axis, [(0, 1), (1, 0)])


def exchange(block, axis):
    return lax.all_to_all(block, axis, 0, 0, tiled=True)


def spread(block, axis):
    copies = jnp.broadcast_to(block[None], (lax.axis_size(axis),) + block.shape)
    return exchange(copies, axis)


def pick(blocks, place):
    return lax.dynamic_index_in_dim(blocks, place, 0, keepdims=False)


def slot_orders():
    for c in range(C):
        for y in range(Y):
            for zh in range(ZH):
                yield (c * Y + y) * ZH + zh, (zh * Y + y) * C + c


def to_slots_kernel(tokens, rows_ref, out_ref):
    rows = rows_ref[...].astype(f32)
    for slot, place in slot_orders():
        block = rows[place * tokens : (place + 1) * tokens]
        block = jnp.concatenate([block, block[2 * tokens - SLOT :]], axis=0)
        out_ref[slot * SLOT : (slot + 1) * SLOT] = block.astype(bf16)


def from_slots_kernel(tokens, mask_ref, slots_ref, out_ref):
    blocks = [None] * (ZH * Y * C)
    for slot, place in slot_orders():
        rows = slots_ref[slot * SLOT : (slot + 1) * SLOT].astype(f32)
        blocks[place] = rows[:tokens]
    rows = jnp.concatenate(blocks, axis=0)
    out_ref[...] = jnp.where(mask_ref[0] != 0, rows, 0.0).astype(bf16)


def packed_width(count, width):
    return 3 * count * width + (width if count == 2 else 3 * LANES)


def pack(product, place, count, tally, out_ref):
    slots, width = HALF // SLOT, product.shape[1]
    groups = product.reshape(slots, 4, GROUP, width)
    for g in range(3):
        start = (g * count + place) * width
        out_ref[:, :, start : start + width] = groups[:, g]
    rest = groups[:, 3]
    base = 3 * count * width
    if count == 2:
        lower = slice(4 * place, 4 * place + 4)
        out_ref[:, lower, base : base + width] = rest[:, lower]
    else:
        cut = 3 * LANES
        out_ref[:, 0:4, base : base + cut] = rest[:, 0:4, :cut]
        out_ref[:, 4:8, base : base + width - cut] = rest[:, 4:8, cut:]
        spare = base + width - cut
        out_ref[:, 4:8, spare:] = jnp.full((slots, 4, base + cut - spare), tally, f32)


def unpack(block, place, count, width):
    rows = [
        block[:, (g * count + place) * width : (g * count + place + 1) * width] for g in range(3)
    ]
    base = 3 * count * width
    rest = block[:, base:]
    turned = pltpu.roll(rest, 4, 0)
    if count == 2:
        rows.append(turned if place else rest)
    else:
        cut = 3 * LANES
        rows.append(jnp.concatenate([rest, turned[:, : width - cut]], axis=1))
    return jnp.concatenate(rows, axis=0)


def logits_kernel(places, half_ref, tally_ref, tiles_ref, heads_ref, out_ref):
    parts = HALF // PART
    for j, place in enumerate(places):
        rows = tiles_ref[pl.ds(half_ref[0] * parts, parts), j].reshape(HALF, -1)
        product = jnp.dot(rows, heads_ref[place], preferred_element_type=f32)
        pack(product, j, len(places), tally_ref[0], out_ref)


def half_logits(tiles, heads, places, half, tally):
    count, (_, depth, width) = len(places), heads.shape
    shape = (HALF // SLOT, GROUP, packed_width(count, width))
    return pl.pallas_call(
        functools.partial(logits_kernel, places),
        in_specs=[SMALL, SMALL, WHOLE, WHOLE],
        out_specs=WHOLE,
        out_shape=jax.ShapeDtypeStruct(shape, f32),
        compiler_params=LIMIT,
        cost_estimate=pl.CostEstimate(
            flops=2 * HALF * depth * width * count,
            bytes_accessed=2 * count * depth * width + 2 * tiles.size,
            transcendentals=0,
        ),
    )(half.reshape(1), tally.reshape(1), tiles, heads)


def fold_kernel(place_ref, parts_ref, keep_ref, send_ref):
    place = place_ref[0]
    for side, out_ref in ((place, keep_ref), (1 - place, send_ref)):
        total = parts_ref[0, side]
        for i in range(1, parts_ref.shape[0]):
            total = total + parts_ref[i, side]
        out_ref[...] = total


def fold(parts, place):
    shape = jax.ShapeDtypeStruct(parts.shape[2:], f32)
    return pl.pallas_call(
        fold_kernel,
        in_specs=[SMALL, WHOLE],
        out_specs=[WHOLE, WHOLE],
        out_shape=[shape, shape],
        compiler_params=LIMIT,
    )(place.reshape(1), parts)


def stats_kernel(width, flags_ref, a_keep, a_come, b_keep, b_come, logits_ref, weights_ref, out_ref):
    first = a_keep[...] + a_come[...]
    pair = b_keep[...] + b_come[...]
    heads = [unpack(first, 0, 1, width)] + [unpack(pair, j, 2, width) for j in range(2)]
    tops, sums = [], []
    for j, logits in enumerate(heads):
        logits_ref[j] = logits
        tops.append(jnp.max(logits, axis=1, keepdims=True))
        sums.append(jnp.sum(jnp.exp(logits - tops[-1]), axis=1, keepdims=True))
    blank = jnp.zeros((LANES - len(heads) * SLOT, 1), f32)
    lane = lax.broadcasted_iota(jnp.int32, (LANES, LANES), 1)
    table = jnp.where(
        lane == 0,
        jnp.concatenate(tops + [blank], axis=0),
        jnp.where(lane == 1, jnp.concatenate(sums + [blank], axis=0), 0.0),
    ).T
    line = jnp.concatenate([table[0:1], table[1:2]], axis=1)
    out_ref[...] = jnp.broadcast_to(line[None], out_ref.shape)
    count = first[GROUP - 1 :, first.shape[1] - 1 :]
    weights_ref[...] = jnp.broadcast_to(loss_scale * flags_ref[...] / count, (SLOT, LANES))


def delta_kernel(stats_ref, logits_ref, weights_ref, out_ref):
    lines = stats_ref[...].reshape(stats_ref.shape[0], 2 * LANES)
    tops, sums = lines[:, :LANES], lines[:, LANES:]
    top = jnp.max(tops, axis=0, keepdims=True)
    total = jnp.sum(sums * jnp.exp(tops - top), axis=0, keepdims=True)
    row = lax.broadcasted_iota(jnp.int32, (LANES, LANES), 0)
    table = jnp.where(row == 0, top, jnp.where(row == 1, total, 0.0)).T
    probs = []
    for j in range(logits_ref.shape[0]):
        rows = table[j * SLOT : (j + 1) * SLOT]
        probs.append(jnp.exp(logits_ref[j] - rows[:, 0:1]) / rows[:, 1:2])
    width = logits_ref.shape[2]
    for k in range(2):
        delta = weights_ref[:, :1] * (probs[k] - probs[2])
        out_ref[:, k * width : (k + 1) * width] = delta.astype(bf16)


def hidden_grads_kernel(half_ref, heads_ref, near_ref, far_ref, out_ref):
    exits, width = out_ref.shape[1], heads_ref.shape[2]
    parts = HALF // PART
    for place, delta_ref in ((half_ref[0], near_ref), (1 - half_ref[0], far_ref)):
        for k in range(exits):
            grad = lax.dot_general(
                delta_ref[:, k * width : (k + 1) * width],
                heads_ref[k],
                (((1,), (1,)), ((), ())),
                preferred_element_type=f32,
            )
            out_ref[pl.ds(place * parts, parts), k] = grad.reshape(parts, PART, -1).astype(bf16)


def head_grads_kernel(half_ref, first_ref, pair_ref, near_ref, far_ref, out_ref):
    exits, _, width = out_ref.shape
    parts = HALF // PART
    for k, tiles_ref in enumerate((first_ref, pair_ref)):
        total = None
        for place, delta_ref in ((half_ref[0], near_ref), (1 - half_ref[0], far_ref)):
            rows = tiles_ref[pl.ds(place * parts, parts), 0].reshape(HALF, -1)
            term = lax.dot_general(
                rows,
                delta_ref[:, k * width : (k + 1) * width],
                (((0,), (0,)), ((), ())),
                preferred_element_type=f32,
            )
            total = term if total is None else total + term
        out_ref[k] = total.astype(bf16)


def copies_kernel(place_ref, own_ref, across_ref, out_ref):
    place = place_ref[0]
    for i in range(out_ref.shape[0]):
        out_ref[i, place] = own_ref[...]
        out_ref[i, 1 - place] = across_ref[...]


def outgoing_kernel(place_ref, tree_ref, come_ref, first_ref, out_ref):
    total = tree_ref[...] + come_ref[...].astype(f32)
    first = first_ref[...].astype(f32)
    for i in range(out_ref.shape[0]):
        out_ref[i] = jnp.where(place_ref[0] == i, total, first).astype(bf16)


def local(hidden, heads, valid, exit_section):
    total, depth, width = heads.shape
    exits = total - 1
    tokens = valid.shape[0]
    zl, x, c = lax.axis_index("zl"), lax.axis_index("x"), lax.axis_index("c")
    zh = lax.axis_index("zh")
    last = ZL * X - 1
    dynamic = exit_section[0]

    own = pl.pallas_call(
        functools.partial(to_slots_kernel, tokens),
        in_specs=[WHOLE],
        out_specs=WHOLE,
        out_shape=jax.ShapeDtypeStruct((ROWS, depth), bf16),
        compiler_params=LIMIT,
    )(hidden[0])
    row_parts = exchange(own, "x").reshape(X, PART, depth)

    def down(step):
        pairs = [(z, z - step) for z in range(ZL - 1, -1, -2 * step)]
        return lax.ppermute(tree, "zl", pairs)

    def across_zl(step):
        return lax.ppermute(first, "zl", [(z, z ^ step) for z in range(ZL)])

    def grown(come, step):
        return jnp.where((zl % (2 * step)) == step - 1, come, tree)

    def taken(come, step):
        return jnp.where((zl ^ (dynamic // X)) & step != 0, come, first)

    tree = jnp.stack([pick(row_parts, exit_section[1] % X), row_parts[last % X]])
    first = pick(row_parts, dynamic % X)
    tree_come, first_come = lax.optimization_barrier((down(4), across_zl(1)))
    tree, first = grown(tree_come, 4), taken(first_come, 1)
    tree = grown(down(2), 2)
    tree_come, first_come = lax.optimization_barrier((down(1), across_zl(2)))
    tree, first = grown(tree_come, 1), taken(first_come, 2)
    pair_tiles, first_come = lax.optimization_barrier((spread(tree, "x"), across_zl(4)))
    first = taken(first_come, 4)
    first_tiles = spread(first[None], "x").reshape(X, 1, PART, depth)

    tally = jnp.sum(valid.astype(f32))
    def halved(tiles, places):
        send = half_logits(tiles, heads, places, 1 - c, tally)
        return half_logits(tiles, heads, places, c, tally) + swap(send, "c")

    def over_y(both):
        return exchange(both, "y").reshape(Y, ZH, GROUP, both.shape[-1])

    pair, first_tiles = lax.optimization_barrier((halved(pair_tiles, (1, 2)), first_tiles))
    pair, first = lax.optimization_barrier((over_y(pair), halved(first_tiles, (0,))))
    pieces = []
    for parts in (over_y(first), pair):
        keep, send = fold(parts, zh)
        pieces += [keep, swap(send, "zh")]

    flags = jnp.pad(valid.astype(f32), (0, SLOT - tokens))[:, None]
    logits, weights, stats = pl.pallas_call(
        functools.partial(stats_kernel, width),
        in_specs=[WHOLE] * 5,
        out_specs=[WHOLE] * 3,
        out_shape=[
            jax.ShapeDtypeStruct((total, SLOT, width), f32),
            jax.ShapeDtypeStruct((SLOT, LANES), f32),
            jax.ShapeDtypeStruct((ZL * X, 1, 2 * LANES), f32),
        ],
        compiler_params=LIMIT,
    )(flags, *pieces)
    delta = pl.pallas_call(
        delta_kernel,
        in_specs=[WHOLE] * 3,
        out_specs=WHOLE,
        out_shape=jax.ShapeDtypeStruct((SLOT, exits * width), bf16),
        compiler_params=LIMIT,
    )(exchange(stats, PIPE), logits, weights)

    across = swap(delta, "zh")
    copies = pl.pallas_call(
        copies_kernel,
        in_specs=[SMALL, WHOLE, WHOLE],
        out_specs=WHOLE,
        out_shape=jax.ShapeDtypeStruct((Y, ZH) + delta.shape, bf16),
        compiler_params=LIMIT,
    )(zh.reshape(1), delta, across)
    near = exchange(copies, "y").reshape(HALF, exits * width)
    far = swap(near, "c")
    half = c.reshape(1)
    partial = pl.pallas_call(
        hidden_grads_kernel,
        in_specs=[SMALL, WHOLE, WHOLE, WHOLE],
        out_specs=WHOLE,
        out_shape=jax.ShapeDtypeStruct((X, exits, PART, depth), bf16),
        compiler_params=LIMIT,
    )(half, heads, near, far)
    d_heads = pl.pallas_call(
        head_grads_kernel,
        in_specs=[SMALL, WHOLE, WHOLE, WHOLE, WHOLE],
        out_specs=WHOLE,
        out_shape=jax.ShapeDtypeStruct((exits, depth, width), bf16),
        compiler_params=LIMIT,
    )(half, first_tiles, pair_tiles, near, far)

    def up(block, step):
        pairs = [(z, z + step) for z in range(step - 1, ZL, 2 * step)]
        return lax.ppermute(block.astype(bf16), "zl", pairs)

    summed = jnp.sum(exchange(partial, "x").astype(f32), axis=0)
    tree = summed[1]
    tree = tree + up(tree, 1).astype(f32)
    come, bits = lax.optimization_barrier(
        (up(tree, 2), exchange(summed[0].astype(bf16).reshape(ZL, BIT, depth), "zl"))
    )
    tree = tree + come.astype(f32)
    bit = jnp.sum(bits.astype(f32), axis=0).astype(bf16)
    come, first = lax.optimization_barrier((up(tree, 4), spread(bit, "zl")))
    outgoing = pl.pallas_call(
        outgoing_kernel,
        in_specs=[SMALL, WHOLE, WHOLE, WHOLE],
        out_specs=WHOLE,
        out_shape=jax.ShapeDtypeStruct((X, PART, depth), bf16),
        compiler_params=LIMIT,
    )((exit_section[1] - zl * X).reshape(1), tree, come, first.reshape(PART, depth))
    mask = jnp.any(exit_section == zl * X + x).astype(jnp.int32).reshape(1)
    grad = pl.pallas_call(
        functools.partial(from_slots_kernel, tokens),
        in_specs=[SMALL, WHOLE],
        out_specs=WHOLE,
        out_shape=jax.ShapeDtypeStruct(hidden.shape[1:], bf16),
        compiler_params=LIMIT,
    )(mask, exchange(outgoing, "x").reshape(ROWS, depth))
    grad = grad[None]
    return d_heads, grad


def solution(mesh):
    fine = Mesh(mesh.devices.reshape(ZL, X, ZH, Y, C), ("zl", "x", "zh", "y", "c"))
    placed = (P(PIPE, None, TENSOR), P(None, TENSOR, PIPE), P(TENSOR), P())
    return jax.shard_map(
        local,
        mesh=fine,
        in_specs=placed,
        out_specs=(P(None, TENSOR, PIPE), P(PIPE, None, TENSOR)),
        check_vma=False,
    )
```

```python
import functools

import jax
import jax.numpy as jnp
from jax import lax
from jax.experimental import pallas as pl
from jax.experimental.pallas import tpu as pltpu
from jax.sharding import Mesh, PartitionSpec as P

loss_scale = 16384.0
ZL, X, ZH, Y, C = 8, 4, 2, 4, 2
PIPE = ("zl", "x")
TENSOR = ("zh", "y", "c")
SLOT = 32
ROWS = ZH * Y * C * SLOT
HALF = ROWS // 2
PART = ROWS // X
BIT = PART // ZL
LANES = 128
GROUP = 8
f32, bf16 = jnp.float32, jnp.bfloat16
SMALL = pl.BlockSpec(memory_space=pltpu.SMEM)
WHOLE = pl.BlockSpec(memory_space=pltpu.VMEM)
LIMIT = pltpu.CompilerParams(vmem_limit_bytes=16 << 20)


def swap(block, axis):
    return lax.ppermute(block, axis, [(0, 1), (1, 0)])


def exchange(block, axis):
    return lax.all_to_all(block, axis, 0, 0, tiled=True)


def spread(block, axis):
    copies = jnp.broadcast_to(block[None], (lax.axis_size(axis),) + block.shape)
    return exchange(copies, axis)


def pick(blocks, place):
    return lax.dynamic_index_in_dim(blocks, place, 0, keepdims=False)


def slot_orders():
    for c in range(C):
        for y in range(Y):
            for zh in range(ZH):
                yield (c * Y + y) * ZH + zh, (zh * Y + y) * C + c


def to_slots_kernel(tokens, rows_ref, out_ref):
    rows = rows_ref[...].astype(f32)
    for slot, place in slot_orders():
        block = rows[place * tokens : (place + 1) * tokens]
        block = jnp.concatenate([block, block[2 * tokens - SLOT :]], axis=0)
        out_ref[slot * SLOT : (slot + 1) * SLOT] = block.astype(bf16)


def from_slots_kernel(tokens, mask_ref, slots_ref, out_ref):
    blocks = [None] * (ZH * Y * C)
    for slot, place in slot_orders():
        rows = slots_ref[slot * SLOT : (slot + 1) * SLOT].astype(f32)
        blocks[place] = rows[:tokens]
    rows = jnp.concatenate(blocks, axis=0)
    out_ref[...] = jnp.where(mask_ref[0] != 0, rows, 0.0).astype(bf16)


def packed_width(count, width):
    return 3 * count * width + (width if count == 2 else 3 * LANES)


def pack(product, place, count, tally, out_ref):
    slots, width = HALF // SLOT, product.shape[1]
    groups = product.reshape(slots, 4, GROUP, width)
    for g in range(3):
        start = (g * count + place) * width
        out_ref[:, :, start : start + width] = groups[:, g]
    rest = groups[:, 3]
    base = 3 * count * width
    if count == 2:
        lower = slice(4 * place, 4 * place + 4)
        out_ref[:, lower, base : base + width] = rest[:, lower]
    else:
        cut = 3 * LANES
        out_ref[:, 0:4, base : base + cut] = rest[:, 0:4, :cut]
        out_ref[:, 4:8, base : base + width - cut] = rest[:, 4:8, cut:]
        spare = base + width - cut
        out_ref[:, 4:8, spare:] = jnp.full((slots, 4, base + cut - spare), tally, f32)


def unpack(block, place, count, width):
    rows = [
        block[:, (g * count + place) * width : (g * count + place + 1) * width] for g in range(3)
    ]
    base = 3 * count * width
    rest = block[:, base:]
    turned = pltpu.roll(rest, 4, 0)
    if count == 2:
        rows.append(turned if place else rest)
    else:
        cut = 3 * LANES
        rows.append(jnp.concatenate([rest, turned[:, : width - cut]], axis=1))
    return jnp.concatenate(rows, axis=0)


def logits_kernel(places, half_ref, tally_ref, tiles_ref, heads_ref, out_ref):
    parts = HALF // PART
    for j, place in enumerate(places):
        rows = tiles_ref[pl.ds(half_ref[0] * parts, parts), j].reshape(HALF, -1)
        product = jnp.dot(rows, heads_ref[place], preferred_element_type=f32)
        pack(product, j, len(places), tally_ref[0], out_ref)


def half_logits(tiles, heads, places, half, tally):
    count, (_, depth, width) = len(places), heads.shape
    shape = (HALF // SLOT, GROUP, packed_width(count, width))
    return pl.pallas_call(
        functools.partial(logits_kernel, places),
        in_specs=[SMALL, SMALL, WHOLE, WHOLE],
        out_specs=WHOLE,
        out_shape=jax.ShapeDtypeStruct(shape, f32),
        compiler_params=LIMIT,
        cost_estimate=pl.CostEstimate(
            flops=2 * HALF * depth * width * count,
            bytes_accessed=2 * count * depth * width + 2 * tiles.size,
            transcendentals=0,
        ),
    )(half.reshape(1), tally.reshape(1), tiles, heads)


def fold_kernel(place_ref, parts_ref, keep_ref, send_ref):
    place = place_ref[0]
    for side, out_ref in ((place, keep_ref), (1 - place, send_ref)):
        total = parts_ref[0, side]
        for i in range(1, parts_ref.shape[0]):
            total = total + parts_ref[i, side]
        out_ref[...] = total


def fold(parts, place):
    shape = jax.ShapeDtypeStruct(parts.shape[2:], f32)
    return pl.pallas_call(
        fold_kernel,
        in_specs=[SMALL, WHOLE],
        out_specs=[WHOLE, WHOLE],
        out_shape=[shape, shape],
        compiler_params=LIMIT,
    )(place.reshape(1), parts)


def stats_kernel(width, flags_ref, a_keep, a_come, b_keep, b_come, logits_ref, weights_ref, out_ref):
    first = a_keep[...] + a_come[...]
    pair = b_keep[...] + b_come[...]
    heads = [unpack(first, 0, 1, width)] + [unpack(pair, j, 2, width) for j in range(2)]
    tops, sums = [], []
    for j, logits in enumerate(heads):
        logits_ref[j] = logits
        tops.append(jnp.max(logits, axis=1, keepdims=True))
        sums.append(jnp.sum(jnp.exp(logits - tops[-1]), axis=1, keepdims=True))
    blank = jnp.zeros((LANES - len(heads) * SLOT, 1), f32)
    lane = lax.broadcasted_iota(jnp.int32, (LANES, LANES), 1)
    table = jnp.where(
        lane == 0,
        jnp.concatenate(tops + [blank], axis=0),
        jnp.where(lane == 1, jnp.concatenate(sums + [blank], axis=0), 0.0),
    ).T
    line = jnp.concatenate([table[0:1], table[1:2]], axis=1)
    out_ref[...] = jnp.broadcast_to(line[None], out_ref.shape)
    count = first[GROUP - 1 :, first.shape[1] - 1 :]
    weights_ref[...] = jnp.broadcast_to(loss_scale * flags_ref[...] / count, (SLOT, LANES))


def delta_kernel(stats_ref, logits_ref, weights_ref, out_ref):
    lines = stats_ref[...].reshape(stats_ref.shape[0], 2 * LANES)
    tops, sums = lines[:, :LANES], lines[:, LANES:]
    top = jnp.max(tops, axis=0, keepdims=True)
    total = jnp.sum(sums * jnp.exp(tops - top), axis=0, keepdims=True)
    row = lax.broadcasted_iota(jnp.int32, (LANES, LANES), 0)
    table = jnp.where(row == 0, top, jnp.where(row == 1, total, 0.0)).T
    probs = []
    for j in range(logits_ref.shape[0]):
        rows = table[j * SLOT : (j + 1) * SLOT]
        probs.append(jnp.exp(logits_ref[j] - rows[:, 0:1]) / rows[:, 1:2])
    width = logits_ref.shape[2]
    for k in range(2):
        delta = weights_ref[:, :1] * (probs[k] - probs[2])
        out_ref[:, k * width : (k + 1) * width] = delta.astype(bf16)


def hidden_grads_kernel(half_ref, heads_ref, near_ref, far_ref, out_ref):
    exits, width = out_ref.shape[1], heads_ref.shape[2]
    parts = HALF // PART
    for place, delta_ref in ((half_ref[0], near_ref), (1 - half_ref[0], far_ref)):
        for k in range(exits):
            grad = lax.dot_general(
                delta_ref[:, k * width : (k + 1) * width],
                heads_ref[k],
                (((1,), (1,)), ((), ())),
                preferred_element_type=f32,
            )
            out_ref[pl.ds(place * parts, parts), k] = grad.reshape(parts, PART, -1).astype(bf16)


def head_grads_kernel(half_ref, first_ref, pair_ref, near_ref, far_ref, out_ref):
    exits, _, width = out_ref.shape
    parts = HALF // PART
    for k, tiles_ref in enumerate((first_ref, pair_ref)):
        total = None
        for place, delta_ref in ((half_ref[0], near_ref), (1 - half_ref[0], far_ref)):
            rows = tiles_ref[pl.ds(place * parts, parts), 0].reshape(HALF, -1)
            term = lax.dot_general(
                rows,
                delta_ref[:, k * width : (k + 1) * width],
                (((0,), (0,)), ((), ())),
                preferred_element_type=f32,
            )
            total = term if total is None else total + term
        out_ref[k] = total.astype(bf16)


def copies_kernel(place_ref, own_ref, across_ref, out_ref):
    place = place_ref[0]
    for i in range(out_ref.shape[0]):
        out_ref[i, place] = own_ref[...]
        out_ref[i, 1 - place] = across_ref[...]


def outgoing_kernel(place_ref, tree_ref, come_ref, first_ref, out_ref):
    total = tree_ref[...] + come_ref[...].astype(f32)
    first = first_ref[...].astype(f32)
    for i in range(out_ref.shape[0]):
        out_ref[i] = jnp.where(place_ref[0] == i, total, first).astype(bf16)


def local(hidden, heads, valid, exit_section):
    total, depth, width = heads.shape
    exits = total - 1
    tokens = valid.shape[0]
    zl, x, c = lax.axis_index("zl"), lax.axis_index("x"), lax.axis_index("c")
    zh = lax.axis_index("zh")
    last = ZL * X - 1
    dynamic = exit_section[0]

    own = pl.pallas_call(
        functools.partial(to_slots_kernel, tokens),
        in_specs=[WHOLE],
        out_specs=WHOLE,
        out_shape=jax.ShapeDtypeStruct((ROWS, depth), bf16),
        compiler_params=LIMIT,
    )(hidden[0])
    row_parts = exchange(own, "x").reshape(X, PART, depth)

    def down(step):
        pairs = [(z, z - step) for z in range(ZL - 1, -1, -2 * step)]
        return lax.ppermute(tree, "zl", pairs)

    def across_zl(step):
        return lax.ppermute(first, "zl", [(z, z ^ step) for z in range(ZL)])

    def grown(come, step):
        return jnp.where((zl % (2 * step)) == step - 1, come, tree)

    def taken(come, step):
        return jnp.where((zl ^ (dynamic // X)) & step != 0, come, first)

    tree = jnp.stack([pick(row_parts, exit_section[1] % X), row_parts[last % X]])
    first = pick(row_parts, dynamic % X)
    tree = grown(down(4), 4)
    tree_come, first_come = lax.optimization_barrier((down(2), across_zl(1)))
    tree, first = grown(tree_come, 2), taken(first_come, 1)
    tree_come, first_come = lax.optimization_barrier((down(1), across_zl(2)))
    tree, first = grown(tree_come, 1), taken(first_come, 2)
    pair_tiles, first_come = lax.optimization_barrier((spread(tree, "x"), across_zl(4)))
    first = taken(first_come, 4)
    first_tiles = spread(first[None], "x").reshape(X, 1, PART, depth)

    tally = jnp.sum(valid.astype(f32))
    def halved(tiles, places):
        send = half_logits(tiles, heads, places, 1 - c, tally)
        return half_logits(tiles, heads, places, c, tally) + swap(send, "c")

    def over_y(both):
        return exchange(both, "y").reshape(Y, ZH, GROUP, both.shape[-1])

    pair, first_tiles = lax.optimization_barrier((halved(pair_tiles, (1, 2)), first_tiles))
    pair, first = lax.optimization_barrier((over_y(pair), halved(first_tiles, (0,))))
    pieces = []
    for parts in (over_y(first), pair):
        keep, send = fold(parts, zh)
        pieces += [keep, swap(send, "zh")]

    flags = jnp.pad(valid.astype(f32), (0, SLOT - tokens))[:, None]
    logits, weights, stats = pl.pallas_call(
        functools.partial(stats_kernel, width),
        in_specs=[WHOLE] * 5,
        out_specs=[WHOLE] * 3,
        out_shape=[
            jax.ShapeDtypeStruct((total, SLOT, width), f32),
            jax.ShapeDtypeStruct((SLOT, LANES), f32),
            jax.ShapeDtypeStruct((ZL * X, 1, 2 * LANES), f32),
        ],
        compiler_params=LIMIT,
    )(flags, *pieces)
    delta = pl.pallas_call(
        delta_kernel,
        in_specs=[WHOLE] * 3,
        out_specs=WHOLE,
        out_shape=jax.ShapeDtypeStruct((SLOT, exits * width), bf16),
        compiler_params=LIMIT,
    )(exchange(stats, PIPE), logits, weights)

    across = swap(delta, "zh")
    copies = pl.pallas_call(
        copies_kernel,
        in_specs=[SMALL, WHOLE, WHOLE],
        out_specs=WHOLE,
        out_shape=jax.ShapeDtypeStruct((Y, ZH) + delta.shape, bf16),
        compiler_params=LIMIT,
    )(zh.reshape(1), delta, across)
    near = exchange(copies, "y").reshape(HALF, exits * width)
    far = swap(near, "c")
    half = c.reshape(1)
    partial = pl.pallas_call(
        hidden_grads_kernel,
        in_specs=[SMALL, WHOLE, WHOLE, WHOLE],
        out_specs=WHOLE,
        out_shape=jax.ShapeDtypeStruct((X, exits, PART, depth), bf16),
        compiler_params=LIMIT,
    )(half, heads, near, far)
    d_heads = pl.pallas_call(
        head_grads_kernel,
        in_specs=[SMALL, WHOLE, WHOLE, WHOLE, WHOLE],
        out_specs=WHOLE,
        out_shape=jax.ShapeDtypeStruct((exits, depth, width), bf16),
        compiler_params=LIMIT,
    )(half, first_tiles, pair_tiles, near, far)

    def up(block, step):
        pairs = [(z, z + step) for z in range(step - 1, ZL, 2 * step)]
        return lax.ppermute(block.astype(bf16), "zl", pairs)

    summed = jnp.sum(exchange(partial, "x").astype(f32), axis=0)
    tree = summed[1]
    tree = tree + up(tree, 1).astype(f32)
    come, bits = lax.optimization_barrier(
        (up(tree, 2), exchange(summed[0].astype(bf16).reshape(ZL, BIT, depth), "zl"))
    )
    tree = tree + come.astype(f32)
    bit = jnp.sum(bits.astype(f32), axis=0).astype(bf16)
    come, first = lax.optimization_barrier((up(tree, 4), spread(bit, "zl")))
    outgoing = pl.pallas_call(
        outgoing_kernel,
        in_specs=[SMALL, WHOLE, WHOLE, WHOLE],
        out_specs=WHOLE,
        out_shape=jax.ShapeDtypeStruct((X, PART, depth), bf16),
        compiler_params=LIMIT,
    )((exit_section[1] - zl * X).reshape(1), tree, come, first.reshape(PART, depth))
    mask = jnp.any(exit_section == zl * X + x).astype(jnp.int32).reshape(1)
    grad = pl.pallas_call(
        functools.partial(from_slots_kernel, tokens),
        in_specs=[SMALL, WHOLE],
        out_specs=WHOLE,
        out_shape=jax.ShapeDtypeStruct(hidden.shape[1:], bf16),
        compiler_params=LIMIT,
    )(mask, exchange(outgoing, "x").reshape(ROWS, depth))
    grad = grad[None]
    return d_heads, grad


def solution(mesh):
    fine = Mesh(mesh.devices.reshape(ZL, X, ZH, Y, C), ("zl", "x", "zh", "y", "c"))
    placed = (P(PIPE, None, TENSOR), P(None, TENSOR, PIPE), P(TENSOR), P())
    return jax.shard_map(
        local,
        mesh=fine,
        in_specs=placed,
        out_specs=(P(None, TENSOR, PIPE), P(PIPE, None, TENSOR)),
        check_vma=False,
    )
```
